32 devices in a mesh: dp: 8 (over z, y), fsdp: 4 (over x, core).
Axes of the slice: x: 2, y: 2, z: 4, core: 2. Of those that a mesh axis runs over, the one named last changes fastest.
Arguments:
- inputs: bfloat16 [32768, 768], P(('dp', 'fsdp')), may hold values from -6 to 6
- lengths: int32 [64, 2], P(('dp', 'fsdp')), may hold values from 1 to 507, as said below
- query_matrix: bfloat16 [768, 768], P(('dp', 'fsdp')), may hold values from -0.21875 to 0.21875
- key_weight: bfloat16 [768, 768], P(('dp', 'fsdp')), may hold values from -0.21875 to 0.21875
- value_matrix: bfloat16 [768, 768], P(('dp', 'fsdp')), may hold values from -0.21875 to 0.21875
- output_weight: bfloat16 [768, 768], P(('dp', 'fsdp')), may hold values from -1.25 to 1.25
- inner_weight: bfloat16 [768, 3072], P(('dp', 'fsdp')), may hold values from -0.21875 to 0.21875
- outer_weight: bfloat16 [3072, 768], P(('dp', 'fsdp')), may hold values from -0.109375 to 0.109375
- attn_gain: bfloat16 [768], replicated, may hold values from 0.5 to 1.5
- attn_shift: bfloat16 [768], replicated, may hold values from -1.5 to 1.5
- ffn_gain: bfloat16 [768], replicated, may hold values from 0.5 to 1.5
- ffn_shift: bfloat16 [768], replicated, may hold values from -1.5 to 1.5
- query_down: float32 [768, 8], replicated, may hold values from -0.21875 to 0.21875
- query_raise_weight: float32 [8, 768], replicated, may hold values from -1 to 1
- value_down: float32 [768, 8], replicated, may hold values from -0.21875 to 0.21875
- value_raise_weight: float32 [8, 768], replicated, may hold values from -1 to 1
- grad_output: bfloat16 [32768, 768], P(('dp', 'fsdp')), may hold values from -6 to 6
Outputs:
- outputs: bfloat16 [32768, 768], P(('dp', 'fsdp'))
- grad_inputs: float32 [32768, 768], P(('dp', 'fsdp'))
- grad_query_down: float32 [768, 8], replicated
- grad_query_up: float32 [8, 768], replicated
- grad_value_down: float32 [768, 8], replicated
- grad_value_up: float32 [8, 768], replicated
The draws below stay inside these ranges and needn't reach their ends.
Inputs may be any that keep to these rules, and one draw needn't show every extreme that they name: lengths[s, 0] and lengths[s, 1] are slot s's premise and hypothesis token counts, each 1 or more, with lengths[s, 0] + lengths[s, 1] + 4 <= 512; in every draw some slot has lengths[s, 0] + lengths[s, 1] + 4 == 512.
All inputs are finite; a program needn't handle non-finite values.
Results may differ from the reference program's by a relative error of at most 0.017.
The reference program's roundings to bfloat16 on the way count: a program that leaves them out, or rounds other values in their place, can miss the bound.
Values may be sent and summed in bfloat16 or wider, within the bound.
No kernel may reach another device: no remote copies, remote signals or barrier semaphores. Data moves between devices by JAX's collectives and lax.ppermute only.
A program may use at most 128 MiB of HBM per device.

```python
import math
import jax
import jax.numpy as jnp
from jax import lax

D = 768
FF = 3072
HEADS = 12
HEAD_DIM = 64
RANK = 8
SLOT_LEN = 512
SLOTS = 64
TOKENS = 32768


def draw_lengths(key, part):
    key = jax.random.fold_in(key, 11)
    key_total, key_choice, key_split = jax.random.split(key, 3)
    slot_total = jax.random.randint(key_total, (SLOTS,), SLOT_LEN // 4, SLOT_LEN + 1)
    chosen = jax.random.randint(key_choice, (), 0, SLOTS)
    is_chosen = jnp.arange(SLOTS) == chosen
    slot_total = jnp.where(is_chosen, SLOT_LEN, slot_total)
    content = slot_total - 4
    premise = jax.random.randint(key_split, (SLOTS,), 1, content)
    premise = jnp.where(is_chosen, 1, premise)
    return jnp.stack([premise, content - premise], axis=1).astype(jnp.int32)


def block_levels(own_key, extent, cuts, least, largest):
    factor_of = 1.0
    for axis_at, shards_of in cuts:
        steps = jax.random.uniform(jax.random.fold_in(jax.random.fold_in(own_key, 6), axis_at), (shards_of,), jnp.float32, least / len(cuts), largest / len(cuts))
        factor_of = factor_of * jnp.repeat(jnp.exp(steps), extent[axis_at] // shards_of).reshape((-1,) + (1,) * (len(extent) - 1 - axis_at))
    return factor_of


def bell_draw(rng, shape, deviation, reach, shards=(), kind=jnp.bfloat16):
    values = jax.random.normal(rng, shape, jnp.float32) * deviation
    if len(shards) > 0:
        values = block_levels(rng, shape, shards, -0.22, 0.18) * values
    return jnp.clip(values, min=-reach, max=reach).astype(kind)


def setup_inputs(seed: int = 0) -> dict:
    arg_keys = jax.random.split(jax.random.key(seed), 18)
    return {
        "inputs": bell_draw(arg_keys[0], (TOKENS, D), 1.0, 6.0, ((0, 32),)),
        "lengths": draw_lengths(jax.random.fold_in(arg_keys[17], 71), 0),
        "query_matrix": bell_draw(arg_keys[2], (D, D), D ** -0.5, 0.21875, ((0, 32),)),
        "key_weight": bell_draw(arg_keys[3], (D, D), D ** -0.5, 0.21875, ((0, 32),)),
        "value_matrix": bell_draw(arg_keys[4], (D, D), D ** -0.5, 0.21875, ((0, 32),)),
        "output_weight": bell_draw(arg_keys[5], (D, D), (D // 32) ** -0.5, 1.25, ((0, 32),)),
        "inner_weight": bell_draw(arg_keys[6], (D, FF), D ** -0.5, 0.21875, ((0, 32),)),
        "outer_weight": bell_draw(arg_keys[7], (FF, D), FF ** -0.5, 0.109375, ((0, 32),)),
        "attn_gain": jnp.clip(1.0 + 0.1 * jax.random.normal(arg_keys[8], (D,), jnp.float32), 0.5, 1.5).astype(jnp.bfloat16),
        "attn_shift": bell_draw(arg_keys[9], (D,), 0.3, 1.5),
        "ffn_gain": jnp.clip(1.0 + 0.1 * jax.random.normal(arg_keys[10], (D,), jnp.float32), 0.5, 1.5).astype(jnp.bfloat16),
        "ffn_shift": bell_draw(arg_keys[11], (D,), 0.3, 1.5),
        "query_down": bell_draw(arg_keys[12], (D, RANK), D ** -0.5, 0.21875, (), jnp.float32),
        "query_raise_weight": bell_draw(arg_keys[13], (RANK, D), (4 * RANK) ** -0.5, 1.0, (), jnp.float32),
        "value_down": bell_draw(arg_keys[14], (D, RANK), D ** -0.5, 0.21875, (), jnp.float32),
        "value_raise_weight": bell_draw(arg_keys[15], (RANK, D), (4 * RANK) ** -0.5, 1.0, (), jnp.float32),
        "grad_output": bell_draw(arg_keys[16], (TOKENS, D), 1.0, 6.0, ((0, 32),)),
    }


@jax.custom_vjp
def reduced_rank(v):
    return lax.optimization_barrier(v.astype(jnp.bfloat16)).astype(jnp.float32)

@jax.custom_vjp
def reduced_backward(v):
    return v

def low_keep(v):
    return (reduced_rank(v), None)

def low_pass(kept, grad):
    return (grad,)

def back_keep(v):
    return (v, None)

def back_low(kept, grad):
    return (reduced_rank(grad),)
reduced_rank.defvjp(low_keep, low_pass)
reduced_backward.defvjp(back_keep, back_low)
adapter_scale = 2.0
score_scale = 0.125
norm_eps = 1e-05
masked_score = -1e+30

def matrix_product(left, right):
    return jnp.dot(left, right, precision=lax.Precision.HIGHEST)

def norm_apply(value, norm_gain, norm_shift):
    row_mean = lax.optimization_barrier(jnp.mean(value, axis=-1, keepdims=True))
    centred = value - row_mean
    spread = lax.optimization_barrier(jnp.mean(centred * centred, axis=-1, keepdims=True))
    return centred * lax.rsqrt(spread + norm_eps) * norm_gain + norm_shift

def slot_attention(slot_item):
    query_rows, key_rows, value_rows, valid_len = slot_item
    scores = jnp.einsum('qhe,khe->hqk', query_rows, key_rows, precision=lax.Precision.HIGHEST)
    scores = reduced_backward(score_scale * scores)
    places = jnp.arange(query_rows.shape[0], dtype=jnp.int32) < valid_len
    scores = jnp.where(places[None, None, :], scores, masked_score)
    prob_low = reduced_rank(jax.nn.softmax(scores, axis=-1))
    return jnp.einsum('hqk,khe->qhe', prob_low, value_rows, precision=lax.Precision.HIGHEST)

def layer_block(block_row_span, valid_len, frozen, adapter_factors):
    query_matrix, key_weight, value_matrix, output_weight, inner_weight, outer_weight, attn_gain, attn_shift, ffn_gain, ffn_shift = frozen
    query_down, query_raise_weight, value_down, value_raise_weight = adapter_factors
    row_count = block_row_span.shape[0]
    slot_count = valid_len.shape[0]
    reduced_query = reduced_backward(reduced_rank(matrix_product(block_row_span, query_down)))
    reduced_value = reduced_backward(reduced_rank(matrix_product(block_row_span, value_down)))
    query_rows = reduced_backward(reduced_rank(matrix_product(block_row_span, query_matrix) + adapter_scale * matrix_product(reduced_query, query_raise_weight)))
    key_rows = reduced_backward(reduced_rank(matrix_product(block_row_span, key_weight)))
    value_rows = reduced_backward(reduced_rank(matrix_product(block_row_span, value_matrix) + adapter_scale * matrix_product(reduced_value, value_raise_weight)))

    def heads_view(matrix):
        return matrix.reshape(slot_count, SLOT_LEN, HEADS, HEAD_DIM)
    attn_mixed = lax.map(jax.checkpoint(slot_attention), (heads_view(query_rows), heads_view(key_rows), heads_view(value_rows), valid_len))
    attn_mixed = reduced_backward(reduced_rank(attn_mixed.reshape(row_count, D)))
    attended = reduced_backward(matrix_product(attn_mixed, output_weight))
    first_norm = norm_apply(block_row_span + attended, attn_gain, attn_shift)
    inner_act = reduced_backward(matrix_product(reduced_rank(first_norm), inner_weight))
    active = reduced_rank(jax.nn.gelu(inner_act, approximate=False))
    second_sum = first_norm + reduced_backward(matrix_product(active, outer_weight))
    return norm_apply(second_sum, ffn_gain, ffn_shift)

def reference(inputs, lengths, query_matrix, key_weight, value_matrix, output_weight, inner_weight, outer_weight, attn_gain, attn_shift, ffn_gain, ffn_shift, query_down, query_raise_weight, value_down, value_raise_weight, grad_output):
    frozen = (query_matrix.astype(jnp.float32), key_weight.astype(jnp.float32), value_matrix.astype(jnp.float32), output_weight.astype(jnp.float32), inner_weight.astype(jnp.float32), outer_weight.astype(jnp.float32), attn_gain.astype(jnp.float32), attn_shift.astype(jnp.float32), ffn_gain.astype(jnp.float32), ffn_shift.astype(jnp.float32))
    valid_len = (lengths[:, 0] + lengths[:, 1] + 4).astype(jnp.int32)
    group_size = math.gcd(SLOTS, 8)
    group_count = SLOTS // group_size

    def forward(rows_in, down_q, up_q, down_v, up_v):
        adapter_factors = (reduced_rank(down_q), reduced_rank(up_q), reduced_rank(down_v), reduced_rank(up_v))

        def run_group(group_item):
            return layer_block(group_item[0], group_item[1], frozen, adapter_factors)
        stacked = rows_in.reshape(group_count, group_size * SLOT_LEN, D)
        result = lax.map(jax.checkpoint(run_group), (stacked, valid_len.reshape(group_count, group_size)))
        return result.reshape(TOKENS, D)
    output_rows, pullback = jax.vjp(forward, inputs.astype(jnp.float32), query_down, query_raise_weight, value_down, value_raise_weight)
    gradients = pullback(grad_output.astype(jnp.float32))
    slot_scale = 1.0 / SLOTS
    return (output_rows.astype(jnp.bfloat16), gradients[0], gradients[1] * slot_scale, gradients[2] * slot_scale, gradients[3] * slot_scale, gradients[4] * slot_scale)
```

```python
import functools
import jax
import jax.numpy as jnp
from jax import lax
from jax.experimental import pallas as pl
from jax.experimental.pallas import tpu as pltpu
from jax.sharding import PartitionSpec as P

HEAD_DIM=64; SLOT=512
F32=jnp.float32; BF=jnp.bfloat16
VM=58*1024*1024

def dg(a,b,ca,cb):
    return lax.dot_general(a,b,(((ca,),(cb,)),((),())),preferred_element_type=F32)

def attend_kernel(valid_ref, x_ref, wq_ref, wk_ref, wv_ref, dn_ref, upq_ref, upv_ref,
                  q_ref, k_ref, v_ref, e_ref, ot_ref, o_ref, rt_ref, low_ref, lowv):
    s=pl.program_id(0); j=pl.program_id(1)
    x=x_ref[...]
    @pl.when(j==0)
    def _():
        low=dg(x,dn_ref[...],1,0).astype(BF)
        lowv[...]=low
        low_ref[0]=low.T[:32]
    low=lowv[...]
    q=(dg(x,wq_ref[...],1,0)+2.0*dg(low,upq_ref[...],1,0)).astype(BF)
    k=dg(x,wk_ref[...],1,0).astype(BF)
    v=(dg(x,wv_ref[...],1,0)+2.0*dg(low,upv_ref[...],1,0)).astype(BF)
    q_ref[...]=q; k_ref[...]=k; v_ref[...]=v
    valid=valid_ref[s]
    lane=lax.broadcasted_iota(jnp.int32,(SLOT,128),1)
    row=lax.broadcasted_iota(jnp.int32,(SLOT,128),0)
    bias=jnp.where(row<valid,0.0,-1e30).astype(F32)
    totals=[]
    for p in range(2):
        qp=q[:,128*p:128*p+128].astype(F32)*0.125
        kp=k[:,128*p:128*p+128].astype(F32)
        vp=v[:,128*p:128*p+128].astype(F32)
        for h in range(2):
            own=(lane<64) if h==0 else (lane>=64)
            aux=64 if h==0 else 0
            one=jnp.where(lane==aux,1.0,0.0)
            qm=jnp.where(own,qp,one).astype(BF)
            km=jnp.where(own,kp,jnp.where(lane==aux,bias,0.0)).astype(BF)
            vm=jnp.where(own,vp,one).astype(BF)
            st=dg(km,qm,1,1)
            top=jnp.max(st,axis=0,keepdims=True)
            e=jnp.exp(st-top).astype(BF)
            e_ref[0,2*p+h]=e
            ot=dg(vm,e,0,0)
            total=ot[aux:aux+1]
            r=1.0/total
            totals.append(r)
            lo=64*h
            ob=(ot[lo:lo+64]*r).astype(BF)
            ot_ref[0,128*p+lo:128*p+lo+64]=ob
    o_ref[...]=ot_ref[0].T
    rt_ref[0,0]=jnp.concatenate(totals+totals,axis=0)

def attend(valid,x,wq,wk,wv,dn,upq,upv):
    rows,D=x.shape; S=rows//SLOT; J=D//256; H=D//HEAD_DIM
    gs=pltpu.PrefetchScalarGridSpec(num_scalar_prefetch=1,grid=(S,J),
        in_specs=[pl.BlockSpec((SLOT,D),lambda s,j,_:(s,0)),
                  *[pl.BlockSpec((D,256),lambda s,j,_:(0,j))]*3,
                  pl.BlockSpec((D,128),lambda s,j,_:(0,0)),
                  *[pl.BlockSpec((128,256),lambda s,j,_:(0,j))]*2],
        out_specs=[*[pl.BlockSpec((SLOT,256),lambda s,j,_:(s,j))]*3,
                   pl.BlockSpec((1,4,SLOT,SLOT),lambda s,j,_:(s,j,0,0)),
                   pl.BlockSpec((1,256,SLOT),lambda s,j,_:(s,j,0)),
                   pl.BlockSpec((SLOT,256),lambda s,j,_:(s,j)),
                   pl.BlockSpec((1,1,8,SLOT),lambda s,j,_:(s,j,0,0)),
                   pl.BlockSpec((1,32,SLOT),lambda s,j,_:(s,0,0))],
        scratch_shapes=[pltpu.VMEM((SLOT,128),BF)])
    sd=jax.ShapeDtypeStruct
    return pl.pallas_call(attend_kernel,grid_spec=gs,
        out_shape=[*[sd((rows,D),BF)]*3, sd((S,H,SLOT,SLOT),BF), sd((S,D,SLOT),BF), sd((rows,D),BF),
                   sd((S,J,8,SLOT),F32), sd((S,32,SLOT),BF)],
        compiler_params=pltpu.CompilerParams(vmem_limit_bytes=VM),name="attend")(valid,x,wq,wk,wv,dn,upq,upv)

def norm_stats(value):
    mean=jnp.mean(value,axis=-1,keepdims=True)
    c=value-mean
    r=lax.rsqrt(jnp.mean(c*c,axis=-1,keepdims=True)+1e-5)
    return c*r,r

def norm_back(g,n,r):
    return r*(g-jnp.mean(g,axis=-1,keepdims=True)-n*jnp.mean(g*n,axis=-1,keepdims=True))

def gelu_pair(v):
    a=jnp.abs(v)
    t=1.0/(1.0+(0.3275911*0.7071067811865476)*a)
    ex=jnp.exp(-0.5*v*v)
    poly=t*(0.127414796+t*(-0.142248368+t*(0.7107068705+t*(-0.7265760135+t*0.5307027145))))
    half=poly*ex
    cdf=jnp.where(v>=0,1.0-half,half)
    return v*cdf, cdf+v*(ex*0.3989422804014327)

CH=512
def feed_kernel(x_ref,o_ref,go_ref,wo_ref,wi_ref,wt_ref,nm_ref,out_ref,gfs_ref,gmt_ref,gp_ref):
    ag,ash,fg,fsh=(nm_ref[i:i+1,:] for i in range(4))
    first=x_ref[...].astype(F32)+dg(o_ref[...],wo_ref[...],1,0)
    n1,r1=norm_stats(first)
    h=n1*ag+ash
    hb=h.astype(BF)
    acc=h
    nc=wi_ref.shape[1]//CH
    for c in range(nc):
        z=dg(hb,wi_ref[:,c*CH:(c+1)*CH],1,0)
        act,gp=gelu_pair(z)
        gp_ref[:,c*CH:(c+1)*CH]=gp
        acc=acc+dg(act.astype(BF),wt_ref[c*CH:(c+1)*CH,:],1,0)
    n2,r2=norm_stats(acc)
    out_ref[...]=(n2*fg+fsh).astype(BF)
    g2=norm_back(go_ref[...].astype(F32)*fg,n2,r2)
    g2b=g2.astype(BF)
    acc=g2
    for c in range(nc):
        ga=dg(g2b,wt_ref[c*CH:(c+1)*CH,:],1,1)
        gi=(ga*gp_ref[:,c*CH:(c+1)*CH]).astype(BF)
        acc=acc+dg(gi,wi_ref[:,c*CH:(c+1)*CH],1,1)
    g1=norm_back(acc*ag,n1,r1)
    gfs_ref[...]=g1
    gmt_ref[...]=dg(wo_ref[...],g1.astype(BF),1,1).astype(BF)

def feed(x,o,go,wo,wi,wt,nm,T=256):
    rows,D=x.shape; FF=wi.shape[1]
    sd=jax.ShapeDtypeStruct
    row=pl.BlockSpec((T,D),lambda i:(i,0))
    one=lambda shape: pl.BlockSpec(shape,lambda i:(0,0),pipeline_mode=pl.Buffered(1))
    return pl.pallas_call(feed_kernel,grid=(rows//T,),
        in_specs=[row,row,row,one((D,D)),one((D,FF)),one((FF,D)),one((8,D))],
        out_specs=[row,row,pl.BlockSpec((D,T),lambda i:(0,i))],
        out_shape=[sd((rows,D),BF),sd((rows,D),F32),sd((D,rows),BF)],
        scratch_shapes=[pltpu.VMEM((T,FF),F32)],
        compiler_params=pltpu.CompilerParams(vmem_limit_bytes=VM),name="feed")(x,o,go,wo,wi,wt,nm)

def attend_back_kernel(q_ref,k_ref,v_ref,e_ref,ot_ref,rt_ref,gmt_ref,x_ref,low_ref,upq_ref,upv_ref,
                       dq_ref,dk_ref,dv_ref,gl_ref,ad_ref,glacc):
    s=pl.program_id(0); j=pl.program_id(1); J=pl.num_programs(1)
    lane=lax.broadcasted_iota(jnp.int32,(SLOT,128),1)
    rowi=lax.broadcasted_iota(jnp.int32,(128,SLOT),0)
    dqts=[]
    for p in range(2):
        cols=slice(128*p,128*p+128)
        qp=q_ref[:,cols].astype(F32)*0.125; kp=k_ref[:,cols].astype(F32)*0.125; vp=v_ref[:,cols].astype(F32)
        gm=gmt_ref[cols,:].astype(F32); om=ot_ref[0,cols,:].astype(F32)
        pr=gm*om
        dkp=None; dvp=None; dqt=None
        for h in range(2):
            own=(lane<64) if h==0 else (lane>=64)
            ownr=(rowi<64) if h==0 else (rowi>=64)
            aux=64 if h==0 else 0
            r=rt_ref[0,0,2*p+h:2*p+h+1,:]
            d=-jnp.sum(pr[64*h:64*h+64],axis=0,keepdims=True)*r
            dhi=d.astype(BF).astype(F32)
            dlo=d-dhi
            gs=gm*r
            gaug=jnp.where(ownr,gs,jnp.where(rowi==aux,dhi,jnp.where(rowi==aux+1,dlo,0.0))).astype(BF)
            gown=jnp.where(ownr,gs,0.0).astype(BF)
            vm=jnp.where(own,vp,jnp.where((lane==aux)|(lane==aux+1),1.0,0.0)).astype(BF)
            e=e_ref[0,2*p+h]
            ds=(dg(vm,gaug,1,0)*e.astype(F32)).astype(BF)
            qm=jnp.where(own,qp,0.0).astype(BF)
            km=jnp.where(own,kp,0.0).astype(BF)
            dv=dg(e,gown,1,1)
            dk=dg(ds,qm,1,0)
            dq=dg(km,ds,0,0)
            dvp=dv if dvp is None else dvp+dv
            dkp=dk if dkp is None else dkp+dk
            dqt=dq if dqt is None else dqt+dq
        dk_ref[:,cols]=dkp.astype(BF)
        dv_ref[:,cols]=dvp.astype(BF)
        dqts.append(dqt.astype(BF))
    dqt=jnp.concatenate(dqts,axis=0)
    dqb=dqt.T
    dq_ref[...]=dqb
    dvb=dv_ref[...]
    glq=dg(upq_ref[...],dqt,1,0)
    glv=dg(upv_ref[...],dvb,1,1)
    part=2.0*(glq+glv)
    @pl.when(j==0)
    def _(): glacc[...]=part
    @pl.when(j>0)
    def _(): glacc[...]+=part
    low=low_ref[0]
    c0=pl.multiple_of(j*256,256)
    upq=2.0*dg(low[:16],dqb,1,0)
    upv=2.0*dg(low[:16],dvb,1,0)
    upg=jnp.concatenate([upq[0:8],upv[8:16]],axis=0)
    @pl.when(s==0)
    def _(): ad_ref[16:32,pl.ds(c0,256)]=upg
    @pl.when(s>0)
    def _(): ad_ref[16:32,pl.ds(c0,256)]+=upg
    @pl.when(j==J-1)
    def _():
        gl=glacc[...].astype(BF)
        gl_ref[0]=gl
        dn=dg(gl,x_ref[...],1,0)
        @pl.when(s==0)
        def _(): ad_ref[0:16,:]=dn
        @pl.when(s>0)
        def _(): ad_ref[0:16,:]+=dn

def attend_back(q,k,v,e,ot,rt,gmt,x,low,upq,upv):
    rows,D=x.shape; S=rows//SLOT; J=D//256
    sd=jax.ShapeDtypeStruct
    blk=pl.BlockSpec((SLOT,256),lambda s,j:(s,j))
    return pl.pallas_call(attend_back_kernel,grid=(S,J),
        in_specs=[blk,blk,blk,pl.BlockSpec((1,4,SLOT,SLOT),lambda s,j:(s,j,0,0)),
                  pl.BlockSpec((1,256,SLOT),lambda s,j:(s,j,0)),
                  pl.BlockSpec((1,1,8,SLOT),lambda s,j:(s,j,0,0)),
                  pl.BlockSpec((256,SLOT),lambda s,j:(j,s)),
                  pl.BlockSpec((SLOT,D),lambda s,j:(s,0)),
                  pl.BlockSpec((1,32,SLOT),lambda s,j:(s,0,0)),
                  pl.BlockSpec((16,256),lambda s,j:(0,j)),pl.BlockSpec((16,256),lambda s,j:(0,j))],
        out_specs=[blk,blk,blk,pl.BlockSpec((1,16,SLOT),lambda s,j:(s,0,0)),pl.BlockSpec((32,D),lambda s,j:(0,0))],
        out_shape=[sd((rows,D),BF)]*3+[sd((S,16,SLOT),BF),sd((32,D),F32)],
        scratch_shapes=[pltpu.VMEM((16,SLOT),F32)],
        compiler_params=pltpu.CompilerParams(vmem_limit_bytes=VM),name="attend_back")(q,k,v,e,ot,rt,gmt,x,low,upq,upv)

def inputs_kernel(gfs_ref,dq_ref,dk_ref,dv_ref,gl_ref,wq_ref,wk_ref,wv_ref,dnt_ref,out_ref):
    out_ref[...]=(gfs_ref[...]+dg(dq_ref[...],wq_ref[...],1,1)+dg(dk_ref[...],wk_ref[...],1,1)
        +dg(dv_ref[...],wv_ref[...],1,1)+dg(gl_ref[0],dnt_ref[...],0,0))

def inputs_grad(gfs,dq,dk,dv,gl,wq,wk,wv,dnt):
    rows,D=gfs.shape
    T=SLOT
    row=pl.BlockSpec((T,D),lambda i:(i,0))
    one=lambda shape: pl.BlockSpec(shape,lambda i:(0,0),pipeline_mode=pl.Buffered(1))
    return pl.pallas_call(inputs_kernel,grid=(rows//T,),
        in_specs=[row,row,row,row,pl.BlockSpec((1,16,T),lambda i:(i,0,0)),one((D,D)),one((D,D)),one((D,D)),one((16,D))],
        out_specs=row,out_shape=jax.ShapeDtypeStruct((rows,D),F32),
        compiler_params=pltpu.CompilerParams(vmem_limit_bytes=VM),name="inputs_grad")(gfs,dq,dk,dv,gl,wq,wk,wv,dnt)

def layer(x,valid,wq,wk,wv,wo,wi,wt,ag,ash,fg,fsh,qd,qu,vd,vu,go):
    D=x.shape[1]
    dn16=jnp.concatenate([qd,vd],1).astype(BF)
    dn=jnp.pad(dn16,((0,0),(0,112)))
    qub=qu.astype(BF); vub=vu.astype(BF)
    z8=jnp.zeros_like(qub)
    upq16=jnp.concatenate([qub,z8],0); upv16=jnp.concatenate([z8,vub],0)
    upq=jnp.pad(upq16,((0,112),(0,0))); upv=jnp.pad(upv16,((0,112),(0,0)))
    nm=jnp.pad(jnp.stack([ag,ash,fg,fsh]).astype(F32),((0,4),(0,0)))
    q,k,v,e,ot,o,rt,low=attend(valid,x,wq,wk,wv,dn,upq,upv)
    out,gfs,gmt=feed(x,o,go,wo,wi,wt,nm)
    dq,dk,dv,gl,ad=attend_back(q,k,v,e,ot,rt,gmt,x,low,upq16,upv16)
    gx=inputs_grad(gfs,dq,dk,dv,gl,wq,wk,wv,dn16.T)
    return out,gx,ad


AXES=("dp","fsdp")

def gather_all(pieces):
    width=pieces[0].shape[1]
    packed=jnp.concatenate([p.reshape(-1,width) for p in pieces],0)
    n=lax.axis_size("dp")*lax.axis_size("fsdp")
    got=lax.all_gather(packed,AXES,axis=0,tiled=True).reshape(n,packed.shape[0],width)
    out=[];at=0
    for p in pieces:
        r=p.size//width
        out.append(got[:,at:at+r].reshape(n*p.shape[0],p.shape[1])); at+=r
    return out

def shards(x,lengths,wq,wk,wv,wo,wi,wt,ag,ash,fg,fsh,qd,qu,vd,vu,go):
    valid=lengths[:,0]+lengths[:,1]+4
    wq,wk,wv,wo,wi,wt=gather_all((wq,wk,wv,wo,wi,wt))
    out,gx,ad=layer(x,valid,wq,wk,wv,wo,wi,wt,ag,ash,fg,fsh,qd,qu,vd,vu,go)
    slots=lengths.shape[0]*lax.axis_size("dp")*lax.axis_size("fsdp")
    ad=lax.psum(ad,AXES)/slots
    return out,gx,ad[0:8].T,ad[16:24],ad[8:16].T,ad[24:32]

def solution(mesh):
    sp=P(AXES,None)
    return jax.shard_map(shards,mesh=mesh,in_specs=(sp,)*8+(P(),)*8+(sp,),
        out_specs=(sp,sp,P(),P(),P(),P()),check_vma=False)
```

```python
import functools
import jax
import jax.numpy as jnp
from jax import lax
from jax.experimental import pallas as pl
from jax.experimental.pallas import tpu as pltpu
from jax.sharding import PartitionSpec as P

HEAD_DIM=64; SLOT=512
F32=jnp.float32; BF=jnp.bfloat16
MIB=1024*1024
AXES=("dp","fsdp")
sd=jax.ShapeDtypeStruct
ANY=pl.BlockSpec(memory_space=pl.ANY)
HELD=pl.BlockSpec(memory_space=pltpu.VMEM)
SCALARS=pl.BlockSpec(memory_space=pltpu.SMEM)


def params(mib=56):
    return pltpu.CompilerParams(vmem_limit_bytes=mib*MIB)

def takes(us):
    return pl.CostEstimate(flops=int(us*1.1e9),bytes_accessed=0,transcendentals=0)


def dg(a,b,ca,cb):
    return lax.dot_general(a,b,(((ca,),(cb,)),((),())),preferred_element_type=F32)

def far(v):
    return pltpu.with_memory_space_constraint(v,pltpu.HBM)


def block_copies(layout,me,bufs,outs,sems):
    if layout is None:
        return [[pltpu.make_async_copy(b,o,sems.at[t])] for t,(b,o) in enumerate(zip(bufs,outs))]
    first,second,other_first,other_second=bufs
    chip=lax.div(me,2); core=lax.rem(me,2)
    lists=[[] for _ in layout]
    count=[0]
    def add(lay,buf,at_block,origin,rel):
        dst=lax.bitwise_xor(chip,rel)
        half=buf.shape[-1]
        at=0
        for t,(bands,rows,start,size) in enumerate(lay):
            for b in range(bands):
                to=outs[t].at[pl.ds(pl.multiple_of(dst*rows+start,16),size),pl.ds(pl.multiple_of(2*half*b+origin*half,128),half)]
                lists[t].append(pltpu.make_async_copy(buf.at[at_block,pl.ds(at,size),:],to,sems.at[count[0]]))
                count[0]+=1
                at+=size
    for which,(near,far) in enumerate(((first,second),(other_first,other_second))):
        origin=core if which==0 else 1-core
        near_axis=1+origin
        far_axis=2-origin
        for hop,buf in enumerate((near,far)):
            for i in range(8):
                add(layout,buf,i,origin,hop*far_axis+(i//4)*near_axis+4*(i%4))
    return lists

def start_all(copies):
    for c in copies: c.start()

def wait_all(copies):
    for c in copies: c.wait()

def copy_count(layout):
    return 2 if layout is None else 32*sum(l[0] for l in layout)

def prep_kernel(qdt_ref,vdt_ref,qu_ref,vu_ref,ag_ref,ash_ref,fg_ref,fsh_ref,dn_ref,upq_ref,upv_ref,dnt_ref,nm_ref):
    D=qu_ref.shape[1]
    both=jnp.concatenate([qdt_ref[...],vdt_ref[...]],axis=0)
    dnt_ref[...]=both.astype(BF)
    dn_ref[...]=jnp.concatenate([both,jnp.zeros((112,D),F32)],axis=0).T.astype(BF)
    z8=jnp.zeros((8,D),F32); z=jnp.zeros((112,D),F32)
    upq_ref[...]=jnp.concatenate([qu_ref[...],z8,z],axis=0).astype(BF)
    upv_ref[...]=jnp.concatenate([z8,vu_ref[...],z],axis=0).astype(BF)
    for i,r in enumerate((ag_ref,ash_ref,fg_ref,fsh_ref)):
        nm_ref[i:i+1,:]=r[...].astype(F32)
    nm_ref[4:8,:]=jnp.zeros((4,D),F32)

def prep(qd,qu,vd,vu,ag,ash,fg,fsh):
    D=qu.shape[1]
    return pl.pallas_call(prep_kernel,out_shape=[sd((D,128),BF),sd((128,D),BF),sd((128,D),BF),sd((16,D),BF),sd((8,D),F32)],
        compiler_params=params(8),cost_estimate=takes(1),name="prep")(qd.T,vd.T,qu,vu,*(v.reshape(1,D) for v in (ag,ash,fg,fsh)))


def project_kernel(layout,sc_ref,x_ref,dn_ref,upq_ref,upv_ref,*rest):
    *blocks,qkv_ref,low_ref,wo,w,sems,osem=rest
    i=pl.program_id(0)
    D=x_ref.shape[1]
    whole=[pltpu.make_async_copy(w,wo,osem.at[0])]
    @pl.when(i==0)
    def _():
        copies,=block_copies(layout,sc_ref[0],blocks,(w,),sems)
        start_all(copies); wait_all(copies); start_all(whole)
    x=x_ref[...]
    rows=pl.ds(pl.multiple_of(i*SLOT,SLOT),SLOT)
    low=dg(x,dn_ref[...],1,0).astype(BF)
    low_ref[...]=low.T[:32]
    qkv_ref[rows,0:D]=(dg(x,w[:,0:D],1,0)+2.0*dg(low,upq_ref[...],1,0)).astype(BF)
    qkv_ref[rows,D:2*D]=dg(x,w[:,D:2*D],1,0).astype(BF)
    qkv_ref[rows,2*D:]=(dg(x,w[:,2*D:],1,0)+2.0*dg(low,upv_ref[...],1,0)).astype(BF)
    @pl.when(i==pl.num_programs(0)-1)
    def _(): wait_all(whole)

def project(scalars,x,dn,upq,upv,blocks,layout):
    rows,D=x.shape
    return pl.pallas_call(functools.partial(project_kernel,layout),grid=(rows//SLOT,),
        in_specs=[SCALARS,pl.BlockSpec((SLOT,D),lambda i:(i,0)),HELD,HELD,HELD]+[ANY]*len(blocks),
        out_specs=[HELD,pl.BlockSpec((32,SLOT),lambda i:(0,i)),ANY],
        out_shape=[sd((rows,3*D),BF),sd((32,rows),BF),pltpu.HBM((D,3*D),BF)],
        scratch_shapes=[pltpu.VMEM((D,3*D),BF),pltpu.SemaphoreType.DMA((copy_count(layout),)),pltpu.SemaphoreType.DMA((1,))],
        compiler_params=params(LIM["project"]),cost_estimate=takes(8),name="project")(scalars,x,dn,upq,upv,*map(far,blocks))

def attend_kernel(sc_ref,qkv_ref,e_ref,ot_ref,o_ref,rt_ref):
    s=pl.program_id(0); j=pl.program_id(1); J=pl.num_programs(1); D=256*J
    lane=lax.broadcasted_iota(jnp.int32,(SLOT,128),1)
    row=lax.broadcasted_iota(jnp.int32,(SLOT,128),0)
    bias=jnp.where(row<sc_ref[1+s],0.0,-1e30).astype(F32)
    rows=pl.ds(pl.multiple_of(s*SLOT,SLOT),SLOT)
    def part(which,p):
        return qkv_ref[rows,pl.ds(pl.multiple_of(which*D+256*j+128*p,128),128)].astype(F32)
    totals=[]; os=[]
    for p in range(2):
        qp=part(0,p)*0.125
        kp=part(1,p)
        vp=part(2,p)
        for h in range(2):
            own=(lane<64) if h==0 else (lane>=64)
            aux=64 if h==0 else 0
            one=jnp.where(lane==aux,1.0,0.0)
            qm=jnp.where(own,qp,one).astype(BF)
            km=jnp.where(own,kp,jnp.where(lane==aux,bias,0.0)).astype(BF)
            vm=jnp.where(own,vp,one).astype(BF)
            st=dg(km,qm,1,1)
            top=jnp.max(st,axis=0,keepdims=True)
            e=jnp.exp(st-top).astype(BF)
            e_ref[2*p+h]=e
            ot=dg(vm,e,0,0)
            r=1.0/ot[aux:aux+1]
            totals.append(r)
            lo=64*h
            os.append((ot[lo:lo+64]*r).astype(BF))
    ot=jnp.concatenate(os,axis=0)
    ot_ref[...]=ot
    o_ref[rows,pl.ds(pl.multiple_of(256*j,256),256)]=ot.T
    rt_ref[0]=jnp.concatenate(totals+totals,axis=0)

def attend(scalars,qkv,slots):
    rows=qkv.shape[0]; D=qkv.shape[1]//3; J=D//256; H=D//HEAD_DIM
    return pl.pallas_call(attend_kernel,grid=(slots,J),
        in_specs=[SCALARS,HELD],
        out_specs=[pl.BlockSpec((4,SLOT,SLOT),lambda s,j:(s*J+j,0,0)),pl.BlockSpec((256,SLOT),lambda s,j:(s*J+j,0)),HELD,pl.BlockSpec((1,8,SLOT),lambda s,j:(s*J+j,0,0))],
        out_shape=[pltpu.HBM((slots*H,SLOT,SLOT),BF),pltpu.HBM((slots*D,SLOT),BF),pltpu.VMEM((rows,D),BF),pltpu.HBM((slots*J,8,SLOT),F32)],
        compiler_params=params(LIM["attend"]),cost_estimate=takes(16),name="attend")(scalars,qkv)


def norm_stats(value):
    mean=jnp.mean(value,axis=-1,keepdims=True)
    c=value-mean
    r=lax.rsqrt(jnp.mean(c*c,axis=-1,keepdims=True)+1e-5)
    return c*r,r

def norm_back(g,n,r):
    return r*(g-jnp.mean(g,axis=-1,keepdims=True)-n*jnp.mean(g*n,axis=-1,keepdims=True))

def gelu_pair(v):
    cdf=0.5+0.5*lax.erf(v*0.7071067811865476)
    return v*cdf, cdf+(0.3989422804014327*v)*jnp.exp(-0.5*v*v)

CH=512
TILE=256
LIM={"project":20,"attend":24,"feed_in":16,"feed_out":24,"attend_back":24,"inputs_grad":24}

def feed_in_kernel(layout,sc_ref,x_ref,o_ref,nm_ref,*rest):
    *blocks,n1_ref,r1_ref,act_ref,gp_ref,wo,wi,sems=rest
    i=pl.program_id(0)
    @pl.when(i==0)
    def _():
        lists=block_copies(layout,sc_ref[0],blocks,(wo,wi),sems)
        for l in lists: start_all(l)
        for l in lists: wait_all(l)
    T=x_ref.shape[0]
    rows=pl.ds(pl.multiple_of(i*T,T),T)
    first=x_ref[...].astype(F32)+dg(o_ref[rows,:],wo[...],1,0)
    n1,r1=norm_stats(first)
    n1_ref[rows,:]=n1; r1_ref[rows,:]=jnp.broadcast_to(r1,(T,128))
    hb=(n1*nm_ref[0:1,:]+nm_ref[1:2,:]).astype(BF)
    for c in range(wi.shape[1]//CH):
        z=dg(hb,wi[:,c*CH:(c+1)*CH],1,0)
        act,gp=gelu_pair(z)
        act_ref[rows,c*CH:(c+1)*CH]=act.astype(BF)
        gp_ref[rows,c*CH:(c+1)*CH]=gp.astype(BF)

def feed_in(scalars,x,o,nm,blocks,layout,FF):
    rows,D=x.shape
    return pl.pallas_call(functools.partial(feed_in_kernel,layout),grid=(rows//TILE,),
        in_specs=[SCALARS,pl.BlockSpec((TILE,D),lambda i:(i,0)),HELD,HELD]+[ANY]*len(blocks),
        out_specs=[HELD]*6,
        out_shape=[pltpu.VMEM((rows,D),F32),pltpu.VMEM((rows,128),F32),pltpu.VMEM((rows,FF),BF),pltpu.VMEM((rows,FF),BF),pltpu.VMEM((D,D),BF),pltpu.VMEM((D,FF),BF)],
        scratch_shapes=[pltpu.SemaphoreType.DMA((copy_count(layout),))],
        compiler_params=params(LIM["feed_in"]),cost_estimate=takes(17),name="feed_in")(scalars,x,o,nm,*map(far,blocks))

def feed_out_kernel(layout,sc_ref,n1_ref,r1_ref,act_ref,gp_ref,go_ref,nm_ref,wo,wi,*rest):
    *blocks,out_ref,gfs_ref,gmt_ref,wt,gi_ref,sems=rest
    i=pl.program_id(0)
    @pl.when(i==0)
    def _():
        copies,=block_copies(layout,sc_ref[0],blocks,(wt,),sems)
        start_all(copies); wait_all(copies)
    T=go_ref.shape[0]
    rows=pl.ds(pl.multiple_of(i*T,T),T)
    ag,ash,fg,fsh=(nm_ref[i:i+1,:] for i in range(4))
    n1=n1_ref[rows,:]; r1=r1_ref[rows,0:1]
    acc=n1*ag+ash+dg(act_ref[rows,:],wt[...],1,0)
    n2,r2=norm_stats(acc)
    out_ref[...]=(n2*fg+fsh).astype(BF)
    g2=norm_back(go_ref[...].astype(F32)*fg,n2,r2)
    g2b=g2.astype(BF)
    for c in range(wi.shape[1]//CH):
        ga=dg(g2b,wt[c*CH:(c+1)*CH,:],1,1)
        gi_ref[:,c*CH:(c+1)*CH]=(ga*gp_ref[rows,c*CH:(c+1)*CH].astype(F32)).astype(BF)
    g1=norm_back((g2+dg(gi_ref[...],wi[...],1,1))*ag,n1,r1)
    gfs_ref[...]=g1
    gmt_ref[:,rows]=dg(wo[...],g1.astype(BF),1,1).astype(BF)

def feed_out(scalars,n1,r1,act,gp,go,wo,wi,nm,blocks,layout):
    rows,D=n1.shape; FF=wi.shape[1]
    row=pl.BlockSpec((TILE,D),lambda i:(i,0))
    return pl.pallas_call(functools.partial(feed_out_kernel,layout),grid=(rows//TILE,),
        in_specs=[SCALARS,HELD,HELD,HELD,HELD,row,HELD,HELD,HELD]+[ANY]*len(blocks),
        out_specs=[row,row,HELD],
        out_shape=[sd((rows,D),BF),pltpu.HBM((rows,D),F32),pltpu.VMEM((D,rows),BF)],
        scratch_shapes=[pltpu.VMEM((FF,D),BF),pltpu.VMEM((TILE,FF),BF),pltpu.SemaphoreType.DMA((copy_count(layout),))],
        compiler_params=params(LIM["feed_out"]),cost_estimate=takes(28),name="feed_out")(scalars,n1,r1,act,gp,go,nm,wo,wi,*map(far,blocks))


def attend_back_kernel(sc_ref,q_ref,k_ref,v_ref,e_ref,ot_ref,rt_ref,gmt_ref,x_ref,low_ref,upq_ref,upv_ref,
                       d_ref,gl_ref,mine_ref,other_ref,glacc,ad_ref):
    s=pl.program_id(0); j=pl.program_id(1); J=pl.num_programs(1)
    lane=lax.broadcasted_iota(jnp.int32,(SLOT,128),1)
    rowi=lax.broadcasted_iota(jnp.int32,(128,SLOT),0)
    D=256*J
    rows=pl.ds(pl.multiple_of(s*SLOT,SLOT),SLOT)
    def place_of(which,p):
        return rows,pl.ds(pl.multiple_of(which*D+256*j+128*p,128),128)
    gmq=gmt_ref[pl.ds(pl.multiple_of(256*j,256),256),rows]
    otq=ot_ref[...]
    dqts=[]; dvs=[]
    for p in range(2):
        cols=slice(128*p,128*p+128)
        qp,kp,vp=(w[:,cols].astype(F32) for w in (q_ref,k_ref,v_ref))
        qp=qp*0.125; kp=kp*0.125
        gm=gmq[cols,:].astype(F32); om=otq[cols,:].astype(F32)
        pr=gm*om
        dkp=None; dvp=None; dqt=None
        for h in range(2):
            own=(lane<64) if h==0 else (lane>=64)
            ownr=(rowi<64) if h==0 else (rowi>=64)
            aux=64 if h==0 else 0
            r=rt_ref[0,2*p+h:2*p+h+1,:]
            d=-jnp.sum(pr[64*h:64*h+64],axis=0,keepdims=True)*r
            dhi=d.astype(BF).astype(F32)
            dlo=d-dhi
            gs=gm*r
            gaug=jnp.where(ownr,gs,jnp.where(rowi==aux,dhi,jnp.where(rowi==aux+1,dlo,0.0))).astype(BF)
            gown=jnp.where(ownr,gs,0.0).astype(BF)
            vm=jnp.where(own,vp,jnp.where((lane==aux)|(lane==aux+1),1.0,0.0)).astype(BF)
            e=e_ref[2*p+h]
            ds=(dg(vm,gaug,1,0)*e.astype(F32)).astype(BF)
            qm=jnp.where(own,qp,0.0).astype(BF)
            km=jnp.where(own,kp,0.0).astype(BF)
            dv=dg(e,gown,1,1)
            dk=dg(ds,qm,1,0)
            dq=dg(km,ds,0,0)
            dvp=dv if dvp is None else dvp+dv
            dkp=dk if dkp is None else dkp+dk
            dqt=dq if dqt is None else dqt+dq
        d_ref[place_of(1,p)]=dkp.astype(BF)
        dvs.append(dvp.astype(BF))
        d_ref[place_of(2,p)]=dvs[p]
        dqts.append(dqt.astype(BF))
    dqt=jnp.concatenate(dqts,axis=0)
    dqb=dqt.T
    d_ref[rows,pl.ds(pl.multiple_of(256*j,256),256)]=dqb
    dvb=jnp.concatenate(dvs,axis=1)
    glq=dg(upq_ref[...],dqt,1,0)
    glv=dg(upv_ref[...],dvb,1,1)
    part=2.0*(glq+glv)
    @pl.when(j==0)
    def _(): glacc[...]=part
    @pl.when(j>0)
    def _(): glacc[...]+=part
    low=low_ref[...]
    c0=pl.multiple_of(j*256,256)
    upq=2.0*dg(low[:16],dqb,1,0)
    upv=2.0*dg(low[:16],dvb,1,0)
    upg=jnp.concatenate([upq[0:8],upv[8:16]],axis=0)
    def add(rows,cols,v):
        @pl.when(s==0)
        def _(): ad_ref[rows,cols]=v
        @pl.when(s>0)
        def _(): ad_ref[rows,cols]+=v
    add(slice(16,32),pl.ds(c0,256),upg)
    @pl.when(j==J-1)
    def _():
        gl=glacc[...].astype(BF)
        gl_ref[...]=gl
        add(slice(0,16),slice(None),dg(gl,x_ref[...],1,0))
        core=lax.rem(sc_ref[0],2)
        for c,(a,b) in enumerate(((mine_ref,other_ref),(other_ref,mine_ref))):
            @pl.when((s==pl.num_programs(0)-1)&(core==c))
            def _():
                a[...]=ad_ref[0:16,:]
                b[...]=ad_ref[16:32,:]

def attend_back(scalars,qkv,e,ot,rt,gmt,x,low,upq,upv):
    rows,D=x.shape; J=D//256; S=rows//SLOT
    up=pl.BlockSpec((16,256),lambda s,j:(0,j))
    return pl.pallas_call(attend_back_kernel,grid=(S,J),
        in_specs=[SCALARS,*[pl.BlockSpec((SLOT,256),lambda s,j,w=w:(s,w*J+j)) for w in range(3)],
                  pl.BlockSpec((4,SLOT,SLOT),lambda s,j:(s*J+j,0,0)),pl.BlockSpec((256,SLOT),lambda s,j:(s*J+j,0)),
                  pl.BlockSpec((1,8,SLOT),lambda s,j:(s*J+j,0,0)),HELD,
                  pl.BlockSpec((SLOT,D),lambda s,j:(s,0)),pl.BlockSpec((32,SLOT),lambda s,j:(0,s)),up,up],
        out_specs=[HELD,pl.BlockSpec((16,SLOT),lambda s,j:(0,s)),HELD,HELD],
        out_shape=[pltpu.VMEM((rows,3*D),BF),sd((16,rows),BF),pltpu.VMEM((16,D),F32),pltpu.VMEM((16,D),F32)],
        scratch_shapes=[pltpu.VMEM((16,SLOT),F32),pltpu.VMEM((32,D),F32)],
        compiler_params=params(LIM["attend_back"]),cost_estimate=takes(18),name="attend_back")(scalars,far(qkv),far(qkv),far(qkv),far(e),far(ot),rt,gmt,x,low,upq,upv)

def inputs_kernel(gfs_ref,d_ref,gl,w_ref,dnt_ref,out_ref):
    T=gfs_ref.shape[0]
    rows=pl.ds(pl.multiple_of(pl.program_id(0)*T,T),T)
    out_ref[...]=gfs_ref[...]+dg(d_ref[rows,:],w_ref[...],1,1)+dg(gl[...],dnt_ref[...],0,0)

def inputs_grad(gfs,d,gl,w,dnt):
    rows,D=gfs.shape
    row=pl.BlockSpec((SLOT,D),lambda i:(i,0))
    return pl.pallas_call(inputs_kernel,grid=(rows//SLOT,),
        in_specs=[row,HELD,pl.BlockSpec((16,SLOT),lambda i:(0,i)),HELD,HELD],
        out_specs=row,out_shape=sd((rows,D),F32),
        compiler_params=params(LIM["inputs_grad"]),cost_estimate=takes(7),name="inputs_grad")(gfs,d,gl,w,dnt)


def device_count():
    return lax.axis_size("dp")*lax.axis_size("fsdp")

def permute(v,target):
    return lax.ppermute(v,AXES,[(i,target(i)) for i in range(device_count())])

def exchange(v,mask):
    return permute(v,lambda i:i^mask)

def along_z(block):
    top=device_count()//4
    return [block]+[exchange(block,top*m) for m in (1,2,3)]

def near_hop(v):
    return permute(v,lambda i:i^(4 if i%2 else 2))

def far_hop(v):
    return permute(v,lambda i:i^(2 if i%2 else 4))

def core_pair(v):
    groups=[[2*i,2*i+1] for i in range(lax.axis_size("fsdp")//2)]
    return lax.all_gather(v,"fsdp",axis=0,tiled=False,axis_index_groups=groups)

def column_half(both):
    c=lax.axis_index("fsdp")%2
    half=both.shape[2]//2
    return lax.dynamic_slice_in_dim(both,c*half,half,axis=2).reshape(-1,half)

def total_over_devices(mine,other,meanwhile):
    n=device_count()
    mine=mine+exchange(other,1)
    got=[exchange(mine,m) for m in range(2,n//4,2)]
    for g in got: mine=mine+g
    got=[exchange(mine,m) for m in (n//4,n//2,3*n//4)]
    got,done=tie(got,meanwhile())
    for g in got: mine=mine+g
    return mine,exchange(mine,1),done

def finish_kernel(scale,sc_ref,mine_ref,other_ref,*outs):
    core=lax.rem(sc_ref[0],2)
    for c,halves in enumerate(((mine_ref,other_ref),(other_ref,mine_ref))):
        @pl.when(core==c)
        def _():
            for i,o in enumerate(outs): o[...]=halves[i//2][8*(i%2):8*(i%2)+8,:]*scale

def finish(scalars,mine,other,scale):
    D=mine.shape[1]
    return pl.pallas_call(functools.partial(finish_kernel,scale),in_specs=[SCALARS,HELD,HELD],out_specs=[HELD]*4,
        out_shape=[sd((8,D),F32)]*4,compiler_params=params(8),cost_estimate=takes(1),name="finish")(scalars,mine,other)

def tie(*v):
    return lax.optimization_barrier(v)

def by_hops(scalars,x,wq,wk,wv,wo,wi,wt,ag,ash,fg,fsh,qd,qu,vd,vu,go):
    D=wq.shape[1]; FF=wi.shape[1]; bands=FF//D; r=wq.shape[0]; rt_=wt.shape[0]
    top=device_count()//4
    both=core_pair(jnp.concatenate([wq,wk,wv],0))
    s1=jnp.concatenate([column_half(both[:,r*t:r*t+r]) for t in range(3)],0)
    z1=along_z(s1)
    wo,wi,wt,qd,s1=tie(wo,wi,wt,qd,s1)
    bo,bi,bt=core_pair(wo),core_pair(wi),core_pair(wt)
    s2=jnp.concatenate([column_half(bo)]+[column_half(bi[:,:,D*t:D*t+D]) for t in range(bands)],0)
    s3=column_half(bt)
    dn,upq,upv,dnt,nm=prep(qd,qu,vd,vu,ag,ash,fg,fsh)
    z1,s2,s3,dn,scalars=tie(z1,s2,s3,dn,scalars)
    a1=jnp.stack(z1,0)
    n1=near_hop(a1)
    z22=exchange(s2,2*top)
    n1,z22,s2=tie(n1,z22,s2)
    f1=jnp.concatenate([a1,n1],0)
    h1=far_hop(f1); of1=exchange(f1,1)
    z23=exchange(s2,3*top); z21=exchange(s2,top)
    h1,of1,z23,z21,s3=tie(h1,of1,z23,z21,s3)
    oh1=exchange(h1,1)
    a2=jnp.stack([s2,z21,z22,z23],0)
    n2=near_hop(a2)
    z31,z32,z33=(exchange(s3,m*top) for m in (1,2,3))
    oh1,=tie(oh1)
    qkv,low,wqkv=project(scalars,x,dn,upq,upv,(f1,h1,of1,oh1),((3,2*r,0,2*r),))
    n2,qkv,z31,z32,z33,s3=tie(n2,qkv,z31,z32,z33,s3)
    f2=jnp.concatenate([a2,n2],0)
    h2=far_hop(f2); of2=exchange(f2,1)
    a3=jnp.stack([s3,z31,z32,z33],0)
    n3=near_hop(a3)
    e,ot,o,rt=attend(scalars,qkv,x.shape[0]//SLOT)
    h2,o,of2=tie(h2,o,of2)
    oh2=exchange(h2,1)
    n3,oh2=tie(n3,oh2)
    f3=jnp.concatenate([a3,n3],0)
    h3=far_hop(f3); of3=exchange(f3,1)
    nn,r1,act,gp,wo,wi=feed_in(scalars,x,o,nm,(f2,h2,of2,oh2),((1,2*r,0,2*r),(bands,2*r,0,2*r)),FF)
    h3,nn,of3=tie(h3,nn,of3)
    oh3=exchange(h3,1)
    out,gfs,gmt=feed_out(scalars,nn,r1,act,gp,go,wo,wi,nm,(f3,h3,of3,oh3),((1,2*rt_,0,2*rt_),))
    return qkv,low,wqkv,e,ot,rt,out,gfs,gmt,upq,upv,dnt

def by_all_gather(scalars,x,wq,wk,wv,wo,wi,wt,ag,ash,fg,fsh,qd,qu,vd,vu,go):
    wq,wk,wv,wo,wi,wt=(lax.all_gather(w,AXES,axis=0,tiled=True) for w in (wq,wk,wv,wo,wi,wt))
    dn,upq,upv,dnt,nm=prep(qd,qu,vd,vu,ag,ash,fg,fsh)
    qkv,low,wqkv=project(scalars,x,dn,upq,upv,(jnp.concatenate([wq,wk,wv],1),),None)
    e,ot,o,rt=attend(scalars,qkv,x.shape[0]//SLOT)
    nn,r1,act,gp,wo,wi=feed_in(scalars,x,o,nm,(wo,wi),None,wi.shape[1])
    out,gfs,gmt=feed_out(scalars,nn,r1,act,gp,go,wo,wi,nm,(wt,),None)
    return qkv,low,wqkv,e,ot,rt,out,gfs,gmt,upq,upv,dnt

def shards(x,lengths,wq,wk,wv,wo,wi,wt,ag,ash,fg,fsh,qd,qu,vd,vu,go):
    n=device_count()
    valid=lengths[:,0]+lengths[:,1]+4
    me=(lax.axis_index("dp")*lax.axis_size("fsdp")+lax.axis_index("fsdp")).reshape(1)
    scalars=jnp.concatenate([me,valid]).astype(jnp.int32)
    forward=by_hops if n==32 and wq.shape[0]%8==0 else by_all_gather
    qkv,low,wqkv,e,ot,rt,out,gfs,gmt,upq,upv,dnt=forward(scalars,x,wq,wk,wv,wo,wi,wt,ag,ash,fg,fsh,qd,qu,vd,vu,go)
    d,gl,mine,other=attend_back(scalars,qkv,e,ot,rt,gmt,x,low,upq,upv)
    mine,other,gx=total_over_devices(mine,other,lambda: inputs_grad(gfs,d,gl,wqkv,dnt))
    qd,vd,qu,vu=finish(scalars,mine,other,1.0/(lengths.shape[0]*n))
    return out,gx,qd.T,qu,vd.T,vu

def solution(mesh):
    sp=P(AXES,None)
    return jax.shard_map(shards,mesh=mesh,in_specs=(sp,)*8+(P(),)*8+(sp,),
        out_specs=(sp,sp,P(),P(),P(),P()),check_vma=False)
```

```python
import functools
import jax
import jax.numpy as jnp
from jax import lax
from jax.experimental import pallas as pl
from jax.experimental.pallas import tpu as pltpu
from jax.sharding import PartitionSpec as P

HEAD_DIM=64; SLOT=512
F32=jnp.float32; BF=jnp.bfloat16
MIB=1024*1024
AXES=("dp","fsdp")
sd=jax.ShapeDtypeStruct
ANY=pl.BlockSpec(memory_space=pl.ANY)
HELD=pl.BlockSpec(memory_space=pltpu.VMEM)
SCALARS=pl.BlockSpec(memory_space=pltpu.SMEM)


def params(mib=56):
    return pltpu.CompilerParams(vmem_limit_bytes=mib*MIB)

def takes(us):
    return pl.CostEstimate(flops=int(us*1.1e9),bytes_accessed=0,transcendentals=0)


def dg(a,b,ca,cb):
    return lax.dot_general(a,b,(((ca,),(cb,)),((),())),preferred_element_type=F32)

def far(v):
    return pltpu.with_memory_space_constraint(v,pltpu.HBM)


def block_copies(layout,me,bufs,outs,sems,near_inside=False):
    if layout is None:
        return [[pltpu.make_async_copy(b,o,sems.at[t])] for t,(b,o) in enumerate(zip(bufs,outs))]
    first,second,other_first,other_second=bufs
    chip=lax.div(me,2); core=lax.rem(me,2)
    lists=[[] for _ in layout]
    count=[0]
    def add(lay,buf,at_block,origin,rel):
        dst=lax.bitwise_xor(chip,rel)
        half=buf.shape[-1]
        at=0
        for t,(bands,rows,start,size) in enumerate(lay):
            for b in range(bands):
                to=outs[t].at[pl.ds(pl.multiple_of(dst*rows+start,16),size),pl.ds(pl.multiple_of(2*half*b+origin*half,128),half)]
                lists[t].append(pltpu.make_async_copy(buf.at[at_block,pl.ds(at,size),:],to,sems.at[count[0]]))
                count[0]+=1
                at+=size
    for which,(near,far) in enumerate(((first,second),(other_first,other_second))):
        origin=core if which==0 else 1-core
        near_axis=1+origin
        far_axis=2-origin
        for hop,buf in enumerate((near,far)):
            for i in range(8):
                n,z=(i%2,i//2) if near_inside else (i//4,i%4)
                add(layout,buf,i,origin,hop*far_axis+n*near_axis+4*z)
    return lists

def start_all(copies):
    for c in copies: c.start()

def wait_all(copies):
    for c in copies: c.wait()

def copy_count(layout):
    return 2 if layout is None else 32*sum(l[0] for l in layout)

def prep_kernel(qdt_ref,vdt_ref,qu_ref,vu_ref,ag_ref,ash_ref,fg_ref,fsh_ref,dn_ref,upq_ref,upv_ref,dnt_ref,nm_ref):
    D=qu_ref.shape[1]
    both=jnp.concatenate([qdt_ref[...],vdt_ref[...]],axis=0)
    dnt_ref[...]=both.astype(BF)
    dn_ref[...]=jnp.concatenate([both,jnp.zeros((112,D),F32)],axis=0).T.astype(BF)
    z8=jnp.zeros((8,D),F32); z=jnp.zeros((112,D),F32)
    upq_ref[...]=jnp.concatenate([qu_ref[...],z8,z],axis=0).astype(BF)
    upv_ref[...]=jnp.concatenate([z8,vu_ref[...],z],axis=0).astype(BF)
    for i,r in enumerate((ag_ref,ash_ref,fg_ref,fsh_ref)):
        nm_ref[i:i+1,:]=r[...].astype(F32)
    nm_ref[4:8,:]=jnp.zeros((4,D),F32)

def prep(qd,qu,vd,vu,ag,ash,fg,fsh):
    D=qu.shape[1]
    return pl.pallas_call(prep_kernel,out_shape=[sd((D,128),BF),sd((128,D),BF),sd((128,D),BF),sd((16,D),BF),sd((8,D),F32)],
        compiler_params=params(8),cost_estimate=takes(1),name="prep")(qd.T,vd.T,qu,vu,*(v.reshape(1,D) for v in (ag,ash,fg,fsh)))


def project_kernel(layout,sc_ref,x_ref,dn_ref,upq_ref,upv_ref,*rest):
    *blocks,qkv_ref,low_ref,wo,w,sems,osem=rest
    i=pl.program_id(0)
    D=x_ref.shape[1]
    whole=[pltpu.make_async_copy(w,wo,osem.at[0])]
    @pl.when(i==0)
    def _():
        copies,=block_copies(layout,sc_ref[0],blocks,(w,),sems)
        start_all(copies); wait_all(copies); start_all(whole)
    x=x_ref[...]
    rows=pl.ds(pl.multiple_of(i*SLOT,SLOT),SLOT)
    low=dg(x,dn_ref[...],1,0).astype(BF)
    low_ref[...]=low.T[:32]
    qkv_ref[rows,0:D]=(dg(x,w[:,0:D],1,0)+2.0*dg(low,upq_ref[...],1,0)).astype(BF)
    qkv_ref[rows,D:2*D]=dg(x,w[:,D:2*D],1,0).astype(BF)
    qkv_ref[rows,2*D:]=(dg(x,w[:,2*D:],1,0)+2.0*dg(low,upv_ref[...],1,0)).astype(BF)
    @pl.when(i==pl.num_programs(0)-1)
    def _(): wait_all(whole)

def project(scalars,x,dn,upq,upv,blocks,layout):
    rows,D=x.shape
    return pl.pallas_call(functools.partial(project_kernel,layout),grid=(rows//SLOT,),
        in_specs=[SCALARS,pl.BlockSpec((SLOT,D),lambda i:(i,0)),HELD,HELD,HELD]+[ANY]*len(blocks),
        out_specs=[HELD,pl.BlockSpec((32,SLOT),lambda i:(0,i)),ANY],
        out_shape=[sd((rows,3*D),BF),sd((32,rows),BF),pltpu.HBM((D,3*D),BF)],
        scratch_shapes=[pltpu.VMEM((D,3*D),BF),pltpu.SemaphoreType.DMA((copy_count(layout),)),pltpu.SemaphoreType.DMA((1,))],
        compiler_params=params(LIM["project"]),cost_estimate=takes(8),name="project")(scalars,x,dn,upq,upv,*blocks)

def attend_kernel(sc_ref,qkv_ref,e_ref,ot_ref,o_ref,rt_ref):
    s=pl.program_id(0); j=pl.program_id(1); J=pl.num_programs(1); D=256*J
    lane=lax.broadcasted_iota(jnp.int32,(SLOT,128),1)
    row=lax.broadcasted_iota(jnp.int32,(SLOT,128),0)
    bias=jnp.where(row<sc_ref[1+s],0.0,-1e30).astype(F32)
    rows=pl.ds(pl.multiple_of(s*SLOT,SLOT),SLOT)
    def part(which,p):
        return qkv_ref[rows,pl.ds(pl.multiple_of(which*D+256*j+128*p,128),128)].astype(F32)
    totals=[]; os=[]
    for p in range(2):
        qp=part(0,p)*0.125
        kp=part(1,p)
        vp=part(2,p)
        for h in range(2):
            own=(lane<64) if h==0 else (lane>=64)
            aux=64 if h==0 else 0
            one=jnp.where(lane==aux,1.0,0.0)
            qm=jnp.where(own,qp,one).astype(BF)
            km=jnp.where(own,kp,jnp.where(lane==aux,bias,0.0)).astype(BF)
            vm=jnp.where(own,vp,one).astype(BF)
            st=dg(km,qm,1,1)
            top=jnp.max(st,axis=0,keepdims=True)
            e=jnp.exp(st-top).astype(BF)
            e_ref[2*p+h]=e
            ot=dg(vm,e,0,0)
            r=1.0/ot[aux:aux+1]
            totals.append(r)
            lo=64*h
            os.append((ot[lo:lo+64]*r).astype(BF))
    ot=jnp.concatenate(os,axis=0)
    ot_ref[...]=ot
    o_ref[rows,pl.ds(pl.multiple_of(256*j,256),256)]=ot.T
    rt_ref[0]=jnp.concatenate(totals+totals,axis=0)

def attend(scalars,qkv,slots):
    rows=qkv.shape[0]; D=qkv.shape[1]//3; J=D//256; H=D//HEAD_DIM
    return pl.pallas_call(attend_kernel,grid=(slots,J),
        in_specs=[SCALARS,HELD],
        out_specs=[pl.BlockSpec((4,SLOT,SLOT),lambda s,j:(s*J+j,0,0)),pl.BlockSpec((256,SLOT),lambda s,j:(s*J+j,0)),HELD,pl.BlockSpec((1,8,SLOT),lambda s,j:(s*J+j,0,0))],
        out_shape=[pltpu.HBM((slots*H,SLOT,SLOT),BF),pltpu.HBM((slots*D,SLOT),BF),pltpu.VMEM((rows,D),BF),pltpu.HBM((slots*J,8,SLOT),F32)],
        compiler_params=params(LIM["attend"]),cost_estimate=takes(16),name="attend")(scalars,qkv)


def norm_stats(value):
    mean=jnp.mean(value,axis=-1,keepdims=True)
    c=value-mean
    r=lax.rsqrt(jnp.mean(c*c,axis=-1,keepdims=True)+1e-5)
    return c*r,r

def norm_back(g,n,r):
    return r*(g-jnp.mean(g,axis=-1,keepdims=True)-n*jnp.mean(g*n,axis=-1,keepdims=True))

def gelu_pair(v):
    cdf=0.5+0.5*lax.erf(v*0.7071067811865476)
    return v*cdf, cdf+(0.3989422804014327*v)*jnp.exp(-0.5*v*v)

CH=512
TILE=256
LIM={"project":8,"attend":10,"feed_in":6,"feed_out":14,"attend_back":10,"inputs_grad":6}

def feed_in_kernel(layout,sc_ref,x_ref,o_ref,nm_ref,*rest):
    *blocks,n1_ref,r1_ref,act_ref,gp_ref,wo,wi,sems=rest
    i=pl.program_id(0)
    @pl.when(i==0)
    def _():
        lists=block_copies(layout,sc_ref[0],blocks,(wo,wi),sems)
        for l in lists: start_all(l)
        for l in lists: wait_all(l)
    T=x_ref.shape[0]
    rows=pl.ds(pl.multiple_of(i*T,T),T)
    first=x_ref[...].astype(F32)+dg(o_ref[rows,:],wo[...],1,0)
    n1,r1=norm_stats(first)
    n1_ref[rows,:]=n1; r1_ref[rows,:]=jnp.broadcast_to(r1,(T,128))
    hb=(n1*nm_ref[0:1,:]+nm_ref[1:2,:]).astype(BF)
    for c in range(wi.shape[1]//CH):
        z=dg(hb,wi[:,c*CH:(c+1)*CH],1,0)
        act,gp=gelu_pair(z)
        act_ref[rows,c*CH:(c+1)*CH]=act.astype(BF)
        gp_ref[rows,c*CH:(c+1)*CH]=gp.astype(BF)

def feed_in(scalars,x,o,nm,blocks,layout,FF):
    rows,D=x.shape
    return pl.pallas_call(functools.partial(feed_in_kernel,layout),grid=(rows//TILE,),
        in_specs=[SCALARS,pl.BlockSpec((TILE,D),lambda i:(i,0)),HELD,HELD]+[ANY]*len(blocks),
        out_specs=[HELD]*6,
        out_shape=[pltpu.VMEM((rows,D),F32),pltpu.VMEM((rows,128),F32),pltpu.VMEM((rows,FF),BF),pltpu.VMEM((rows,FF),BF),pltpu.VMEM((D,D),BF),pltpu.VMEM((D,FF),BF)],
        scratch_shapes=[pltpu.SemaphoreType.DMA((copy_count(layout),))],
        compiler_params=params(LIM["feed_in"]),cost_estimate=takes(17),name="feed_in")(scalars,x,o,nm,*blocks)

def feed_out_kernel(layout,sc_ref,n1_ref,r1_ref,act_ref,gp_ref,go_ref,nm_ref,wo,wi,*rest):
    *blocks,out_ref,gfs_ref,gmt_ref,wt,gi_ref,sems=rest
    i=pl.program_id(0)
    @pl.when(i==0)
    def _():
        copies,=block_copies(layout,sc_ref[0],blocks,(wt,),sems,True)
        start_all(copies); wait_all(copies)
    T=go_ref.shape[0]
    rows=pl.ds(pl.multiple_of(i*T,T),T)
    ag,ash,fg,fsh=(nm_ref[i:i+1,:] for i in range(4))
    n1=n1_ref[rows,:]; r1=r1_ref[rows,0:1]
    acc=n1*ag+ash+dg(act_ref[rows,:],wt[...],1,0)
    n2,r2=norm_stats(acc)
    out_ref[...]=(n2*fg+fsh).astype(BF)
    g2=norm_back(go_ref[...].astype(F32)*fg,n2,r2)
    g2b=g2.astype(BF)
    for c in range(wi.shape[1]//CH):
        ga=dg(g2b,wt[c*CH:(c+1)*CH,:],1,1)
        gi_ref[:,c*CH:(c+1)*CH]=(ga*gp_ref[rows,c*CH:(c+1)*CH].astype(F32)).astype(BF)
    g1=norm_back((g2+dg(gi_ref[...],wi[...],1,1))*ag,n1,r1)
    gfs_ref[...]=g1
    gmt_ref[:,rows]=dg(wo[...],g1.astype(BF),1,1).astype(BF)

def feed_out(scalars,n1,r1,act,gp,go,wo,wi,nm,blocks,layout):
    rows,D=n1.shape; FF=wi.shape[1]
    row=pl.BlockSpec((TILE,D),lambda i:(i,0))
    return pl.pallas_call(functools.partial(feed_out_kernel,layout),grid=(rows//TILE,),
        in_specs=[SCALARS,HELD,HELD,HELD,HELD,row,HELD,HELD,HELD]+[ANY]*len(blocks),
        out_specs=[row,row,HELD],
        out_shape=[sd((rows,D),BF),pltpu.HBM((rows,D),F32),pltpu.VMEM((D,rows),BF)],
        scratch_shapes=[pltpu.VMEM((FF,D),BF),pltpu.VMEM((TILE,FF),BF),pltpu.SemaphoreType.DMA((copy_count(layout),))],
        compiler_params=params(LIM["feed_out"]),cost_estimate=takes(28),name="feed_out")(scalars,n1,r1,act,gp,go,nm,wo,wi,*blocks)


def attend_back_kernel(sc_ref,q_ref,k_ref,v_ref,e_ref,ot_ref,rt_ref,gmt_ref,x_ref,low_ref,upq_ref,upv_ref,
                       d_ref,gl_ref,mine_ref,other_ref,glacc,ad_ref):
    s=pl.program_id(0); j=pl.program_id(1); J=pl.num_programs(1)
    lane=lax.broadcasted_iota(jnp.int32,(SLOT,128),1)
    rowi=lax.broadcasted_iota(jnp.int32,(128,SLOT),0)
    D=256*J
    rows=pl.ds(pl.multiple_of(s*SLOT,SLOT),SLOT)
    def place_of(which,p):
        return rows,pl.ds(pl.multiple_of(which*D+256*j+128*p,128),128)
    gmq=gmt_ref[pl.ds(pl.multiple_of(256*j,256),256),rows]
    otq=ot_ref[...]
    dqts=[]; dvs=[]
    for p in range(2):
        cols=slice(128*p,128*p+128)
        qp,kp,vp=(w[:,cols].astype(F32) for w in (q_ref,k_ref,v_ref))
        qp=qp*0.125; kp=kp*0.125
        gm=gmq[cols,:].astype(F32); om=otq[cols,:].astype(F32)
        pr=gm*om
        dkp=None; dvp=None; dqt=None
        for h in range(2):
            own=(lane<64) if h==0 else (lane>=64)
            ownr=(rowi<64) if h==0 else (rowi>=64)
            aux=64 if h==0 else 0
            r=rt_ref[0,2*p+h:2*p+h+1,:]
            d=-jnp.sum(pr[64*h:64*h+64],axis=0,keepdims=True)*r
            dhi=d.astype(BF).astype(F32)
            dlo=d-dhi
            gs=gm*r
            gaug=jnp.where(ownr,gs,jnp.where(rowi==aux,dhi,jnp.where(rowi==aux+1,dlo,0.0))).astype(BF)
            gown=jnp.where(ownr,gs,0.0).astype(BF)
            vm=jnp.where(own,vp,jnp.where((lane==aux)|(lane==aux+1),1.0,0.0)).astype(BF)
            e=e_ref[2*p+h]
            ds=(dg(vm,gaug,1,0)*e.astype(F32)).astype(BF)
            qm=jnp.where(own,qp,0.0).astype(BF)
            km=jnp.where(own,kp,0.0).astype(BF)
            dv=dg(e,gown,1,1)
            dk=dg(ds,qm,1,0)
            dq=dg(km,ds,0,0)
            dvp=dv if dvp is None else dvp+dv
            dkp=dk if dkp is None else dkp+dk
            dqt=dq if dqt is None else dqt+dq
        d_ref[place_of(1,p)]=dkp.astype(BF)
        dvs.append(dvp.astype(BF))
        d_ref[place_of(2,p)]=dvs[p]
        dqts.append(dqt.astype(BF))
    dqt=jnp.concatenate(dqts,axis=0)
    dqb=dqt.T
    d_ref[rows,pl.ds(pl.multiple_of(256*j,256),256)]=dqb
    dvb=jnp.concatenate(dvs,axis=1)
    glq=dg(upq_ref[...],dqt,1,0)
    glv=dg(upv_ref[...],dvb,1,1)
    part=2.0*(glq+glv)
    @pl.when(j==0)
    def _(): glacc[...]=part
    @pl.when(j>0)
    def _(): glacc[...]+=part
    low=low_ref[...]
    c0=pl.multiple_of(j*256,256)
    upq=2.0*dg(low[:16],dqb,1,0)
    upv=2.0*dg(low[:16],dvb,1,0)
    upg=jnp.concatenate([upq[0:8],upv[8:16]],axis=0)
    def add(rows,cols,v):
        @pl.when(s==0)
        def _(): ad_ref[rows,cols]=v
        @pl.when(s>0)
        def _(): ad_ref[rows,cols]+=v
    add(slice(16,32),pl.ds(c0,256),upg)
    @pl.when(j==J-1)
    def _():
        gl=glacc[...].astype(BF)
        gl_ref[...]=gl
        add(slice(0,16),slice(None),dg(gl,x_ref[...],1,0))
        core=lax.rem(sc_ref[0],2)
        for c,(a,b) in enumerate(((mine_ref,other_ref),(other_ref,mine_ref))):
            @pl.when((s==pl.num_programs(0)-1)&(core==c))
            def _():
                a[...]=ad_ref[0:16,:]
                b[...]=ad_ref[16:32,:]

def attend_back(scalars,qkv,e,ot,rt,gmt,x,low,upq,upv):
    rows,D=x.shape; J=D//256; S=rows//SLOT
    up=pl.BlockSpec((16,256),lambda s,j:(0,j))
    return pl.pallas_call(attend_back_kernel,grid=(S,J),
        in_specs=[SCALARS,*[pl.BlockSpec((SLOT,256),lambda s,j,w=w:(s,w*J+j)) for w in range(3)],
                  pl.BlockSpec((4,SLOT,SLOT),lambda s,j:(s*J+j,0,0)),pl.BlockSpec((256,SLOT),lambda s,j:(s*J+j,0)),
                  pl.BlockSpec((1,8,SLOT),lambda s,j:(s*J+j,0,0)),HELD,
                  pl.BlockSpec((SLOT,D),lambda s,j:(s,0)),pl.BlockSpec((32,SLOT),lambda s,j:(0,s)),up,up],
        out_specs=[HELD,pl.BlockSpec((16,SLOT),lambda s,j:(0,s)),HELD,HELD],
        out_shape=[pltpu.VMEM((rows,3*D),BF),sd((16,rows),BF),pltpu.VMEM((16,D),F32),pltpu.VMEM((16,D),F32)],
        scratch_shapes=[pltpu.VMEM((16,SLOT),F32),pltpu.VMEM((32,D),F32)],
        compiler_params=params(LIM["attend_back"]),cost_estimate=takes(18),name="attend_back")(scalars,far(qkv),far(qkv),far(qkv),far(e),far(ot),rt,gmt,x,low,upq,upv)

def inputs_kernel(gfs_ref,d_ref,gl,w_ref,dnt_ref,out_ref):
    T=gfs_ref.shape[0]
    rows=pl.ds(pl.multiple_of(pl.program_id(0)*T,T),T)
    out_ref[...]=gfs_ref[...]+dg(d_ref[rows,:],w_ref[...],1,1)+dg(gl[...],dnt_ref[...],0,0)

def inputs_grad(gfs,d,gl,w,dnt):
    rows,D=gfs.shape
    row=pl.BlockSpec((SLOT,D),lambda i:(i,0))
    return pl.pallas_call(inputs_kernel,grid=(rows//SLOT,),
        in_specs=[row,HELD,pl.BlockSpec((16,SLOT),lambda i:(0,i)),HELD,HELD],
        out_specs=row,out_shape=sd((rows,D),F32),
        compiler_params=params(LIM["inputs_grad"]),cost_estimate=takes(7),name="inputs_grad")(gfs,d,gl,w,dnt)


def device_count():
    return lax.axis_size("dp")*lax.axis_size("fsdp")

def permute(v,target):
    return lax.ppermute(v,AXES,[(i,target(i)) for i in range(device_count())])

def exchange(v,mask):
    return permute(v,lambda i:i^mask)

def along_z(block):
    top=device_count()//4
    return [block]+[exchange(block,top*m) for m in (1,2,3)]

def near_hop(v):
    return permute(v,lambda i:i^(4 if i%2 else 2))

def far_hop(v):
    return permute(v,lambda i:i^(2 if i%2 else 4))

def core_pair(v):
    groups=[[2*i,2*i+1] for i in range(lax.axis_size("fsdp")//2)]
    return lax.all_gather(v,"fsdp",axis=0,tiled=False,axis_index_groups=groups)

def column_half(both):
    c=lax.axis_index("fsdp")%2
    half=both.shape[2]//2
    return lax.dynamic_slice_in_dim(both,c*half,half,axis=2).reshape(-1,half)

def total_over_devices(mine,other,meanwhile):
    n=device_count()
    mine=mine+exchange(other,1)
    got=[exchange(mine,m) for m in range(2,n//4,2)]
    for g in got: mine=mine+g
    got=[exchange(mine,m) for m in (n//4,n//2,3*n//4)]
    got,done=tie(got,meanwhile())
    for g in got: mine=mine+g
    return mine,exchange(mine,1),done

def finish_kernel(scale,sc_ref,mine_ref,other_ref,*outs):
    core=lax.rem(sc_ref[0],2)
    for c,halves in enumerate(((mine_ref,other_ref),(other_ref,mine_ref))):
        @pl.when(core==c)
        def _():
            for i,o in enumerate(outs): o[...]=halves[i//2][8*(i%2):8*(i%2)+8,:]*scale

def finish(scalars,mine,other,scale):
    D=mine.shape[1]
    return pl.pallas_call(functools.partial(finish_kernel,scale),in_specs=[SCALARS,HELD,HELD],out_specs=[HELD]*4,
        out_shape=[sd((8,D),F32)]*4,compiler_params=params(8),cost_estimate=takes(1),name="finish")(scalars,mine,other)

def tie(*v):
    return lax.optimization_barrier(v)

def by_hops(scalars,x,wq,wk,wv,wo,wi,wt,ag,ash,fg,fsh,qd,qu,vd,vu,go):
    D=wq.shape[1]; FF=wi.shape[1]; bands=FF//D; r=wq.shape[0]; rt_=wt.shape[0]
    top=device_count()//4
    both=core_pair(jnp.concatenate([wq,wk,wv],0))
    s1=jnp.concatenate([column_half(both[:,r*t:r*t+r]) for t in range(3)],0)
    z1=along_z(s1)
    wo,wi,wt,qd,s1=tie(wo,wi,wt,qd,s1)
    bo,bi,bt=core_pair(wo),core_pair(wi),core_pair(wt)
    s2=jnp.concatenate([column_half(bo)]+[column_half(bi[:,:,D*t:D*t+D]) for t in range(bands)],0)
    s3=column_half(bt)
    dn,upq,upv,dnt,nm=prep(qd,qu,vd,vu,ag,ash,fg,fsh)
    n3=near_hop(s3)
    z1,s2,dn,scalars=tie(z1,s2,dn,scalars)
    a1=jnp.stack(z1,0)
    n1=near_hop(a1)
    z22=exchange(s2,2*top)
    n1,z22,s2,n3=tie(n1,z22,s2,n3)
    f1=jnp.concatenate([a1,n1],0)
    h1=far_hop(f1); of1=exchange(f1,1)
    z23=exchange(s2,3*top); z21=exchange(s2,top)
    h1,of1,z23,z21,n3=tie(h1,of1,z23,z21,n3)
    oh1=exchange(h1,1)
    a2=jnp.stack([s2,z21,z22,z23],0)
    n2=near_hop(a2)
    z3=along_z(jnp.stack([s3,n3],0))
    oh1,=tie(oh1)
    qkv,low,wqkv=project(scalars,x,dn,upq,upv,(f1,h1,of1,oh1),((3,2*r,0,2*r),))
    n2,qkv=tie(n2,qkv)
    f2=jnp.concatenate([a2,n2],0)
    h2=far_hop(f2); of2=exchange(f2,1)
    e,ot,o,rt=attend(scalars,qkv,x.shape[0]//SLOT)
    h2,o,of2,z3=tie(h2,o,of2,z3)
    oh2=exchange(h2,1)
    f3=jnp.concatenate(z3,0)
    h3=far_hop(f3); of3=exchange(f3,1)
    oh2,=tie(oh2)
    nn,r1,act,gp,wo,wi=feed_in(scalars,x,o,nm,(f2,h2,of2,oh2),((1,2*r,0,2*r),(bands,2*r,0,2*r)),FF)
    h3,nn,of3=tie(h3,nn,of3)
    oh3=exchange(h3,1)
    out,gfs,gmt=feed_out(scalars,nn,r1,act,gp,go,wo,wi,nm,(f3,h3,of3,oh3),((1,2*rt_,0,2*rt_),))
    return qkv,low,wqkv,e,ot,rt,out,gfs,gmt,upq,upv,dnt

def by_all_gather(scalars,x,wq,wk,wv,wo,wi,wt,ag,ash,fg,fsh,qd,qu,vd,vu,go):
    wq,wk,wv,wo,wi,wt=(lax.all_gather(w,AXES,axis=0,tiled=True) for w in (wq,wk,wv,wo,wi,wt))
    dn,upq,upv,dnt,nm=prep(qd,qu,vd,vu,ag,ash,fg,fsh)
    qkv,low,wqkv=project(scalars,x,dn,upq,upv,(jnp.concatenate([wq,wk,wv],1),),None)
    e,ot,o,rt=attend(scalars,qkv,x.shape[0]//SLOT)
    nn,r1,act,gp,wo,wi=feed_in(scalars,x,o,nm,(wo,wi),None,wi.shape[1])
    out,gfs,gmt=feed_out(scalars,nn,r1,act,gp,go,wo,wi,nm,(wt,),None)
    return qkv,low,wqkv,e,ot,rt,out,gfs,gmt,upq,upv,dnt

def shards(x,lengths,wq,wk,wv,wo,wi,wt,ag,ash,fg,fsh,qd,qu,vd,vu,go):
    n=device_count()
    valid=lengths[:,0]+lengths[:,1]+4
    me=(lax.axis_index("dp")*lax.axis_size("fsdp")+lax.axis_index("fsdp")).reshape(1)
    scalars=jnp.concatenate([me,valid]).astype(jnp.int32)
    forward=by_hops if n==32 and wq.shape[0]%8==0 else by_all_gather
    qkv,low,wqkv,e,ot,rt,out,gfs,gmt,upq,upv,dnt=forward(scalars,x,wq,wk,wv,wo,wi,wt,ag,ash,fg,fsh,qd,qu,vd,vu,go)
    d,gl,mine,other=attend_back(scalars,qkv,e,ot,rt,gmt,x,low,upq,upv)
    mine,other,gx=total_over_devices(mine,other,lambda: inputs_grad(gfs,d,gl,wqkv,dnt))
    qd,vd,qu,vu=finish(scalars,mine,other,1.0/(lengths.shape[0]*n))
    return out,gx,qd.T,qu,vd.T,vu

def solution(mesh):
    sp=P(AXES,None)
    return jax.shard_map(shards,mesh=mesh,in_specs=(sp,)*8+(P(),)*8+(sp,),
        out_specs=(sp,sp,P(),P(),P(),P()),check_vma=False)
```

```python
import functools
import jax
import jax.numpy as jnp
from jax import lax
from jax.experimental import pallas as pl
from jax.experimental.pallas import tpu as pltpu
from jax.sharding import PartitionSpec as P

HEAD_DIM=64; SLOT=512
F32=jnp.float32; BF=jnp.bfloat16
MIB=1024*1024
AXES=("dp","fsdp")
sd=jax.ShapeDtypeStruct
ANY=pl.BlockSpec(memory_space=pl.ANY)
HELD=pl.BlockSpec(memory_space=pltpu.VMEM)
SCALARS=pl.BlockSpec(memory_space=pltpu.SMEM)


def params(mib=56):
    return pltpu.CompilerParams(vmem_limit_bytes=mib*MIB)

def takes(us):
    return pl.CostEstimate(flops=int(us*1.1e9),bytes_accessed=0,transcendentals=0)


def dg(a,b,ca,cb):
    return lax.dot_general(a,b,(((ca,),(cb,)),((),())),preferred_element_type=F32)

def far(v):
    return pltpu.with_memory_space_constraint(v,pltpu.HBM)


def block_copies(me,bufs,to,sems):
    if len(bufs)==1:
        return [pltpu.make_async_copy(bufs[0],to,sems.at[0])]
    chip=lax.div(me,2); core=lax.rem(me,2)
    copies=[]
    for which,buf in enumerate(bufs):
        origin=core if which<2 else 1-core
        _,_,rows,half=buf.shape
        for i in range(8):
            dst=lax.bitwise_xor(chip,(which%2)*(2-origin)+(i//4)*(1+origin)+4*(i%4))
            at=to.at[:,pl.ds(pl.multiple_of(dst*rows,16),rows),pl.ds(pl.multiple_of(origin*half,128),half)]
            copies.append(pltpu.make_async_copy(buf.at[i],at,sems.at[len(copies)]))
    return copies

def start_all(copies):
    for c in copies: c.start()

def wait_all(copies):
    for c in copies: c.wait()

BLOCK_COPIES=32

def prep_kernel(qdt_ref,vdt_ref,qu_ref,vu_ref,ag_ref,ash_ref,fg_ref,fsh_ref,dn_ref,upq_ref,upv_ref,dnt_ref,nm_ref):
    D=qu_ref.shape[1]
    both=jnp.concatenate([qdt_ref[...],vdt_ref[...]],axis=0)
    dnt_ref[...]=both.astype(BF)
    dn_ref[...]=jnp.concatenate([both,jnp.zeros((112,D),F32)],axis=0).T.astype(BF)
    z8=jnp.zeros((8,D),F32); z=jnp.zeros((112,D),F32)
    upq_ref[...]=jnp.concatenate([qu_ref[...],z8,z],axis=0).astype(BF)
    upv_ref[...]=jnp.concatenate([z8,vu_ref[...],z],axis=0).astype(BF)
    for i,r in enumerate((ag_ref,ash_ref,fg_ref,fsh_ref)):
        nm_ref[i:i+1,:]=r[...].astype(F32)
    nm_ref[4:8,:]=jnp.zeros((4,D),F32)

def prep(qd,qu,vd,vu,ag,ash,fg,fsh):
    D=qu.shape[1]
    return pl.pallas_call(prep_kernel,out_shape=[sd((D,128),BF),sd((128,D),BF),sd((128,D),BF),sd((16,D),BF),sd((8,D),F32)],
        compiler_params=params(8),cost_estimate=takes(1),name="prep")(qd.T,vd.T,qu,vu,*(v.reshape(1,D) for v in (ag,ash,fg,fsh)))


def project_kernel(sc_ref,x_ref,dn_ref,upq_ref,upv_ref,*rest):
    *blocks,qkv_ref,low_ref,wo,w,sems,osem=rest
    rows,D=x_ref.shape
    copies=block_copies(sc_ref[0],blocks,w,sems)
    start_all(copies)
    lows=[]
    for s in range(rows//SLOT):
        low=dg(x_ref[s*SLOT:(s+1)*SLOT,:],dn_ref[...],1,0).astype(BF)
        low_ref[:,s*SLOT:(s+1)*SLOT]=low.T[:32]
        lows.append(low)
    wait_all(copies)
    whole=[pltpu.make_async_copy(w,wo,osem.at[0])]
    start_all(whole)
    for t,up in enumerate((upq_ref,None,upv_ref)):
        for s in range(rows//SLOT):
            r=slice(s*SLOT,(s+1)*SLOT)
            v=dg(x_ref[r,:],w[t],1,0)
            if up is not None: v=v+2.0*dg(lows[s],up[...],1,0)
            qkv_ref[r,t*D:(t+1)*D]=v.astype(BF)
    wait_all(whole)

def project(scalars,x,dn,upq,upv,blocks):
    rows,D=x.shape
    return pl.pallas_call(project_kernel,
        in_specs=[SCALARS,HELD,HELD,HELD,HELD]+[ANY]*len(blocks),
        out_specs=[HELD,HELD,ANY],
        out_shape=[pltpu.VMEM((rows,3*D),BF),sd((32,rows),BF),pltpu.HBM((3,D,D),BF)],
        scratch_shapes=[pltpu.VMEM((3,D,D),BF),pltpu.SemaphoreType.DMA((BLOCK_COPIES,)),pltpu.SemaphoreType.DMA((1,))],
        compiler_params=params(LIM["project"]),cost_estimate=takes(8),name="project")(scalars,x,dn,upq,upv,*blocks)

def attend_kernel(sc_ref,qkv_ref,e_ref,ot_ref,o_ref,rt_ref):
    s=pl.program_id(0); j=pl.program_id(1); J=pl.num_programs(1); D=256*J
    lane=lax.broadcasted_iota(jnp.int32,(SLOT,128),1)
    row=lax.broadcasted_iota(jnp.int32,(SLOT,128),0)
    bias=jnp.where(row<sc_ref[1+s],0.0,-1e30).astype(F32)
    rows=pl.ds(pl.multiple_of(s*SLOT,SLOT),SLOT)
    def part(which,p):
        return qkv_ref[rows,pl.ds(pl.multiple_of(which*D+256*j+128*p,128),128)].astype(F32)
    heads=[]
    for p in range(2):
        qp,kp,vp=part(0,p)*0.125,part(1,p),part(2,p)
        for h in range(2):
            own=(lane<64) if h==0 else (lane>=64)
            aux=64 if h==0 else 0
            one=jnp.where(lane==aux,1.0,0.0)
            heads.append((64*h,aux,jnp.where(own,qp,one).astype(BF),
                          jnp.where(own,kp,jnp.where(lane==aux,bias,0.0)).astype(BF),jnp.where(own,vp,one).astype(BF)))
    totals=[]; os=[]
    def weights(n,st):
        e_ref[n]=jnp.exp(st-jnp.max(st,axis=0,keepdims=True)).astype(BF)
    def mix(n):
        lo,aux,_,_,vm=heads[n]
        ot=dg(vm,e_ref[n],0,0)
        r=1.0/ot[aux:aux+1]
        totals.append(r)
        os.append((ot[lo:lo+64]*r).astype(BF))
    before=None
    for n in range(4):
        st=dg(heads[n][3],heads[n][2],1,1)
        if before is not None:
            weights(n-1,before)
            if n>1: mix(n-2)
        before=st
    weights(3,before)
    mix(2); mix(3)
    ot=jnp.concatenate(os,axis=0)
    ot_ref[...]=ot
    o_ref[rows,pl.ds(pl.multiple_of(256*j,256),256)]=ot.T
    rt_ref[0]=jnp.concatenate(totals+totals,axis=0)

def attend(scalars,qkv,slots):
    rows=qkv.shape[0]; D=qkv.shape[1]//3; J=D//256; H=D//HEAD_DIM
    return pl.pallas_call(attend_kernel,grid=(slots,J),
        in_specs=[SCALARS,HELD],
        out_specs=[pl.BlockSpec((4,SLOT,SLOT),lambda s,j:(s*J+j,0,0)),pl.BlockSpec((256,SLOT),lambda s,j:(s*J+j,0)),HELD,pl.BlockSpec((1,8,SLOT),lambda s,j:(s*J+j,0,0))],
        out_shape=[pltpu.HBM((slots*H,SLOT,SLOT),BF),pltpu.HBM((slots*D,SLOT),BF),pltpu.VMEM((rows,D),BF),pltpu.HBM((slots*J,8,SLOT),F32)],
        compiler_params=params(LIM["attend"]),cost_estimate=takes(16),name="attend")(scalars,qkv)


def norm_stats(value):
    mean=jnp.mean(value,axis=-1,keepdims=True)
    c=value-mean
    r=lax.rsqrt(jnp.mean(c*c,axis=-1,keepdims=True)+1e-5)
    return c*r,r

def norm_back(g,n,r):
    return r*(g-jnp.mean(g,axis=-1,keepdims=True)-n*jnp.mean(g*n,axis=-1,keepdims=True))

def gelu_pair(v):
    cdf=0.5+0.5*lax.erf(v*0.7071067811865476)
    return v*cdf, cdf+(0.3989422804014327*v)*jnp.exp(-0.5*v*v)

CH=256
LIM={"project":10,"attend":12,"feed_in":8,"feed_out":20,"attend_back":12,"inputs_grad":10}

def feed_in_kernel(sc_ref,x_ref,o_ref,nm_ref,*rest):
    *blocks,n1_ref,r1_ref,act_ref,gp_ref,w,sems=rest
    D=x_ref.shape[1]
    copies=block_copies(sc_ref[0],blocks,w,sems)
    start_all(copies); wait_all(copies)
    parts=[]
    for s in range(x_ref.shape[0]//SLOT):
        rows=slice(s*SLOT,(s+1)*SLOT)
        first=x_ref[rows,:].astype(F32)+dg(o_ref[rows,:],w[0],1,0)
        n1,r1=norm_stats(first)
        n1_ref[rows,:]=n1; r1_ref[rows,:]=jnp.broadcast_to(r1,(SLOT,128))
        parts.append((rows,(n1*nm_ref[0:1,:]+nm_ref[1:2,:]).astype(BF)))
    for c in range(0,act_ref.shape[1],CH):
        for rows,hb in parts:
            act,gp=gelu_pair(dg(hb,w[1+c//D,:,c%D:c%D+CH],1,0))
            act_ref[rows,c:c+CH]=act.astype(BF)
            gp_ref[rows,c:c+CH]=gp.astype(BF)

def feed_in(scalars,x,o,nm,blocks,FF):
    rows,D=x.shape
    return pl.pallas_call(feed_in_kernel,
        in_specs=[SCALARS,HELD,HELD,HELD]+[ANY]*len(blocks),
        out_specs=[HELD]*5,
        out_shape=[pltpu.VMEM((rows,D),F32),pltpu.VMEM((rows,128),F32),pltpu.VMEM((rows,FF),BF),pltpu.VMEM((rows,FF),BF),pltpu.VMEM((1+FF//D,D,D),BF)],
        scratch_shapes=[pltpu.SemaphoreType.DMA((BLOCK_COPIES,))],
        compiler_params=params(LIM["feed_in"]),cost_estimate=takes(14),name="feed_in")(scalars,x,o,nm,*blocks)

def feed_out_kernel(sc_ref,n1_ref,r1_ref,act_ref,gp_ref,go_ref,nm_ref,w,*rest):
    *blocks,out_ref,gfs_ref,gmt_ref,wt,gi_ref,sems=rest
    i=pl.program_id(0)
    @pl.when(i==0)
    def _():
        copies=block_copies(sc_ref[0],blocks,wt,sems)
        start_all(copies); wait_all(copies)
    T,D=go_ref.shape
    rows=pl.ds(pl.multiple_of(i*T,T),T)
    ag,ash,fg,fsh=(nm_ref[i:i+1,:] for i in range(4))
    n1=n1_ref[rows,:]; r1=r1_ref[rows,0:1]
    acc=n1*ag+ash+dg(act_ref[rows,:],wt[0],1,0)
    n2,r2=norm_stats(acc)
    out_ref[...]=(n2*fg+fsh).astype(BF)
    g2=norm_back(go_ref[...].astype(F32)*fg,n2,r2)
    g2b=g2.astype(BF)
    for c in range(0,gi_ref.shape[1],CH):
        ga=dg(g2b,wt[0,c:c+CH,:],1,1)
        gi_ref[:,c:c+CH]=(ga*gp_ref[rows,c:c+CH].astype(F32)).astype(BF)
    acc=g2
    for b in range(gi_ref.shape[1]//D):
        acc=acc+dg(gi_ref[:,b*D:(b+1)*D],w[1+b],1,1)
    g1=norm_back(acc*ag,n1,r1)
    gfs_ref[...]=g1
    gmt_ref[:,rows]=dg(w[0],g1.astype(BF),1,1).astype(BF)

def feed_out(scalars,n1,r1,act,gp,go,w,nm,blocks):
    rows,D=n1.shape; FF=act.shape[1]
    row=pl.BlockSpec((SLOT,D),lambda i:(i,0))
    return pl.pallas_call(feed_out_kernel,grid=(rows//SLOT,),
        in_specs=[SCALARS,HELD,HELD,HELD,HELD,row,HELD,HELD]+[ANY]*len(blocks),
        out_specs=[row,row,HELD],
        out_shape=[sd((rows,D),BF),pltpu.HBM((rows,D),F32),pltpu.VMEM((D,rows),BF)],
        scratch_shapes=[pltpu.VMEM((1,FF,D),BF),pltpu.VMEM((SLOT,FF),BF),pltpu.SemaphoreType.DMA((BLOCK_COPIES,))],
        compiler_params=params(LIM["feed_out"]),cost_estimate=takes(24),name="feed_out")(scalars,n1,r1,act,gp,go,nm,w,*blocks)


def attend_back_kernel(sc_ref,q_ref,k_ref,v_ref,e_ref,ot_ref,rt_ref,gmt_ref,x_ref,low_ref,upq_ref,upv_ref,
                       d_ref,gl_ref,mine_ref,other_ref,glacc,ad_ref):
    s=pl.program_id(0); j=pl.program_id(1); J=pl.num_programs(1)
    lane=lax.broadcasted_iota(jnp.int32,(SLOT,128),1)
    rowi=lax.broadcasted_iota(jnp.int32,(128,SLOT),0)
    D=256*J
    rows=pl.ds(pl.multiple_of(s*SLOT,SLOT),SLOT)
    def place_of(which,p):
        return rows,pl.ds(pl.multiple_of(which*D+256*j+128*p,128),128)
    gmq=gmt_ref[pl.ds(pl.multiple_of(256*j,256),256),rows]
    otq=ot_ref[...]
    dqts=[]; dvs=[]
    for p in range(2):
        cols=slice(128*p,128*p+128)
        qp,kp,vp=(w[:,cols].astype(F32) for w in (q_ref,k_ref,v_ref))
        qp=qp*0.125; kp=kp*0.125
        gm=gmq[cols,:].astype(F32); om=otq[cols,:].astype(F32)
        pr=gm*om
        dkp=None; dvp=None; dqt=None
        for h in range(2):
            own=(lane<64) if h==0 else (lane>=64)
            ownr=(rowi<64) if h==0 else (rowi>=64)
            aux=64 if h==0 else 0
            r=rt_ref[0,2*p+h:2*p+h+1,:]
            d=-jnp.sum(pr[64*h:64*h+64],axis=0,keepdims=True)*r
            dhi=d.astype(BF).astype(F32)
            dlo=d-dhi
            gs=gm*r
            gaug=jnp.where(ownr,gs,jnp.where(rowi==aux,dhi,jnp.where(rowi==aux+1,dlo,0.0))).astype(BF)
            gown=jnp.where(ownr,gs,0.0).astype(BF)
            vm=jnp.where(own,vp,jnp.where((lane==aux)|(lane==aux+1),1.0,0.0)).astype(BF)
            e=e_ref[2*p+h]
            ds=(dg(vm,gaug,1,0)*e.astype(F32)).astype(BF)
            qm=jnp.where(own,qp,0.0).astype(BF)
            km=jnp.where(own,kp,0.0).astype(BF)
            dv=dg(e,gown,1,1)
            dk=dg(ds,qm,1,0)
            dq=dg(km,ds,0,0)
            dvp=dv if dvp is None else dvp+dv
            dkp=dk if dkp is None else dkp+dk
            dqt=dq if dqt is None else dqt+dq
        d_ref[place_of(1,p)]=dkp.astype(BF)
        dvs.append(dvp.astype(BF))
        d_ref[place_of(2,p)]=dvs[p]
        dqts.append(dqt.astype(BF))
    dqt=jnp.concatenate(dqts,axis=0)
    dqb=dqt.T
    d_ref[rows,pl.ds(pl.multiple_of(256*j,256),256)]=dqb
    dvb=jnp.concatenate(dvs,axis=1)
    glq=dg(upq_ref[...],dqt,1,0)
    glv=dg(upv_ref[...],dvb,1,1)
    part=2.0*(glq+glv)
    @pl.when(j==0)
    def _(): glacc[...]=part
    @pl.when(j>0)
    def _(): glacc[...]+=part
    low=low_ref[...]
    c0=pl.multiple_of(j*256,256)
    upq=2.0*dg(low[:16],dqb,1,0)
    upv=2.0*dg(low[:16],dvb,1,0)
    upg=jnp.concatenate([upq[0:8],upv[8:16]],axis=0)
    def add(rows,cols,v):
        @pl.when(s==0)
        def _(): ad_ref[rows,cols]=v
        @pl.when(s>0)
        def _(): ad_ref[rows,cols]+=v
    add(slice(16,32),pl.ds(c0,256),upg)
    @pl.when(j==J-1)
    def _():
        gl=glacc[...].astype(BF)
        gl_ref[...]=gl
        add(slice(0,16),slice(None),dg(gl,x_ref[...],1,0))
        core=lax.rem(sc_ref[0],2)
        for c,(a,b) in enumerate(((mine_ref,other_ref),(other_ref,mine_ref))):
            @pl.when((s==pl.num_programs(0)-1)&(core==c))
            def _():
                a[...]=ad_ref[0:16,:]
                b[...]=ad_ref[16:32,:]

def attend_back(scalars,qkv,e,ot,rt,gmt,x,low,upq,upv):
    rows,D=x.shape; J=D//256; S=rows//SLOT
    up=pl.BlockSpec((16,256),lambda s,j:(0,j))
    return pl.pallas_call(attend_back_kernel,grid=(S,J),
        in_specs=[SCALARS,*[pl.BlockSpec((SLOT,256),lambda s,j,w=w:(s,w*J+j)) for w in range(3)],
                  pl.BlockSpec((4,SLOT,SLOT),lambda s,j:(s*J+j,0,0)),pl.BlockSpec((256,SLOT),lambda s,j:(s*J+j,0)),
                  pl.BlockSpec((1,8,SLOT),lambda s,j:(s*J+j,0,0)),HELD,
                  pl.BlockSpec((SLOT,D),lambda s,j:(s,0)),pl.BlockSpec((32,SLOT),lambda s,j:(0,s)),up,up],
        out_specs=[HELD,pl.BlockSpec((16,SLOT),lambda s,j:(0,s)),HELD,HELD],
        out_shape=[pltpu.VMEM((rows,3*D),BF),sd((16,rows),BF),pltpu.VMEM((16,D),F32),pltpu.VMEM((16,D),F32)],
        scratch_shapes=[pltpu.VMEM((16,SLOT),F32),pltpu.VMEM((32,D),F32)],
        compiler_params=params(LIM["attend_back"]),cost_estimate=takes(18),name="attend_back")(scalars,far(qkv),far(qkv),far(qkv),far(e),far(ot),rt,gmt,x,low,upq,upv)

def inputs_kernel(gfs_ref,d_ref,gl,w_ref,dnt_ref,out_ref):
    T=gfs_ref.shape[0]
    rows=pl.ds(pl.multiple_of(pl.program_id(0)*T,T),T)
    D=gfs_ref.shape[1]
    v=gfs_ref[...]+dg(gl[...],dnt_ref[...],0,0)
    for t in range(3): v=v+dg(d_ref[rows,t*D:(t+1)*D],w_ref[t],1,1)
    out_ref[...]=v

def inputs_grad(gfs,d,gl,w,dnt):
    rows,D=gfs.shape
    row=pl.BlockSpec((SLOT,D),lambda i:(i,0))
    return pl.pallas_call(inputs_kernel,grid=(rows//SLOT,),
        in_specs=[row,HELD,pl.BlockSpec((16,SLOT),lambda i:(0,i)),HELD,HELD],
        out_specs=row,out_shape=sd((rows,D),F32),
        compiler_params=params(LIM["inputs_grad"]),cost_estimate=takes(7),name="inputs_grad")(gfs,d,gl,w,dnt)


def device_count():
    return lax.axis_size("dp")*lax.axis_size("fsdp")

def permute(v,target):
    return lax.ppermute(v,AXES,[(i,target(i)) for i in range(device_count())])

def exchange(v,mask):
    return permute(v,lambda i:i^mask)

def along_z(block):
    top=device_count()//4
    return [block]+[exchange(block,top*m) for m in (1,2,3)]

def near_hop(v):
    return permute(v,lambda i:i^(4 if i%2 else 2))

def far_hop(v):
    return permute(v,lambda i:i^(2 if i%2 else 4))

def in_bands(bands,*blocks):
    return tuple(b.reshape(8,bands,-1,b.shape[2]) for b in blocks)

def core_pair(v):
    groups=[[2*i,2*i+1] for i in range(lax.axis_size("fsdp")//2)]
    return lax.all_gather(v,"fsdp",axis=0,tiled=False,axis_index_groups=groups)

def column_half(both):
    c=lax.axis_index("fsdp")%2
    half=both.shape[2]//2
    return lax.dynamic_slice_in_dim(both,c*half,half,axis=2).reshape(-1,half)

def total_over_devices(mine,other,meanwhile):
    n=device_count()
    mine=mine+exchange(other,1)
    got=[exchange(mine,m) for m in range(2,n//4,2)]
    for g in got: mine=mine+g
    got=[exchange(mine,m) for m in (n//4,n//2,3*n//4)]
    got,done=tie(got,meanwhile())
    for g in got: mine=mine+g
    return mine,exchange(mine,1),done

def finish_kernel(scale,sc_ref,mine_ref,other_ref,*outs):
    core=lax.rem(sc_ref[0],2)
    for c,halves in enumerate(((mine_ref,other_ref),(other_ref,mine_ref))):
        @pl.when(core==c)
        def _():
            for i,o in enumerate(outs): o[...]=halves[i//2][8*(i%2):8*(i%2)+8,:]*scale

def finish(scalars,mine,other,scale):
    D=mine.shape[1]
    return pl.pallas_call(functools.partial(finish_kernel,scale),in_specs=[SCALARS,HELD,HELD],out_specs=[HELD]*4,
        out_shape=[sd((8,D),F32)]*4,compiler_params=params(8),cost_estimate=takes(1),name="finish")(scalars,mine,other)

def tie(*v):
    return lax.optimization_barrier(v)

def by_hops(scalars,x,wq,wk,wv,wo,wi,wt,ag,ash,fg,fsh,qd,qu,vd,vu,go):
    D=wq.shape[1]; FF=wi.shape[1]; bands=FF//D; r=wq.shape[0]
    top=device_count()//4
    both=core_pair(jnp.concatenate([wq,wk,wv],0))
    s1=jnp.concatenate([column_half(both[:,r*t:r*t+r]) for t in range(3)],0)
    z1=along_z(s1)
    wo,wi,wt,qd,s1=tie(wo,wi,wt,qd,s1)
    bo,bi,bt=core_pair(wo),core_pair(wi),core_pair(wt)
    s2=jnp.concatenate([column_half(bo)]+[column_half(bi[:,:,D*t:D*t+D]) for t in range(bands)],0)
    s3=column_half(bt)
    dn,upq,upv,dnt,nm=prep(qd,qu,vd,vu,ag,ash,fg,fsh)
    n3=near_hop(s3)
    z1,s2,dn,scalars=tie(z1,s2,dn,scalars)
    a1=jnp.stack(z1,0)
    n1=near_hop(a1)
    z22=exchange(s2,2*top)
    n1,z22,s2,n3=tie(n1,z22,s2,n3)
    f1=jnp.concatenate([a1,n1],0)
    h1=far_hop(f1); of1=exchange(f1,1)
    z23=exchange(s2,3*top); z21=exchange(s2,top)
    h1,of1,z23,z21,n3=tie(h1,of1,z23,z21,n3)
    oh1=exchange(h1,1)
    a2=jnp.stack([s2,z21,z22,z23],0)
    n2=near_hop(a2)
    z3=along_z(jnp.stack([s3,n3],0))
    oh1,=tie(oh1)
    qkv,low,wqkv=project(scalars,x,dn,upq,upv,in_bands(3,f1,h1,of1,oh1))
    n2,qkv=tie(n2,qkv)
    f2=jnp.concatenate([a2,n2],0)
    h2=far_hop(f2); of2=exchange(f2,1)
    e,ot,o,rt=attend(scalars,qkv,x.shape[0]//SLOT)
    h2,o,of2,z3=tie(h2,o,of2,z3)
    oh2=exchange(h2,1)
    f3=jnp.stack(z3,1).reshape(8,-1,D//2)
    h3=far_hop(f3); of3=exchange(f3,1)
    oh2,=tie(oh2)
    nn,r1,act,gp,w=feed_in(scalars,x,o,nm,in_bands(1+bands,f2,h2,of2,oh2),FF)
    h3,nn,of3=tie(h3,nn,of3)
    oh3=exchange(h3,1)
    out,gfs,gmt=feed_out(scalars,nn,r1,act,gp,go,w,nm,in_bands(1,f3,h3,of3,oh3))
    return qkv,low,wqkv,e,ot,rt,out,gfs,gmt,upq,upv,dnt

def by_all_gather(scalars,x,wq,wk,wv,wo,wi,wt,ag,ash,fg,fsh,qd,qu,vd,vu,go):
    wq,wk,wv,wo,wi,wt=(lax.all_gather(w,AXES,axis=0,tiled=True) for w in (wq,wk,wv,wo,wi,wt))
    D=wq.shape[1]; FF=wi.shape[1]
    dn,upq,upv,dnt,nm=prep(qd,qu,vd,vu,ag,ash,fg,fsh)
    qkv,low,wqkv=project(scalars,x,dn,upq,upv,(jnp.stack([wq,wk,wv],0),))
    e,ot,o,rt=attend(scalars,qkv,x.shape[0]//SLOT)
    nn,r1,act,gp,w=feed_in(scalars,x,o,nm,(jnp.stack([wo]+[wi[:,c:c+D] for c in range(0,FF,D)],0),),FF)
    out,gfs,gmt=feed_out(scalars,nn,r1,act,gp,go,w,nm,(wt[None],))
    return qkv,low,wqkv,e,ot,rt,out,gfs,gmt,upq,upv,dnt

def shards(x,lengths,wq,wk,wv,wo,wi,wt,ag,ash,fg,fsh,qd,qu,vd,vu,go):
    n=device_count()
    valid=lengths[:,0]+lengths[:,1]+4
    me=(lax.axis_index("dp")*lax.axis_size("fsdp")+lax.axis_index("fsdp")).reshape(1)
    scalars=jnp.concatenate([me,valid]).astype(jnp.int32)
    forward=by_hops if n==32 and wq.shape[0]%8==0 else by_all_gather
    qkv,low,wqkv,e,ot,rt,out,gfs,gmt,upq,upv,dnt=forward(scalars,x,wq,wk,wv,wo,wi,wt,ag,ash,fg,fsh,qd,qu,vd,vu,go)
    d,gl,mine,other=attend_back(scalars,qkv,e,ot,rt,gmt,x,low,upq,upv)
    mine,other,gx=total_over_devices(mine,other,lambda: inputs_grad(gfs,d,gl,wqkv,dnt))
    qd,vd,qu,vu=finish(scalars,mine,other,1.0/(lengths.shape[0]*n))
    return out,gx,qd.T,qu,vd.T,vu

def solution(mesh):
    sp=P(AXES,None)
    return jax.shard_map(shards,mesh=mesh,in_specs=(sp,)*8+(P(),)*8+(sp,),
        out_specs=(sp,sp,P(),P(),P(),P()),check_vma=False)
```

```python
import functools
import jax
import jax.numpy as jnp
from jax import lax
from jax.experimental import pallas as pl
from jax.experimental.pallas import tpu as pltpu
from jax.sharding import PartitionSpec as P

HEAD_DIM=64; SLOT=512
F32=jnp.float32; BF=jnp.bfloat16
MIB=1024*1024
AXES=("dp","fsdp")
sd=jax.ShapeDtypeStruct
ANY=pl.BlockSpec(memory_space=pl.ANY)
HELD=pl.BlockSpec(memory_space=pltpu.VMEM)
SCALARS=pl.BlockSpec(memory_space=pltpu.SMEM)


def params(mib=56):
    return pltpu.CompilerParams(vmem_limit_bytes=mib*MIB)

def takes(us):
    return pl.CostEstimate(flops=int(us*1.1e9),bytes_accessed=0,transcendentals=0)


def dg(a,b,ca,cb):
    return lax.dot_general(a,b,(((ca,),(cb,)),((),())),preferred_element_type=F32)

def far(v):
    return pltpu.with_memory_space_constraint(v,pltpu.HBM)


def block_copies(me,bufs,to,sems):
    if len(bufs)==1:
        return [pltpu.make_async_copy(bufs[0],to,sems.at[0])]
    chip=lax.div(me,2); core=lax.rem(me,2)
    copies=[]
    for which,buf in enumerate(bufs):
        origin=core if which<2 else 1-core
        _,_,rows,half=buf.shape
        for i in range(8):
            dst=lax.bitwise_xor(chip,(which%2)*(2-origin)+(i//4)*(1+origin)+4*(i%4))
            at=to.at[:,pl.ds(pl.multiple_of(dst*rows,16),rows),pl.ds(pl.multiple_of(origin*half,128),half)]
            copies.append(pltpu.make_async_copy(buf.at[i],at,sems.at[len(copies)]))
    return copies

def start_all(copies):
    for c in copies: c.start()

def wait_all(copies):
    for c in copies: c.wait()

BLOCK_COPIES=32

def prep_kernel(qdt_ref,vdt_ref,qu_ref,vu_ref,ag_ref,ash_ref,fg_ref,fsh_ref,dn_ref,upq_ref,upv_ref,dnt_ref,nm_ref):
    D=qu_ref.shape[1]
    both=jnp.concatenate([qdt_ref[...],vdt_ref[...]],axis=0)
    dnt_ref[...]=both.astype(BF)
    dn_ref[...]=jnp.concatenate([both,jnp.zeros((112,D),F32)],axis=0).T.astype(BF)
    z8=jnp.zeros((8,D),F32); z=jnp.zeros((112,D),F32)
    upq_ref[...]=jnp.concatenate([qu_ref[...],z8,z],axis=0).astype(BF)
    upv_ref[...]=jnp.concatenate([z8,vu_ref[...],z],axis=0).astype(BF)
    for i,r in enumerate((ag_ref,ash_ref,fg_ref,fsh_ref)):
        nm_ref[i:i+1,:]=r[...].astype(F32)
    nm_ref[4:8,:]=jnp.zeros((4,D),F32)

def prep(qd,qu,vd,vu,ag,ash,fg,fsh):
    D=qu.shape[1]
    return pl.pallas_call(prep_kernel,out_shape=[sd((D,128),BF),sd((128,D),BF),sd((128,D),BF),sd((16,D),BF),sd((8,D),F32)],
        compiler_params=params(8),cost_estimate=takes(1),name="prep")(qd.T,vd.T,qu,vu,*(v.reshape(1,D) for v in (ag,ash,fg,fsh)))


def project_kernel(sc_ref,x_ref,dn_ref,upq_ref,upv_ref,*rest):
    *blocks,qkv_ref,low_ref,wo,w,sems,osem=rest
    rows,D=x_ref.shape
    copies=block_copies(sc_ref[0],blocks,w,sems)
    start_all(copies)
    lows=[]
    for s in range(rows//SLOT):
        low=dg(x_ref[s*SLOT:(s+1)*SLOT,:],dn_ref[...],1,0).astype(BF)
        low_ref[:,s*SLOT:(s+1)*SLOT]=low.T[:32]
        lows.append(low)
    wait_all(copies)
    whole=[pltpu.make_async_copy(w,wo,osem.at[0])]
    start_all(whole)
    for t,up in enumerate((upq_ref,None,upv_ref)):
        for s in range(rows//SLOT):
            r=slice(s*SLOT,(s+1)*SLOT)
            v=dg(x_ref[r,:],w[t],1,0)
            if up is not None: v=v+2.0*dg(lows[s],up[...],1,0)
            qkv_ref[r,t*D:(t+1)*D]=v.astype(BF)
    wait_all(whole)

def project(scalars,x,dn,upq,upv,blocks):
    rows,D=x.shape
    return pl.pallas_call(project_kernel,
        in_specs=[SCALARS,HELD,HELD,HELD,HELD]+[ANY]*len(blocks),
        out_specs=[HELD,HELD,ANY],
        out_shape=[pltpu.VMEM((rows,3*D),BF),sd((32,rows),BF),pltpu.HBM((3,D,D),BF)],
        scratch_shapes=[pltpu.VMEM((3,D,D),BF),pltpu.SemaphoreType.DMA((BLOCK_COPIES,)),pltpu.SemaphoreType.DMA((1,))],
        compiler_params=params(LIM["project"]),cost_estimate=takes(8),name="project")(scalars,x,dn,upq,upv,*blocks)

def attend_kernel(sc_ref,qkv_ref,e_ref,ot_ref,o_ref,rt_ref):
    s=pl.program_id(0); j=pl.program_id(1); J=pl.num_programs(1); D=256*J
    lane=lax.broadcasted_iota(jnp.int32,(SLOT,128),1)
    row=lax.broadcasted_iota(jnp.int32,(SLOT,128),0)
    bias=jnp.where(row<sc_ref[1+s],0.0,-1e30).astype(F32)
    rows=pl.ds(pl.multiple_of(s*SLOT,SLOT),SLOT)
    def part(which,p):
        return qkv_ref[rows,pl.ds(pl.multiple_of(which*D+256*j+128*p,128),128)].astype(F32)
    heads=[]
    for p in range(2):
        qp,kp,vp=part(0,p)*0.125,part(1,p),part(2,p)
        for h in range(2):
            own=(lane<64) if h==0 else (lane>=64)
            aux=64 if h==0 else 0
            one=jnp.where(lane==aux,1.0,0.0)
            heads.append((64*h,aux,jnp.where(own,qp,one).astype(BF),
                          jnp.where(own,kp,jnp.where(lane==aux,bias,0.0)).astype(BF),jnp.where(own,vp,one).astype(BF)))
    totals=[]; os=[]
    def weights(n,st):
        e_ref[n]=jnp.exp(st-jnp.max(st,axis=0,keepdims=True)).astype(BF)
    def mix(n):
        lo,aux,_,_,vm=heads[n]
        ot=dg(vm,e_ref[n],0,0)
        r=1.0/ot[aux:aux+1]
        totals.append(r)
        os.append((ot[lo:lo+64]*r).astype(BF))
    before=None
    for n in range(4):
        st=dg(heads[n][3],heads[n][2],1,1)
        if before is not None:
            weights(n-1,before)
            if n>1: mix(n-2)
        before=st
    weights(3,before)
    mix(2); mix(3)
    ot=jnp.concatenate(os,axis=0)
    ot_ref[...]=ot
    o_ref[rows,pl.ds(pl.multiple_of(256*j,256),256)]=ot.T
    rt_ref[0]=jnp.concatenate(totals+totals,axis=0)

def attend(scalars,qkv,slots):
    rows=qkv.shape[0]; D=qkv.shape[1]//3; J=D//256; H=D//HEAD_DIM
    return pl.pallas_call(attend_kernel,grid=(slots,J),
        in_specs=[SCALARS,HELD],
        out_specs=[pl.BlockSpec((4,SLOT,SLOT),lambda s,j:(s*J+j,0,0)),pl.BlockSpec((256,SLOT),lambda s,j:(s*J+j,0)),HELD,pl.BlockSpec((1,8,SLOT),lambda s,j:(s*J+j,0,0))],
        out_shape=[pltpu.HBM((slots*H,SLOT,SLOT),BF),pltpu.HBM((slots*D,SLOT),BF),pltpu.VMEM((rows,D),BF),pltpu.HBM((slots*J,8,SLOT),F32)],
        compiler_params=params(LIM["attend"]),cost_estimate=takes(16),name="attend")(scalars,qkv)


def norm_stats(value):
    mean=jnp.mean(value,axis=-1,keepdims=True)
    c=value-mean
    r=lax.rsqrt(jnp.mean(c*c,axis=-1,keepdims=True)+1e-5)
    return c*r,r

def norm_back(g,n,r):
    return r*(g-jnp.mean(g,axis=-1,keepdims=True)-n*jnp.mean(g*n,axis=-1,keepdims=True))

def gelu_pair(v):
    cdf=0.5+0.5*lax.erf(v*0.7071067811865476)
    return v*cdf, cdf+(0.3989422804014327*v)*jnp.exp(-0.5*v*v)

CH=256
LIM={"project":10,"attend":12,"feed_in":8,"feed_out":20,"attend_back":12,"inputs_grad":10}

def feed_in_kernel(sc_ref,x_ref,o_ref,nm_ref,*rest):
    *blocks,n1_ref,r1_ref,act_ref,gp_ref,w,sems=rest
    D=x_ref.shape[1]
    copies=block_copies(sc_ref[0],blocks,w,sems)
    start_all(copies); wait_all(copies)
    parts=[]
    for s in range(x_ref.shape[0]//SLOT):
        rows=slice(s*SLOT,(s+1)*SLOT)
        first=x_ref[rows,:].astype(F32)+dg(o_ref[rows,:],w[0],1,0)
        n1,r1=norm_stats(first)
        n1_ref[rows,:]=n1; r1_ref[rows,:]=jnp.broadcast_to(r1,(SLOT,128))
        parts.append((rows,(n1*nm_ref[0:1,:]+nm_ref[1:2,:]).astype(BF)))
    for c in range(0,act_ref.shape[1],CH):
        for rows,hb in parts:
            act,gp=gelu_pair(dg(hb,w[1+c//D,:,c%D:c%D+CH],1,0))
            act_ref[rows,c:c+CH]=act.astype(BF)
            gp_ref[rows,c:c+CH]=gp.astype(BF)

def feed_in(scalars,x,o,nm,blocks,FF):
    rows,D=x.shape
    return pl.pallas_call(feed_in_kernel,
        in_specs=[SCALARS,HELD,HELD,HELD]+[ANY]*len(blocks),
        out_specs=[HELD]*5,
        out_shape=[pltpu.VMEM((rows,D),F32),pltpu.VMEM((rows,128),F32),pltpu.VMEM((rows,FF),BF),pltpu.VMEM((rows,FF),BF),pltpu.VMEM((1+FF//D,D,D),BF)],
        scratch_shapes=[pltpu.SemaphoreType.DMA((BLOCK_COPIES,))],
        compiler_params=params(LIM["feed_in"]),cost_estimate=takes(14),name="feed_in")(scalars,x,o,nm,*blocks)

def feed_out_kernel(sc_ref,n1_ref,r1_ref,act_ref,gp_ref,go_ref,nm_ref,w,*rest):
    *blocks,out_ref,gfs_ref,gmt_ref,wt,gi_ref,sems=rest
    i=pl.program_id(0)
    @pl.when(i==0)
    def _():
        copies=block_copies(sc_ref[0],blocks,wt,sems)
        start_all(copies); wait_all(copies)
    T,D=go_ref.shape
    rows=pl.ds(pl.multiple_of(i*T,T),T)
    ag,ash,fg,fsh=(nm_ref[i:i+1,:] for i in range(4))
    n1=n1_ref[rows,:]; r1=r1_ref[rows,0:1]
    acc=n1*ag+ash+dg(act_ref[rows,:],wt[0],1,0)
    n2,r2=norm_stats(acc)
    out_ref[...]=(n2*fg+fsh).astype(BF)
    g2=norm_back(go_ref[...].astype(F32)*fg,n2,r2)
    g2b=g2.astype(BF)
    for c in range(0,gi_ref.shape[1],CH):
        ga=dg(g2b,wt[0,c:c+CH,:],1,1)
        gi_ref[:,c:c+CH]=(ga*gp_ref[rows,c:c+CH].astype(F32)).astype(BF)
    acc=g2
    for b in range(gi_ref.shape[1]//D):
        acc=acc+dg(gi_ref[:,b*D:(b+1)*D],w[1+b],1,1)
    g1=norm_back(acc*ag,n1,r1)
    gfs_ref[...]=g1
    gmt_ref[:,rows]=dg(w[0],g1.astype(BF),1,1).astype(BF)

def feed_out(scalars,n1,r1,act,gp,go,w,nm,blocks):
    rows,D=n1.shape; FF=act.shape[1]
    row=pl.BlockSpec((SLOT,D),lambda i:(i,0))
    return pl.pallas_call(feed_out_kernel,grid=(rows//SLOT,),
        in_specs=[SCALARS,HELD,HELD,HELD,HELD,row,HELD,HELD]+[ANY]*len(blocks),
        out_specs=[row,row,HELD],
        out_shape=[sd((rows,D),BF),pltpu.HBM((rows,D),F32),pltpu.VMEM((D,rows),BF)],
        scratch_shapes=[pltpu.VMEM((1,FF,D),BF),pltpu.VMEM((SLOT,FF),BF),pltpu.SemaphoreType.DMA((BLOCK_COPIES,))],
        compiler_params=params(LIM["feed_out"]),cost_estimate=takes(24),name="feed_out")(scalars,n1,r1,act,gp,go,nm,w,*blocks)


def attend_back_kernel(sc_ref,q_ref,k_ref,v_ref,e_ref,ot_ref,rt_ref,gmt_ref,x_ref,low_ref,upq_ref,upv_ref,
                       d_ref,gl_ref,mine_ref,other_ref,glacc,ad_ref):
    s=pl.program_id(0); j=pl.program_id(1); J=pl.num_programs(1)
    lane=lax.broadcasted_iota(jnp.int32,(SLOT,128),1)
    rowi=lax.broadcasted_iota(jnp.int32,(128,SLOT),0)
    D=256*J
    rows=pl.ds(pl.multiple_of(s*SLOT,SLOT),SLOT)
    def place_of(which,p):
        return rows,pl.ds(pl.multiple_of(which*D+256*j+128*p,128),128)
    gmq=gmt_ref[pl.ds(pl.multiple_of(256*j,256),256),rows]
    otq=ot_ref[...]
    dqts=[]; dvs=[]
    for p in range(2):
        cols=slice(128*p,128*p+128)
        qp,kp,vp=(w[:,cols].astype(F32) for w in (q_ref,k_ref,v_ref))
        qp=qp*0.125; kp=kp*0.125
        gm=gmq[cols,:].astype(F32); om=otq[cols,:].astype(F32)
        pr=gm*om
        dkp=None; dvp=None; dqt=None
        for h in range(2):
            own=(lane<64) if h==0 else (lane>=64)
            ownr=(rowi<64) if h==0 else (rowi>=64)
            aux=64 if h==0 else 0
            r=rt_ref[0,2*p+h:2*p+h+1,:]
            d=-jnp.sum(pr[64*h:64*h+64],axis=0,keepdims=True)*r
            dhi=d.astype(BF).astype(F32)
            dlo=d-dhi
            gs=gm*r
            gaug=jnp.where(ownr,gs,jnp.where(rowi==aux,dhi,jnp.where(rowi==aux+1,dlo,0.0))).astype(BF)
            gown=jnp.where(ownr,gs,0.0).astype(BF)
            vm=jnp.where(own,vp,jnp.where((lane==aux)|(lane==aux+1),1.0,0.0)).astype(BF)
            e=e_ref[2*p+h]
            ds=(dg(vm,gaug,1,0)*e.astype(F32)).astype(BF)
            qm=jnp.where(own,qp,0.0).astype(BF)
            km=jnp.where(own,kp,0.0).astype(BF)
            dv=dg(e,gown,1,1)
            dk=dg(ds,qm,1,0)
            dq=dg(km,ds,0,0)
            dvp=dv if dvp is None else dvp+dv
            dkp=dk if dkp is None else dkp+dk
            dqt=dq if dqt is None else dqt+dq
        d_ref[place_of(1,p)]=dkp.astype(BF)
        dvs.append(dvp.astype(BF))
        d_ref[place_of(2,p)]=dvs[p]
        dqts.append(dqt.astype(BF))
    dqt=jnp.concatenate(dqts,axis=0)
    dqb=dqt.T
    d_ref[rows,pl.ds(pl.multiple_of(256*j,256),256)]=dqb
    dvb=jnp.concatenate(dvs,axis=1)
    glq=dg(upq_ref[...],dqt,1,0)
    glv=dg(upv_ref[...],dvb,1,1)
    part=2.0*(glq+glv)
    @pl.when(j==0)
    def _(): glacc[...]=part
    @pl.when(j>0)
    def _(): glacc[...]+=part
    low=low_ref[...]
    c0=pl.multiple_of(j*256,256)
    upq=2.0*dg(low[:16],dqb,1,0)
    upv=2.0*dg(low[:16],dvb,1,0)
    upg=jnp.concatenate([upq[0:8],upv[8:16]],axis=0)
    def add(rows,cols,v):
        @pl.when(s==0)
        def _(): ad_ref[rows,cols]=v
        @pl.when(s>0)
        def _(): ad_ref[rows,cols]+=v
    add(slice(16,32),pl.ds(c0,256),upg)
    @pl.when(j==J-1)
    def _():
        gl=glacc[...].astype(BF)
        gl_ref[...]=gl
        add(slice(0,16),slice(None),dg(gl,x_ref[...],1,0))
        core=lax.rem(sc_ref[0],2)
        for c,(a,b) in enumerate(((mine_ref,other_ref),(other_ref,mine_ref))):
            @pl.when((s==pl.num_programs(0)-1)&(core==c))
            def _():
                a[...]=ad_ref[0:16,:]
                b[...]=ad_ref[16:32,:]

def attend_back(scalars,qkv,e,ot,rt,gmt,x,low,upq,upv):
    rows,D=x.shape; J=D//256; S=rows//SLOT
    up=pl.BlockSpec((16,256),lambda s,j:(0,j))
    return pl.pallas_call(attend_back_kernel,grid=(S,J),
        in_specs=[SCALARS,*[pl.BlockSpec((SLOT,256),lambda s,j,w=w:(s,w*J+j)) for w in range(3)],
                  pl.BlockSpec((4,SLOT,SLOT),lambda s,j:(s*J+j,0,0)),pl.BlockSpec((256,SLOT),lambda s,j:(s*J+j,0)),
                  pl.BlockSpec((1,8,SLOT),lambda s,j:(s*J+j,0,0)),HELD,
                  pl.BlockSpec((SLOT,D),lambda s,j:(s,0)),pl.BlockSpec((32,SLOT),lambda s,j:(0,s)),up,up],
        out_specs=[HELD,pl.BlockSpec((16,SLOT),lambda s,j:(0,s)),HELD,HELD],
        out_shape=[pltpu.VMEM((rows,3*D),BF),sd((16,rows),BF),pltpu.VMEM((16,D),F32),pltpu.VMEM((16,D),F32)],
        scratch_shapes=[pltpu.VMEM((16,SLOT),F32),pltpu.VMEM((32,D),F32)],
        compiler_params=params(LIM["attend_back"]),cost_estimate=takes(18),name="attend_back")(scalars,far(qkv),far(qkv),far(qkv),far(e),far(ot),rt,gmt,x,low,upq,upv)

def inputs_kernel(gfs_ref,d_ref,gl,w_ref,dnt_ref,out_ref):
    T=gfs_ref.shape[0]
    rows=pl.ds(pl.multiple_of(pl.program_id(0)*T,T),T)
    D=gfs_ref.shape[1]
    v=gfs_ref[...]+dg(gl[...],dnt_ref[...],0,0)
    for t in range(3): v=v+dg(d_ref[rows,t*D:(t+1)*D],w_ref[t],1,1)
    out_ref[...]=v

def inputs_grad(gfs,d,gl,w,dnt):
    rows,D=gfs.shape
    row=pl.BlockSpec((SLOT,D),lambda i:(i,0))
    return pl.pallas_call(inputs_kernel,grid=(rows//SLOT,),
        in_specs=[row,HELD,pl.BlockSpec((16,SLOT),lambda i:(0,i)),HELD,HELD],
        out_specs=row,out_shape=sd((rows,D),F32),
        compiler_params=params(LIM["inputs_grad"]),cost_estimate=takes(7),name="inputs_grad")(gfs,d,gl,w,dnt)


def device_count():
    return lax.axis_size("dp")*lax.axis_size("fsdp")

def permute(v,target):
    return lax.ppermute(v,AXES,[(i,target(i)) for i in range(device_count())])

def exchange(v,mask):
    return permute(v,lambda i:i^mask)

def along_z(block):
    top=device_count()//4
    return [block]+[exchange(block,top*m) for m in (1,2,3)]

def near_hop(v):
    return permute(v,lambda i:i^(4 if i%2 else 2))

def far_hop(v):
    return permute(v,lambda i:i^(2 if i%2 else 4))

def in_bands(bands,*blocks):
    return tuple(b.reshape(8,bands,-1,b.shape[2]) for b in blocks)

def core_pair(v):
    groups=[[2*i,2*i+1] for i in range(lax.axis_size("fsdp")//2)]
    return lax.all_gather(v,"fsdp",axis=0,tiled=False,axis_index_groups=groups)

def column_half(both):
    c=lax.axis_index("fsdp")%2
    half=both.shape[2]//2
    return lax.dynamic_slice_in_dim(both,c*half,half,axis=2).reshape(-1,half)

def total_over_devices(mine,other,meanwhile):
    n=device_count()
    mine=mine+exchange(other,1)
    got=[exchange(mine,m) for m in range(2,n//4,2)]
    for g in got: mine=mine+g
    got=[exchange(mine,m) for m in (n//4,n//2,3*n//4)]
    got,done=tie(got,meanwhile())
    for g in got: mine=mine+g
    return mine,exchange(mine,1),done

def finish_kernel(scale,sc_ref,mine_ref,other_ref,*outs):
    core=lax.rem(sc_ref[0],2)
    for c,halves in enumerate(((mine_ref,other_ref),(other_ref,mine_ref))):
        @pl.when(core==c)
        def _():
            for i,o in enumerate(outs): o[...]=halves[i//2][8*(i%2):8*(i%2)+8,:]*scale

def finish(scalars,mine,other,scale):
    D=mine.shape[1]
    return pl.pallas_call(functools.partial(finish_kernel,scale),in_specs=[SCALARS,HELD,HELD],out_specs=[HELD]*4,
        out_shape=[sd((8,D),F32)]*4,compiler_params=params(8),cost_estimate=takes(1),name="finish")(scalars,mine,other)

def tie(*v):
    return lax.optimization_barrier(v)

def by_hops(scalars,x,wq,wk,wv,wo,wi,wt,ag,ash,fg,fsh,qd,qu,vd,vu,go):
    D=wq.shape[1]; FF=wi.shape[1]; bands=FF//D; r=wq.shape[0]
    top=device_count()//4
    both=core_pair(jnp.concatenate([wq,wk,wv],0))
    s1=jnp.concatenate([column_half(both[:,r*t:r*t+r]) for t in range(3)],0)
    z1=along_z(s1)
    wo,wi,wt,qd,s1=tie(wo,wi,wt,qd,s1)
    bo,bi,bt=core_pair(wo),core_pair(wi),core_pair(wt)
    s2=jnp.concatenate([column_half(bo)]+[column_half(bi[:,:,D*t:D*t+D]) for t in range(bands)],0)
    s3=column_half(bt)
    dn,upq,upv,dnt,nm=prep(qd,qu,vd,vu,ag,ash,fg,fsh)
    n3=near_hop(s3)
    z1,s2,dn,scalars=tie(z1,s2,dn,scalars)
    a1=jnp.stack(z1,0)
    n1=near_hop(a1)
    z2=exchange(s2,2*top)
    n1,z2,s2,n3=tie(n1,z2,s2,n3)
    f1=jnp.concatenate([a1,n1],0)
    h1=far_hop(f1); of1=exchange(f1,1)
    y2=exchange(jnp.stack([s2,z2],0),top)
    h1,of1,y2,n3=tie(h1,of1,y2,n3)
    oh1=exchange(h1,1)
    a2=jnp.stack([s2,y2[0],z2,y2[1]],0)
    n2=near_hop(a2)
    b3=jnp.stack([s3,n3],0)
    z3=exchange(b3,2*top)
    oh1,=tie(oh1)
    qkv,low,wqkv=project(scalars,x,dn,upq,upv,in_bands(3,f1,h1,of1,oh1))
    n2,qkv=tie(n2,qkv)
    z3,_=tie(z3,n2)
    f2=jnp.concatenate([a2,n2],0)
    h2=far_hop(f2); of2=exchange(f2,1)
    y3=exchange(jnp.stack([b3,z3],0),top)
    e,ot,o,rt=attend(scalars,qkv,x.shape[0]//SLOT)
    h2,o,of2,y3=tie(h2,o,of2,y3)
    oh2=exchange(h2,1)
    f3=jnp.stack([b3,y3[0],z3,y3[1]],1).reshape(8,-1,D//2)
    h3=far_hop(f3); of3=exchange(f3,1)
    oh2,=tie(oh2)
    nn,r1,act,gp,w=feed_in(scalars,x,o,nm,in_bands(1+bands,f2,h2,of2,oh2),FF)
    h3,nn,of3=tie(h3,nn,of3)
    oh3=exchange(h3,1)
    out,gfs,gmt=feed_out(scalars,nn,r1,act,gp,go,w,nm,in_bands(1,f3,h3,of3,oh3))
    return qkv,low,wqkv,e,ot,rt,out,gfs,gmt,upq,upv,dnt

def by_all_gather(scalars,x,wq,wk,wv,wo,wi,wt,ag,ash,fg,fsh,qd,qu,vd,vu,go):
    wq,wk,wv,wo,wi,wt=(lax.all_gather(w,AXES,axis=0,tiled=True) for w in (wq,wk,wv,wo,wi,wt))
    D=wq.shape[1]; FF=wi.shape[1]
    dn,upq,upv,dnt,nm=prep(qd,qu,vd,vu,ag,ash,fg,fsh)
    qkv,low,wqkv=project(scalars,x,dn,upq,upv,(jnp.stack([wq,wk,wv],0),))
    e,ot,o,rt=attend(scalars,qkv,x.shape[0]//SLOT)
    nn,r1,act,gp,w=feed_in(scalars,x,o,nm,(jnp.stack([wo]+[wi[:,c:c+D] for c in range(0,FF,D)],0),),FF)
    out,gfs,gmt=feed_out(scalars,nn,r1,act,gp,go,w,nm,(wt[None],))
    return qkv,low,wqkv,e,ot,rt,out,gfs,gmt,upq,upv,dnt

def shards(x,lengths,wq,wk,wv,wo,wi,wt,ag,ash,fg,fsh,qd,qu,vd,vu,go):
    n=device_count()
    valid=lengths[:,0]+lengths[:,1]+4
    me=(lax.axis_index("dp")*lax.axis_size("fsdp")+lax.axis_index("fsdp")).reshape(1)
    scalars=jnp.concatenate([me,valid]).astype(jnp.int32)
    forward=by_hops if n==32 and wq.shape[0]%8==0 else by_all_gather
    qkv,low,wqkv,e,ot,rt,out,gfs,gmt,upq,upv,dnt=forward(scalars,x,wq,wk,wv,wo,wi,wt,ag,ash,fg,fsh,qd,qu,vd,vu,go)
    d,gl,mine,other=attend_back(scalars,qkv,e,ot,rt,gmt,x,low,upq,upv)
    mine,other,gx=total_over_devices(mine,other,lambda: inputs_grad(gfs,d,gl,wqkv,dnt))
    qd,vd,qu,vu=finish(scalars,mine,other,1.0/(lengths.shape[0]*n))
    return out,gx,qd.T,qu,vd.T,vu

def solution(mesh):
    sp=P(AXES,None)
    return jax.shard_map(shards,mesh=mesh,in_specs=(sp,)*8+(P(),)*8+(sp,),
        out_specs=(sp,sp,P(),P(),P(),P()),check_vma=False)
```

```python
import functools
import jax
import jax.numpy as jnp
from jax import lax
from jax.experimental import pallas as pl
from jax.experimental.pallas import tpu as pltpu
from jax.sharding import PartitionSpec as P

HEAD_DIM=64; SLOT=512
F32=jnp.float32; BF=jnp.bfloat16
MIB=1024*1024
AXES=("dp","fsdp")
sd=jax.ShapeDtypeStruct
ANY=pl.BlockSpec(memory_space=pl.ANY)
HELD=pl.BlockSpec(memory_space=pltpu.VMEM)
SCALARS=pl.BlockSpec(memory_space=pltpu.SMEM)


def params(mib=56):
    return pltpu.CompilerParams(vmem_limit_bytes=mib*MIB)

def takes(us):
    return pl.CostEstimate(flops=int(us*1.1e9),bytes_accessed=0,transcendentals=0)


def dg(a,b,ca,cb):
    return lax.dot_general(a,b,(((ca,),(cb,)),((),())),preferred_element_type=F32)

def far(v):
    return pltpu.with_memory_space_constraint(v,pltpu.HBM)


def block_copies(me,bufs,to,sems):
    if len(bufs)==1:
        return [pltpu.make_async_copy(bufs[0],to,sems.at[0])]
    chip=lax.div(me,2); core=lax.rem(me,2)
    copies=[]
    for which,buf in enumerate(bufs):
        origin=core if which<2 else 1-core
        _,_,rows,half=buf.shape
        for i in range(8):
            dst=lax.bitwise_xor(chip,(which%2)*(2-origin)+(i//4)*(1+origin)+4*(i%4))
            at=to.at[:,pl.ds(pl.multiple_of(dst*rows,16),rows),pl.ds(pl.multiple_of(origin*half,128),half)]
            copies.append(pltpu.make_async_copy(buf.at[i],at,sems.at[len(copies)]))
    return copies

def start_all(copies):
    for c in copies: c.start()

def wait_all(copies):
    for c in copies: c.wait()

BLOCK_COPIES=32

def prep_kernel(qdt_ref,vdt_ref,qu_ref,vu_ref,ag_ref,ash_ref,fg_ref,fsh_ref,dn_ref,upq_ref,upv_ref,dnt_ref,nm_ref):
    D=qu_ref.shape[1]
    both=jnp.concatenate([qdt_ref[...],vdt_ref[...]],axis=0)
    dnt_ref[...]=both.astype(BF)
    dn_ref[...]=jnp.concatenate([both,jnp.zeros((112,D),F32)],axis=0).T.astype(BF)
    z8=jnp.zeros((8,D),F32); z=jnp.zeros((112,D),F32)
    upq_ref[...]=jnp.concatenate([qu_ref[...],z8,z],axis=0).astype(BF)
    upv_ref[...]=jnp.concatenate([z8,vu_ref[...],z],axis=0).astype(BF)
    for i,r in enumerate((ag_ref,ash_ref,fg_ref,fsh_ref)):
        nm_ref[i:i+1,:]=r[...].astype(F32)
    nm_ref[4:8,:]=jnp.zeros((4,D),F32)

def prep(qd,qu,vd,vu,ag,ash,fg,fsh):
    D=qu.shape[1]
    return pl.pallas_call(prep_kernel,out_shape=[sd((D,128),BF),sd((128,D),BF),sd((128,D),BF),sd((16,D),BF),sd((8,D),F32)],
        compiler_params=params(8),cost_estimate=takes(1),name="prep")(qd.T,vd.T,qu,vu,*(v.reshape(1,D) for v in (ag,ash,fg,fsh)))


def project_kernel(sc_ref,x_ref,dn_ref,upq_ref,upv_ref,*rest):
    *blocks,qkv_ref,low_ref,wo,w,sems,osem=rest
    rows,D=x_ref.shape
    copies=block_copies(sc_ref[0],blocks,w,sems)
    start_all(copies)
    lows=[]
    for s in range(rows//SLOT):
        low=dg(x_ref[s*SLOT:(s+1)*SLOT,:],dn_ref[...],1,0).astype(BF)
        low_ref[:,s*SLOT:(s+1)*SLOT]=low.T[:32]
        lows.append(low)
    wait_all(copies)
    whole=[pltpu.make_async_copy(w,wo,osem.at[0])]
    start_all(whole)
    for t,up in enumerate((upq_ref,None,upv_ref)):
        for s in range(rows//SLOT):
            r=slice(s*SLOT,(s+1)*SLOT)
            v=dg(x_ref[r,:],w[t],1,0)
            if up is not None: v=v+2.0*dg(lows[s],up[...],1,0)
            qkv_ref[r,t*D:(t+1)*D]=v.astype(BF)
    wait_all(whole)

def project(scalars,x,dn,upq,upv,blocks):
    rows,D=x.shape
    return pl.pallas_call(project_kernel,
        in_specs=[SCALARS,HELD,HELD,HELD,HELD]+[ANY]*len(blocks),
        out_specs=[HELD,HELD,ANY],
        out_shape=[pltpu.VMEM((rows,3*D),BF),sd((32,rows),BF),pltpu.HBM((3,D,D),BF)],
        scratch_shapes=[pltpu.VMEM((3,D,D),BF),pltpu.SemaphoreType.DMA((BLOCK_COPIES,)),pltpu.SemaphoreType.DMA((1,))],
        compiler_params=params(LIM["project"]),cost_estimate=takes(8),name="project")(scalars,x,dn,upq,upv,*blocks)

def attend_kernel(sc_ref,qkv_ref,e_ref,ot_ref,o_ref,rt_ref):
    s=pl.program_id(0); j=pl.program_id(1); J=pl.num_programs(1); D=256*J
    lane=lax.broadcasted_iota(jnp.int32,(SLOT,128),1)
    row=lax.broadcasted_iota(jnp.int32,(SLOT,128),0)
    bias=jnp.where(row<sc_ref[1+s],0.0,-1e30).astype(F32)
    rows=pl.ds(pl.multiple_of(s*SLOT,SLOT),SLOT)
    def part(which,p):
        return qkv_ref[rows,pl.ds(pl.multiple_of(which*D+256*j+128*p,128),128)].astype(F32)
    heads=[]
    for p in range(2):
        qp,kp,vp=part(0,p)*0.125,part(1,p),part(2,p)
        for h in range(2):
            own=(lane<64) if h==0 else (lane>=64)
            aux=64 if h==0 else 0
            one=jnp.where(lane==aux,1.0,0.0)
            heads.append((64*h,aux,jnp.where(own,qp,one).astype(BF),
                          jnp.where(own,kp,jnp.where(lane==aux,bias,0.0)).astype(BF),jnp.where(own,vp,one).astype(BF)))
    totals=[]; os=[]
    def weights(n,st):
        e_ref[n]=jnp.exp(st-jnp.max(st,axis=0,keepdims=True)).astype(BF)
    def mix(n):
        lo,aux,_,_,vm=heads[n]
        ot=dg(vm,e_ref[n],0,0)
        r=1.0/ot[aux:aux+1]
        totals.append(r)
        os.append((ot[lo:lo+64]*r).astype(BF))
    before=None
    for n in range(4):
        st=dg(heads[n][3],heads[n][2],1,1)
        if before is not None:
            weights(n-1,before)
            if n>1: mix(n-2)
        before=st
    weights(3,before)
    mix(2); mix(3)
    ot=jnp.concatenate(os,axis=0)
    ot_ref[...]=ot
    o_ref[rows,pl.ds(pl.multiple_of(256*j,256),256)]=ot.T
    rt_ref[0]=jnp.concatenate(totals+totals,axis=0)

def attend(scalars,qkv,slots):
    rows=qkv.shape[0]; D=qkv.shape[1]//3; J=D//256; H=D//HEAD_DIM
    return pl.pallas_call(attend_kernel,grid=(slots,J),
        in_specs=[SCALARS,HELD],
        out_specs=[pl.BlockSpec((4,SLOT,SLOT),lambda s,j:(s*J+j,0,0)),pl.BlockSpec((256,SLOT),lambda s,j:(s*J+j,0)),HELD,pl.BlockSpec((1,8,SLOT),lambda s,j:(s*J+j,0,0))],
        out_shape=[pltpu.HBM((slots*H,SLOT,SLOT),BF),pltpu.HBM((slots*D,SLOT),BF),pltpu.VMEM((rows,D),BF),pltpu.HBM((slots*J,8,SLOT),F32)],
        compiler_params=params(LIM["attend"]),cost_estimate=takes(16),name="attend")(scalars,qkv)


def norm_stats(value):
    mean=jnp.mean(value,axis=-1,keepdims=True)
    c=value-mean
    r=lax.rsqrt(jnp.mean(c*c,axis=-1,keepdims=True)+1e-5)
    return c*r,r

def norm_back(g,n,r):
    return r*(g-jnp.mean(g,axis=-1,keepdims=True)-n*jnp.mean(g*n,axis=-1,keepdims=True))

def gelu_pair(v):
    cdf=0.5+0.5*lax.erf(v*0.7071067811865476)
    return v*cdf, cdf+(0.3989422804014327*v)*jnp.exp(-0.5*v*v)

CH=256
LIM={"project":10,"attend":12,"feed_in":8,"feed_out":20,"attend_back":12,"inputs_grad":10}

def feed_in_kernel(sc_ref,x_ref,o_ref,nm_ref,*rest):
    *blocks,n1_ref,r1_ref,act_ref,gp_ref,w,sems=rest
    D=x_ref.shape[1]
    copies=block_copies(sc_ref[0],blocks,w,sems)
    start_all(copies); wait_all(copies)
    parts=[]
    for s in range(x_ref.shape[0]//SLOT):
        rows=slice(s*SLOT,(s+1)*SLOT)
        first=x_ref[rows,:].astype(F32)+dg(o_ref[rows,:],w[0],1,0)
        n1,r1=norm_stats(first)
        n1_ref[rows,:]=n1; r1_ref[rows,:]=jnp.broadcast_to(r1,(SLOT,128))
        parts.append((rows,(n1*nm_ref[0:1,:]+nm_ref[1:2,:]).astype(BF)))
    for c in range(0,act_ref.shape[1],CH):
        for rows,hb in parts:
            act,gp=gelu_pair(dg(hb,w[1+c//D,:,c%D:c%D+CH],1,0))
            act_ref[rows,c:c+CH]=act.astype(BF)
            gp_ref[rows,c:c+CH]=gp.astype(BF)

def feed_in(scalars,x,o,nm,blocks,FF):
    rows,D=x.shape
    return pl.pallas_call(feed_in_kernel,
        in_specs=[SCALARS,HELD,HELD,HELD]+[ANY]*len(blocks),
        out_specs=[HELD]*5,
        out_shape=[pltpu.VMEM((rows,D),F32),pltpu.VMEM((rows,128),F32),pltpu.VMEM((rows,FF),BF),pltpu.VMEM((rows,FF),BF),pltpu.VMEM((1+FF//D,D,D),BF)],
        scratch_shapes=[pltpu.SemaphoreType.DMA((BLOCK_COPIES,))],
        compiler_params=params(LIM["feed_in"]),cost_estimate=takes(14),name="feed_in")(scalars,x,o,nm,*blocks)

def feed_out_kernel(sc_ref,n1_ref,r1_ref,act_ref,gp_ref,go_ref,nm_ref,w,*rest):
    *blocks,out_ref,gfs_ref,gmt_ref,wt,gi_ref,sems=rest
    i=pl.program_id(0)
    @pl.when(i==0)
    def _():
        copies=block_copies(sc_ref[0],blocks,wt,sems)
        start_all(copies); wait_all(copies)
    T,D=go_ref.shape
    rows=pl.ds(pl.multiple_of(i*T,T),T)
    ag,ash,fg,fsh=(nm_ref[i:i+1,:] for i in range(4))
    n1=n1_ref[rows,:]; r1=r1_ref[rows,0:1]
    acc=n1*ag+ash+dg(act_ref[rows,:],wt[0],1,0)
    n2,r2=norm_stats(acc)
    out_ref[...]=(n2*fg+fsh).astype(BF)
    g2=norm_back(go_ref[...].astype(F32)*fg,n2,r2)
    g2b=g2.astype(BF)
    for c in range(0,gi_ref.shape[1],CH):
        ga=dg(g2b,wt[0,c:c+CH,:],1,1)
        gi_ref[:,c:c+CH]=(ga*gp_ref[rows,c:c+CH].astype(F32)).astype(BF)
    acc=g2
    for b in range(gi_ref.shape[1]//D):
        acc=acc+dg(gi_ref[:,b*D:(b+1)*D],w[1+b],1,1)
    g1=norm_back(acc*ag,n1,r1)
    gfs_ref[...]=g1
    gmt_ref[:,rows]=dg(w[0],g1.astype(BF),1,1).astype(BF)

def feed_out(scalars,n1,r1,act,gp,go,w,nm,blocks):
    rows,D=n1.shape; FF=act.shape[1]
    row=pl.BlockSpec((SLOT,D),lambda i:(i,0))
    return pl.pallas_call(feed_out_kernel,grid=(rows//SLOT,),
        in_specs=[SCALARS,HELD,HELD,HELD,HELD,row,HELD,HELD]+[ANY]*len(blocks),
        out_specs=[row,row,HELD],
        out_shape=[sd((rows,D),BF),pltpu.HBM((rows,D),F32),pltpu.VMEM((D,rows),BF)],
        scratch_shapes=[pltpu.VMEM((1,FF,D),BF),pltpu.VMEM((SLOT,FF),BF),pltpu.SemaphoreType.DMA((BLOCK_COPIES,))],
        compiler_params=params(LIM["feed_out"]),cost_estimate=takes(24),name="feed_out")(scalars,n1,r1,act,gp,go,nm,w,*blocks)


def attend_back_kernel(sc_ref,q_ref,k_ref,v_ref,e_ref,ot_ref,rt_ref,gmt_ref,x_ref,low_ref,upq_ref,upv_ref,
                       d_ref,gl_ref,mine_ref,other_ref,glacc,ad_ref):
    s=pl.program_id(0); j=pl.program_id(1); J=pl.num_programs(1)
    lane=lax.broadcasted_iota(jnp.int32,(SLOT,128),1)
    rowi=lax.broadcasted_iota(jnp.int32,(128,SLOT),0)
    D=256*J
    rows=pl.ds(pl.multiple_of(s*SLOT,SLOT),SLOT)
    def place_of(which,p):
        return rows,pl.ds(pl.multiple_of(which*D+256*j+128*p,128),128)
    gmq=gmt_ref[pl.ds(pl.multiple_of(256*j,256),256),rows]
    otq=ot_ref[...]
    dqts=[]; dvs=[]
    for p in range(2):
        cols=slice(128*p,128*p+128)
        qp,kp,vp=(w[:,cols].astype(F32) for w in (q_ref,k_ref,v_ref))
        qp=qp*0.125; kp=kp*0.125
        gm=gmq[cols,:].astype(F32); om=otq[cols,:].astype(F32)
        pr=gm*om
        dkp=None; dvp=None; dqt=None
        for h in range(2):
            own=(lane<64) if h==0 else (lane>=64)
            ownr=(rowi<64) if h==0 else (rowi>=64)
            aux=64 if h==0 else 0
            r=rt_ref[0,2*p+h:2*p+h+1,:]
            d=-jnp.sum(pr[64*h:64*h+64],axis=0,keepdims=True)*r
            dhi=d.astype(BF).astype(F32)
            dlo=d-dhi
            gs=gm*r
            gaug=jnp.where(ownr,gs,jnp.where(rowi==aux,dhi,jnp.where(rowi==aux+1,dlo,0.0))).astype(BF)
            gown=jnp.where(ownr,gs,0.0).astype(BF)
            vm=jnp.where(own,vp,jnp.where((lane==aux)|(lane==aux+1),1.0,0.0)).astype(BF)
            e=e_ref[2*p+h]
            ds=(dg(vm,gaug,1,0)*e.astype(F32)).astype(BF)
            qm=jnp.where(own,qp,0.0).astype(BF)
            km=jnp.where(own,kp,0.0).astype(BF)
            dv=dg(e,gown,1,1)
            dk=dg(ds,qm,1,0)
            dq=dg(km,ds,0,0)
            dvp=dv if dvp is None else dvp+dv
            dkp=dk if dkp is None else dkp+dk
            dqt=dq if dqt is None else dqt+dq
        d_ref[place_of(1,p)]=dkp.astype(BF)
        dvs.append(dvp.astype(BF))
        d_ref[place_of(2,p)]=dvs[p]
        dqts.append(dqt.astype(BF))
    dqt=jnp.concatenate(dqts,axis=0)
    dqb=dqt.T
    d_ref[rows,pl.ds(pl.multiple_of(256*j,256),256)]=dqb
    dvb=jnp.concatenate(dvs,axis=1)
    glq=dg(upq_ref[...],dqt,1,0)
    glv=dg(upv_ref[...],dvb,1,1)
    part=2.0*(glq+glv)
    @pl.when(j==0)
    def _(): glacc[...]=part
    @pl.when(j>0)
    def _(): glacc[...]+=part
    low=low_ref[...]
    c0=pl.multiple_of(j*256,256)
    upq=2.0*dg(low[:16],dqb,1,0)
    upv=2.0*dg(low[:16],dvb,1,0)
    upg=jnp.concatenate([upq[0:8],upv[8:16]],axis=0)
    def add(rows,cols,v):
        @pl.when(s==0)
        def _(): ad_ref[rows,cols]=v
        @pl.when(s>0)
        def _(): ad_ref[rows,cols]+=v
    add(slice(16,32),pl.ds(c0,256),upg)
    @pl.when(j==J-1)
    def _():
        gl=glacc[...].astype(BF)
        gl_ref[...]=gl
        add(slice(0,16),slice(None),dg(gl,x_ref[...],1,0))
        core=lax.rem(sc_ref[0],2)
        for c,(a,b) in enumerate(((mine_ref,other_ref),(other_ref,mine_ref))):
            @pl.when((s==pl.num_programs(0)-1)&(core==c))
            def _():
                a[...]=ad_ref[0:16,:]
                b[...]=ad_ref[16:32,:]

def attend_back(scalars,qkv,e,ot,rt,gmt,x,low,upq,upv):
    rows,D=x.shape; J=D//256; S=rows//SLOT
    up=pl.BlockSpec((16,256),lambda s,j:(0,j))
    return pl.pallas_call(attend_back_kernel,grid=(S,J),
        in_specs=[SCALARS,*[pl.BlockSpec((SLOT,256),lambda s,j,w=w:(s,w*J+j)) for w in range(3)],
                  pl.BlockSpec((4,SLOT,SLOT),lambda s,j:(s*J+j,0,0)),pl.BlockSpec((256,SLOT),lambda s,j:(s*J+j,0)),
                  pl.BlockSpec((1,8,SLOT),lambda s,j:(s*J+j,0,0)),HELD,
                  pl.BlockSpec((SLOT,D),lambda s,j:(s,0)),pl.BlockSpec((32,SLOT),lambda s,j:(0,s)),up,up],
        out_specs=[HELD,pl.BlockSpec((16,SLOT),lambda s,j:(0,s)),HELD,HELD],
        out_shape=[pltpu.VMEM((rows,3*D),BF),sd((16,rows),BF),pltpu.VMEM((16,D),F32),pltpu.VMEM((16,D),F32)],
        scratch_shapes=[pltpu.VMEM((16,SLOT),F32),pltpu.VMEM((32,D),F32)],
        compiler_params=params(LIM["attend_back"]),cost_estimate=takes(18),name="attend_back")(scalars,far(qkv),far(qkv),far(qkv),far(e),far(ot),rt,gmt,x,low,upq,upv)

def inputs_kernel(gfs_ref,d_ref,gl,w_ref,dnt_ref,out_ref):
    T=gfs_ref.shape[0]
    rows=pl.ds(pl.multiple_of(pl.program_id(0)*T,T),T)
    D=gfs_ref.shape[1]
    v=gfs_ref[...]+dg(gl[...],dnt_ref[...],0,0)
    for t in range(3): v=v+dg(d_ref[rows,t*D:(t+1)*D],w_ref[t],1,1)
    out_ref[...]=v

def inputs_grad(gfs,d,gl,w,dnt):
    rows,D=gfs.shape
    row=pl.BlockSpec((SLOT,D),lambda i:(i,0))
    return pl.pallas_call(inputs_kernel,grid=(rows//SLOT,),
        in_specs=[row,HELD,pl.BlockSpec((16,SLOT),lambda i:(0,i)),HELD,HELD],
        out_specs=row,out_shape=sd((rows,D),F32),
        compiler_params=params(LIM["inputs_grad"]),cost_estimate=takes(7),name="inputs_grad")(gfs,d,gl,w,dnt)


def device_count():
    return lax.axis_size("dp")*lax.axis_size("fsdp")

def permute(v,target):
    return lax.ppermute(v,AXES,[(i,target(i)) for i in range(device_count())])

def exchange(v,mask):
    return permute(v,lambda i:i^mask)

def along_z(block):
    top=device_count()//4
    return [block]+[exchange(block,top*m) for m in (1,2,3)]

def near_hop(v):
    return permute(v,lambda i:i^(4 if i%2 else 2))

def far_hop(v):
    return permute(v,lambda i:i^(2 if i%2 else 4))

def in_bands(bands,*blocks):
    return tuple(b.reshape(8,bands,-1,b.shape[2]) for b in blocks)

def core_pair(v):
    groups=[[2*i,2*i+1] for i in range(lax.axis_size("fsdp")//2)]
    return lax.all_gather(v,"fsdp",axis=0,tiled=False,axis_index_groups=groups)

def column_half(both):
    c=lax.axis_index("fsdp")%2
    half=both.shape[2]//2
    return lax.dynamic_slice_in_dim(both,c*half,half,axis=2).reshape(-1,half)

def total_over_devices(mine,other,meanwhile):
    n=device_count()
    mine=mine+exchange(other,1)
    got=[exchange(mine,m) for m in range(2,n//4,2)]
    for g in got: mine=mine+g
    got=[exchange(mine,m) for m in (n//4,n//2,3*n//4)]
    got,done=tie(got,meanwhile())
    for g in got: mine=mine+g
    return mine,exchange(mine,1),done

def finish_kernel(scale,sc_ref,mine_ref,other_ref,*outs):
    core=lax.rem(sc_ref[0],2)
    for c,halves in enumerate(((mine_ref,other_ref),(other_ref,mine_ref))):
        @pl.when(core==c)
        def _():
            for i,o in enumerate(outs): o[...]=halves[i//2][8*(i%2):8*(i%2)+8,:]*scale

def finish(scalars,mine,other,scale):
    D=mine.shape[1]
    return pl.pallas_call(functools.partial(finish_kernel,scale),in_specs=[SCALARS,HELD,HELD],out_specs=[HELD]*4,
        out_shape=[sd((8,D),F32)]*4,compiler_params=params(8),cost_estimate=takes(1),name="finish")(scalars,mine,other)

def tie(*v):
    return lax.optimization_barrier(v)

def by_hops(scalars,x,wq,wk,wv,wo,wi,wt,ag,ash,fg,fsh,qd,qu,vd,vu,go):
    D=wq.shape[1]; FF=wi.shape[1]; bands=FF//D; r=wq.shape[0]
    top=device_count()//4
    both=core_pair(jnp.concatenate([wq,wk,wv],0))
    s1=jnp.concatenate([column_half(both[:,r*t:r*t+r]) for t in range(3)],0)
    z1=along_z(s1)
    wo,wi,wt,qd,s1=tie(wo,wi,wt,qd,s1)
    bo,bi,bt=core_pair(wo),core_pair(wi),core_pair(wt)
    s2=jnp.concatenate([column_half(bo)]+[column_half(bi[:,:,D*t:D*t+D]) for t in range(bands)],0)
    s3=column_half(bt)
    dn,upq,upv,dnt,nm=prep(qd,qu,vd,vu,ag,ash,fg,fsh)
    n3=near_hop(s3)
    z1,s2,dn,scalars=tie(z1,s2,dn,scalars)
    a1=jnp.stack(z1,0)
    n1=near_hop(a1)
    z2=exchange(s2,2*top)
    b3=jnp.stack([s3,n3],0)
    y3=exchange(b3,top)
    n1,z2,s2,n3=tie(n1,z2,s2,n3)
    f1=jnp.concatenate([a1,n1],0)
    h1=far_hop(f1); of1=exchange(f1,1)
    e2=jnp.stack([s2,z2],0)
    y2=exchange(e2,top)
    m2=near_hop(e2)
    y2,y3=tie(y2,y3)
    n2=near_hop(y2)
    g3=jnp.stack([b3,y3],0)
    z3=exchange(g3,2*top)
    h1,of1=tie(h1,of1)
    oh1=exchange(h1,1)
    oh1,=tie(oh1)
    f2=jnp.stack([e2[0],y2[0],e2[1],y2[1],m2[0],n2[0],m2[1],n2[1]],0)
    h2=far_hop(f2); of2=exchange(f2,1)
    qkv,low,wqkv=project(scalars,x,dn,upq,upv,in_bands(3,f1,h1,of1,oh1))
    e,ot,o,rt=attend(scalars,qkv,x.shape[0]//SLOT)
    h2,o,of2,z3=tie(h2,o,of2,z3)
    oh2=exchange(h2,1)
    f3=jnp.concatenate([g3,z3],0).swapaxes(0,1).reshape(8,-1,D//2)
    h3=far_hop(f3); of3=exchange(f3,1)
    oh2,=tie(oh2)
    nn,r1,act,gp,w=feed_in(scalars,x,o,nm,in_bands(1+bands,f2,h2,of2,oh2),FF)
    h3,nn,of3=tie(h3,nn,of3)
    oh3=exchange(h3,1)
    out,gfs,gmt=feed_out(scalars,nn,r1,act,gp,go,w,nm,in_bands(1,f3,h3,of3,oh3))
    return qkv,low,wqkv,e,ot,rt,out,gfs,gmt,upq,upv,dnt

def by_all_gather(scalars,x,wq,wk,wv,wo,wi,wt,ag,ash,fg,fsh,qd,qu,vd,vu,go):
    wq,wk,wv,wo,wi,wt=(lax.all_gather(w,AXES,axis=0,tiled=True) for w in (wq,wk,wv,wo,wi,wt))
    D=wq.shape[1]; FF=wi.shape[1]
    dn,upq,upv,dnt,nm=prep(qd,qu,vd,vu,ag,ash,fg,fsh)
    qkv,low,wqkv=project(scalars,x,dn,upq,upv,(jnp.stack([wq,wk,wv],0),))
    e,ot,o,rt=attend(scalars,qkv,x.shape[0]//SLOT)
    nn,r1,act,gp,w=feed_in(scalars,x,o,nm,(jnp.stack([wo]+[wi[:,c:c+D] for c in range(0,FF,D)],0),),FF)
    out,gfs,gmt=feed_out(scalars,nn,r1,act,gp,go,w,nm,(wt[None],))
    return qkv,low,wqkv,e,ot,rt,out,gfs,gmt,upq,upv,dnt

def shards(x,lengths,wq,wk,wv,wo,wi,wt,ag,ash,fg,fsh,qd,qu,vd,vu,go):
    n=device_count()
    valid=lengths[:,0]+lengths[:,1]+4
    me=(lax.axis_index("dp")*lax.axis_size("fsdp")+lax.axis_index("fsdp")).reshape(1)
    scalars=jnp.concatenate([me,valid]).astype(jnp.int32)
    forward=by_hops if n==32 and wq.shape[0]%8==0 else by_all_gather
    qkv,low,wqkv,e,ot,rt,out,gfs,gmt,upq,upv,dnt=forward(scalars,x,wq,wk,wv,wo,wi,wt,ag,ash,fg,fsh,qd,qu,vd,vu,go)
    d,gl,mine,other=attend_back(scalars,qkv,e,ot,rt,gmt,x,low,upq,upv)
    mine,other,gx=total_over_devices(mine,other,lambda: inputs_grad(gfs,d,gl,wqkv,dnt))
    qd,vd,qu,vu=finish(scalars,mine,other,1.0/(lengths.shape[0]*n))
    return out,gx,qd.T,qu,vd.T,vu

def solution(mesh):
    sp=P(AXES,None)
    return jax.shard_map(shards,mesh=mesh,in_specs=(sp,)*8+(P(),)*8+(sp,),
        out_specs=(sp,sp,P(),P(),P(),P()),check_vma=False)
```

```python
import functools
import jax
import jax.numpy as jnp
from jax import lax
from jax.experimental import pallas as pl
from jax.experimental.pallas import tpu as pltpu
from jax.sharding import PartitionSpec as P

HEAD_DIM=64; SLOT=512
F32=jnp.float32; BF=jnp.bfloat16
MIB=1024*1024
AXES=("dp","fsdp")
sd=jax.ShapeDtypeStruct
ANY=pl.BlockSpec(memory_space=pl.ANY)
HELD=pl.BlockSpec(memory_space=pltpu.VMEM)
SCALARS=pl.BlockSpec(memory_space=pltpu.SMEM)


def params(mib=56):
    return pltpu.CompilerParams(vmem_limit_bytes=mib*MIB)

def takes(us):
    return pl.CostEstimate(flops=int(us*1.1e9),bytes_accessed=0,transcendentals=0)


def dg(a,b,ca,cb):
    return lax.dot_general(a,b,(((ca,),(cb,)),((),())),preferred_element_type=F32)

def far(v):
    return pltpu.with_memory_space_constraint(v,pltpu.HBM)


def block_copies(me,bufs,to,sems):
    if len(bufs)==1:
        return [pltpu.make_async_copy(bufs[0],to,sems.at[0])]
    chip=lax.div(me,2); core=lax.rem(me,2)
    copies=[]
    for which,buf in enumerate(bufs):
        origin=core if which<2 else 1-core
        _,_,rows,half=buf.shape
        for i in range(8):
            dst=lax.bitwise_xor(chip,(which%2)*(2-origin)+(i//4)*(1+origin)+4*(i%4))
            at=to.at[:,pl.ds(pl.multiple_of(dst*rows,16),rows),pl.ds(pl.multiple_of(origin*half,128),half)]
            copies.append(pltpu.make_async_copy(buf.at[i],at,sems.at[len(copies)]))
    return copies

def start_all(copies):
    for c in copies: c.start()

def wait_all(copies):
    for c in copies: c.wait()

BLOCK_COPIES=32

def prep_kernel(qdt_ref,vdt_ref,qu_ref,vu_ref,ag_ref,ash_ref,fg_ref,fsh_ref,dn_ref,upq_ref,upv_ref,dnt_ref,nm_ref):
    D=qu_ref.shape[1]
    both=jnp.concatenate([qdt_ref[...],vdt_ref[...]],axis=0)
    dnt_ref[...]=both.astype(BF)
    dn_ref[...]=jnp.concatenate([both,jnp.zeros((112,D),F32)],axis=0).T.astype(BF)
    z8=jnp.zeros((8,D),F32); z=jnp.zeros((112,D),F32)
    upq_ref[...]=jnp.concatenate([qu_ref[...],z8,z],axis=0).astype(BF)
    upv_ref[...]=jnp.concatenate([z8,vu_ref[...],z],axis=0).astype(BF)
    for i,r in enumerate((ag_ref,ash_ref,fg_ref,fsh_ref)):
        nm_ref[i:i+1,:]=r[...].astype(F32)
    nm_ref[4:8,:]=jnp.zeros((4,D),F32)

def prep(qd,qu,vd,vu,ag,ash,fg,fsh):
    D=qu.shape[1]
    return pl.pallas_call(prep_kernel,out_shape=[sd((D,128),BF),sd((128,D),BF),sd((128,D),BF),sd((16,D),BF),sd((8,D),F32)],
        compiler_params=params(8),cost_estimate=takes(1),name="prep")(qd.T,vd.T,qu,vu,*(v.reshape(1,D) for v in (ag,ash,fg,fsh)))


def low_kernel(x_ref,dn_ref,upq_ref,upv_ref,low_ref,lq_ref,lv_ref):
    for s in range(x_ref.shape[0]//SLOT):
        r=slice(s*SLOT,(s+1)*SLOT)
        low=dg(x_ref[r,:],dn_ref[...],1,0).astype(BF)
        low_ref[:,r]=low.T[:32]
        lq_ref[r,:]=2.0*dg(low,upq_ref[...],1,0)
        lv_ref[r,:]=2.0*dg(low,upv_ref[...],1,0)

def low_rank(x,dn,upq,upv):
    rows,D=x.shape
    return pl.pallas_call(low_kernel,in_specs=[HELD]*4,out_specs=[HELD]*3,
        out_shape=[sd((32,rows),BF),pltpu.VMEM((rows,D),F32),pltpu.VMEM((rows,D),F32)],
        compiler_params=params(LIM["low_rank"]),cost_estimate=takes(3),name="low_rank")(x,dn,upq,upv)

def project_kernel(sc_ref,x_ref,lq_ref,lv_ref,*rest):
    *blocks,qkv_ref,wo,w,sems,osem=rest
    rows,D=x_ref.shape
    copies=block_copies(sc_ref[0],blocks,w,sems)
    start_all(copies)
    wait_all(copies)
    whole=[pltpu.make_async_copy(w,wo,osem.at[0])]
    start_all(whole)
    for t,up in enumerate((lq_ref,None,lv_ref)):
        for s in range(rows//SLOT):
            r=slice(s*SLOT,(s+1)*SLOT)
            v=dg(x_ref[r,:],w[t],1,0)
            if up is not None: v=v+up[r,:]
            qkv_ref[r,t*D:(t+1)*D]=v.astype(BF)
    wait_all(whole)

def project(scalars,x,lq,lv,blocks):
    rows,D=x.shape
    return pl.pallas_call(project_kernel,
        in_specs=[SCALARS,HELD,HELD,HELD]+[ANY]*len(blocks),
        out_specs=[HELD,ANY],
        out_shape=[pltpu.VMEM((rows,3*D),BF),pltpu.HBM((3,D,D),BF)],
        scratch_shapes=[pltpu.VMEM((3,D,D),BF),pltpu.SemaphoreType.DMA((BLOCK_COPIES,)),pltpu.SemaphoreType.DMA((1,))],
        compiler_params=params(LIM["project"]),cost_estimate=takes(8),name="project")(scalars,x,lq,lv,*blocks)

def attend_kernel(sc_ref,qkv_ref,e_ref,ot_ref,o_ref,rt_ref):
    s=pl.program_id(0); j=pl.program_id(1); J=pl.num_programs(1); D=256*J
    lane=lax.broadcasted_iota(jnp.int32,(SLOT,128),1)
    row=lax.broadcasted_iota(jnp.int32,(SLOT,128),0)
    bias=jnp.where(row<sc_ref[1+s],0.0,-1e30).astype(F32)
    rows=pl.ds(pl.multiple_of(s*SLOT,SLOT),SLOT)
    def part(which,p):
        return qkv_ref[rows,pl.ds(pl.multiple_of(which*D+256*j+128*p,128),128)].astype(F32)
    heads=[]
    for p in range(2):
        qp,kp,vp=part(0,p)*0.125,part(1,p),part(2,p)
        for h in range(2):
            own=(lane<64) if h==0 else (lane>=64)
            aux=64 if h==0 else 0
            one=jnp.where(lane==aux,1.0,0.0)
            heads.append((64*h,aux,jnp.where(own,qp,one).astype(BF),
                          jnp.where(own,kp,jnp.where(lane==aux,bias,0.0)).astype(BF),jnp.where(own,vp,one).astype(BF)))
    totals=[]; os=[]
    def weights(n,st):
        e_ref[n]=jnp.exp(st-jnp.max(st,axis=0,keepdims=True)).astype(BF)
    def mix(n):
        lo,aux,_,_,vm=heads[n]
        ot=dg(vm,e_ref[n],0,0)
        r=1.0/ot[aux:aux+1]
        totals.append(r)
        os.append((ot[lo:lo+64]*r).astype(BF))
    before=None
    for n in range(4):
        st=dg(heads[n][3],heads[n][2],1,1)
        if before is not None:
            weights(n-1,before)
            if n>1: mix(n-2)
        before=st
    weights(3,before)
    mix(2); mix(3)
    ot=jnp.concatenate(os,axis=0)
    ot_ref[...]=ot
    o_ref[rows,pl.ds(pl.multiple_of(256*j,256),256)]=ot.T
    rt_ref[0]=jnp.concatenate(totals+totals,axis=0)

def attend(scalars,qkv,slots):
    rows=qkv.shape[0]; D=qkv.shape[1]//3; J=D//256; H=D//HEAD_DIM
    return pl.pallas_call(attend_kernel,grid=(slots,J),
        in_specs=[SCALARS,HELD],
        out_specs=[pl.BlockSpec((4,SLOT,SLOT),lambda s,j:(s*J+j,0,0)),pl.BlockSpec((256,SLOT),lambda s,j:(s*J+j,0)),HELD,pl.BlockSpec((1,8,SLOT),lambda s,j:(s*J+j,0,0))],
        out_shape=[pltpu.HBM((slots*H,SLOT,SLOT),BF),pltpu.HBM((slots*D,SLOT),BF),pltpu.VMEM((rows,D),BF),pltpu.HBM((slots*J,8,SLOT),F32)],
        compiler_params=params(LIM["attend"]),cost_estimate=takes(16),name="attend")(scalars,qkv)


def norm_stats(value):
    mean=jnp.mean(value,axis=-1,keepdims=True)
    c=value-mean
    r=lax.rsqrt(jnp.mean(c*c,axis=-1,keepdims=True)+1e-5)
    return c*r,r

def norm_back(g,n,r):
    return r*(g-jnp.mean(g,axis=-1,keepdims=True)-n*jnp.mean(g*n,axis=-1,keepdims=True))

def gelu_pair(v):
    cdf=0.5+0.5*lax.erf(v*0.7071067811865476)
    return v*cdf, cdf+(0.3989422804014327*v)*jnp.exp(-0.5*v*v)

CH=256
LIM={"project":10,"attend":12,"feed_in":8,"feed_out":18,"attend_back":12,"inputs_grad":10,"low_rank":10}

def feed_in_kernel(sc_ref,x_ref,o_ref,nm_ref,*rest):
    *blocks,n1_ref,r1_ref,act_ref,gp_ref,w,sems=rest
    D=x_ref.shape[1]
    copies=block_copies(sc_ref[0],blocks,w,sems)
    start_all(copies); wait_all(copies)
    parts=[]
    for s in range(x_ref.shape[0]//SLOT):
        rows=slice(s*SLOT,(s+1)*SLOT)
        first=x_ref[rows,:].astype(F32)+dg(o_ref[rows,:],w[0],1,0)
        n1,r1=norm_stats(first)
        n1_ref[rows,:]=n1; r1_ref[rows,:]=jnp.broadcast_to(r1,(SLOT,128))
        parts.append((rows,(n1*nm_ref[0:1,:]+nm_ref[1:2,:]).astype(BF)))
    for c in range(0,act_ref.shape[1],CH):
        for rows,hb in parts:
            act,gp=gelu_pair(dg(hb,w[1+c//D,:,c%D:c%D+CH],1,0))
            act_ref[rows,c:c+CH]=act.astype(BF)
            gp_ref[rows,c:c+CH]=gp.astype(BF)

def feed_in(scalars,x,o,nm,blocks,FF):
    rows,D=x.shape
    return pl.pallas_call(feed_in_kernel,
        in_specs=[SCALARS,HELD,HELD,HELD]+[ANY]*len(blocks),
        out_specs=[HELD]*5,
        out_shape=[pltpu.VMEM((rows,D),F32),pltpu.VMEM((rows,128),F32),pltpu.VMEM((rows,FF),BF),pltpu.VMEM((rows,FF),BF),pltpu.VMEM((1+FF//D,D,D),BF)],
        scratch_shapes=[pltpu.SemaphoreType.DMA((BLOCK_COPIES,))],
        compiler_params=params(LIM["feed_in"]),cost_estimate=takes(14),name="feed_in")(scalars,x,o,nm,*blocks)

def feed_out_kernel(sc_ref,n1_ref,r1_ref,act_ref,gp_ref,go_ref,nm_ref,w,*rest):
    *blocks,out_ref,gfs_ref,gmt_ref,gi_ref,wt,held,sems,osems=rest
    copies=block_copies(sc_ref[0],blocks,wt,sems)
    start_all(copies); wait_all(copies)
    rows,D=go_ref.shape; FF=gi_ref.shape[1]
    ag,ash,fg,fsh=(nm_ref[i:i+1,:] for i in range(4))
    part=[slice(s*SLOT,(s+1)*SLOT) for s in range(rows//SLOT)]
    acc={}; g2={}; g1={}
    outs=[pltpu.make_async_copy(held.at[pl.ds(s*SLOT,SLOT),:],out_ref.at[pl.ds(s*SLOT,SLOT),:],osems.at[s]) for s in range(len(part))]
    def second_sum(s):
        acc[s]=n1_ref[part[s],:]*ag+ash+dg(act_ref[part[s],:],wt[0],1,0)
    def second_norm(s):
        n2,r2=norm_stats(acc[s])
        held[part[s],:]=(n2*fg+fsh).astype(BF)
        g2[s]=norm_back(go_ref[part[s],:].astype(F32)*fg,n2,r2)
    def inner_grad(s):
        g=g2[s].astype(BF)
        for c in range(0,FF,CH):
            ga=dg(g,wt[0,c:c+CH,:],1,1)
            gi_ref[part[s],c:c+CH]=(ga*gp_ref[part[s],c:c+CH].astype(F32)).astype(BF)
    def first_grad(s):
        v=g2[s]
        for b in range(FF//D): v=v+dg(gi_ref[part[s],b*D:(b+1)*D],w[1+b],1,1)
        acc[s]=v
    def first_norm(s):
        g=norm_back(acc[s]*ag,n1_ref[part[s],:],r1_ref[part[s],0:1])
        gfs_ref[part[s],:]=g
        g1[s]=g.astype(BF)
    def mixed_grad(s):
        gmt_ref[:,part[s]]=dg(w[0],g1[s],1,1).astype(BF)
    stages=(second_sum,second_norm,inner_grad,first_grad,first_norm,mixed_grad)
    order=sorted((2*k+(3*s if k else 0),s,k) for s in range(len(part)) for k in range(len(stages)))
    for _,s,k in order:
        stages[k](s)
    start_all(outs); wait_all(outs)

def feed_out(scalars,n1,r1,act,gp,go,w,nm,blocks):
    rows,D=n1.shape; FF=act.shape[1]
    return pl.pallas_call(feed_out_kernel,
        in_specs=[SCALARS]+[HELD]*7+[ANY]*len(blocks),
        out_specs=[ANY,HELD,HELD,HELD],
        out_shape=[pltpu.HBM((rows,D),BF),pltpu.VMEM((rows,D),F32),pltpu.VMEM((D,rows),BF),pltpu.VMEM((rows,FF),BF)],
        input_output_aliases={3:3},
        scratch_shapes=[pltpu.VMEM((1,FF,D),BF),pltpu.VMEM((rows,D),BF),
                        pltpu.SemaphoreType.DMA((BLOCK_COPIES,)),pltpu.SemaphoreType.DMA((rows//SLOT,))],
        compiler_params=params(LIM["feed_out"]),cost_estimate=takes(24),name="feed_out")(scalars,n1,r1,act,gp,go,nm,w,*blocks)[:3]


def attend_back_kernel(sc_ref,q_ref,k_ref,v_ref,e_ref,ot_ref,rt_ref,gmt_ref,x_ref,low_ref,upq_ref,upv_ref,
                       d_ref,gl_ref,mine_ref,other_ref,glacc,ad_ref):
    s=pl.program_id(0); j=pl.program_id(1); J=pl.num_programs(1)
    lane=lax.broadcasted_iota(jnp.int32,(SLOT,128),1)
    rowi=lax.broadcasted_iota(jnp.int32,(128,SLOT),0)
    D=256*J
    rows=pl.ds(pl.multiple_of(s*SLOT,SLOT),SLOT)
    def place_of(which,p):
        return rows,pl.ds(pl.multiple_of(which*D+256*j+128*p,128),128)
    gmq=gmt_ref[pl.ds(pl.multiple_of(256*j,256),256),rows]
    otq=ot_ref[...]
    dqts=[]; dvs=[]
    for p in range(2):
        cols=slice(128*p,128*p+128)
        qp,kp,vp=(w[:,cols].astype(F32) for w in (q_ref,k_ref,v_ref))
        qp=qp*0.125; kp=kp*0.125
        gm=gmq[cols,:].astype(F32); om=otq[cols,:].astype(F32)
        pr=gm*om
        dkp=None; dvp=None; dqt=None
        for h in range(2):
            own=(lane<64) if h==0 else (lane>=64)
            ownr=(rowi<64) if h==0 else (rowi>=64)
            aux=64 if h==0 else 0
            r=rt_ref[0,2*p+h:2*p+h+1,:]
            d=-jnp.sum(pr[64*h:64*h+64],axis=0,keepdims=True)*r
            dhi=d.astype(BF).astype(F32)
            dlo=d-dhi
            gs=gm*r
            gaug=jnp.where(ownr,gs,jnp.where(rowi==aux,dhi,jnp.where(rowi==aux+1,dlo,0.0))).astype(BF)
            gown=jnp.where(ownr,gs,0.0).astype(BF)
            vm=jnp.where(own,vp,jnp.where((lane==aux)|(lane==aux+1),1.0,0.0)).astype(BF)
            e=e_ref[2*p+h]
            ds=(dg(vm,gaug,1,0)*e.astype(F32)).astype(BF)
            qm=jnp.where(own,qp,0.0).astype(BF)
            km=jnp.where(own,kp,0.0).astype(BF)
            dv=dg(e,gown,1,1)
            dk=dg(ds,qm,1,0)
            dq=dg(km,ds,0,0)
            dvp=dv if dvp is None else dvp+dv
            dkp=dk if dkp is None else dkp+dk
            dqt=dq if dqt is None else dqt+dq
        d_ref[place_of(1,p)]=dkp.astype(BF)
        dvs.append(dvp.astype(BF))
        d_ref[place_of(2,p)]=dvs[p]
        dqts.append(dqt.astype(BF))
    dqt=jnp.concatenate(dqts,axis=0)
    dqb=dqt.T
    d_ref[rows,pl.ds(pl.multiple_of(256*j,256),256)]=dqb
    dvb=jnp.concatenate(dvs,axis=1)
    glq=dg(upq_ref[...],dqt,1,0)
    glv=dg(upv_ref[...],dvb,1,1)
    part=2.0*(glq+glv)
    @pl.when(j==0)
    def _(): glacc[...]=part
    @pl.when(j>0)
    def _(): glacc[...]+=part
    low=low_ref[...]
    c0=pl.multiple_of(j*256,256)
    upq=2.0*dg(low[:16],dqb,1,0)
    upv=2.0*dg(low[:16],dvb,1,0)
    upg=jnp.concatenate([upq[0:8],upv[8:16]],axis=0)
    def add(rows,cols,v):
        @pl.when(s==0)
        def _(): ad_ref[rows,cols]=v
        @pl.when(s>0)
        def _(): ad_ref[rows,cols]+=v
    add(slice(16,32),pl.ds(c0,256),upg)
    @pl.when(j==J-1)
    def _():
        gl=glacc[...].astype(BF)
        gl_ref[...]=gl
        add(slice(0,16),slice(None),dg(gl,x_ref[...],1,0))
        core=lax.rem(sc_ref[0],2)
        for c,(a,b) in enumerate(((mine_ref,other_ref),(other_ref,mine_ref))):
            @pl.when((s==pl.num_programs(0)-1)&(core==c))
            def _():
                a[...]=ad_ref[0:16,:]
                b[...]=ad_ref[16:32,:]

def attend_back(scalars,qkv,e,ot,rt,gmt,x,low,upq,upv):
    rows,D=x.shape; J=D//256; S=rows//SLOT
    up=pl.BlockSpec((16,256),lambda s,j:(0,j))
    return pl.pallas_call(attend_back_kernel,grid=(S,J),
        in_specs=[SCALARS,*[pl.BlockSpec((SLOT,256),lambda s,j,w=w:(s,w*J+j)) for w in range(3)],
                  pl.BlockSpec((4,SLOT,SLOT),lambda s,j:(s*J+j,0,0)),pl.BlockSpec((256,SLOT),lambda s,j:(s*J+j,0)),
                  pl.BlockSpec((1,8,SLOT),lambda s,j:(s*J+j,0,0)),HELD,
                  pl.BlockSpec((SLOT,D),lambda s,j:(s,0)),pl.BlockSpec((32,SLOT),lambda s,j:(0,s)),up,up],
        out_specs=[HELD,pl.BlockSpec((16,SLOT),lambda s,j:(0,s)),HELD,HELD],
        out_shape=[pltpu.VMEM((rows,3*D),BF),sd((16,rows),BF),pltpu.VMEM((16,D),F32),pltpu.VMEM((16,D),F32)],
        scratch_shapes=[pltpu.VMEM((16,SLOT),F32),pltpu.VMEM((32,D),F32)],
        compiler_params=params(LIM["attend_back"]),cost_estimate=takes(18),name="attend_back")(scalars,far(qkv),far(qkv),far(qkv),far(e),far(ot),rt,gmt,x,low,upq,upv)

def inputs_kernel(gfs_ref,d_ref,gl,w_ref,dnt_ref,out_ref):
    T=gfs_ref.shape[0]
    rows=pl.ds(pl.multiple_of(pl.program_id(0)*T,T),T)
    D=gfs_ref.shape[1]
    v=gfs_ref[...]+dg(gl[...],dnt_ref[...],0,0)
    for t in range(3): v=v+dg(d_ref[rows,t*D:(t+1)*D],w_ref[t],1,1)
    out_ref[...]=v

def inputs_grad(gfs,d,gl,w,dnt):
    rows,D=gfs.shape
    row=pl.BlockSpec((SLOT,D),lambda i:(i,0))
    return pl.pallas_call(inputs_kernel,grid=(rows//SLOT,),
        in_specs=[row,HELD,pl.BlockSpec((16,SLOT),lambda i:(0,i)),HELD,HELD],
        out_specs=row,out_shape=sd((rows,D),F32),
        compiler_params=params(LIM["inputs_grad"]),cost_estimate=takes(7),name="inputs_grad")(gfs,d,gl,w,dnt)


def device_count():
    return lax.axis_size("dp")*lax.axis_size("fsdp")

def permute(v,target):
    return lax.ppermute(v,AXES,[(i,target(i)) for i in range(device_count())])

def exchange(v,mask):
    return permute(v,lambda i:i^mask)

def along_z(block):
    top=device_count()//4
    return [block]+[exchange(block,top*m) for m in (1,2,3)]

def near_hop(v):
    return permute(v,lambda i:i^(4 if i%2 else 2))

def far_hop(v):
    return permute(v,lambda i:i^(2 if i%2 else 4))

def in_bands(bands,*blocks):
    return tuple(b.reshape(8,bands,-1,b.shape[2]) for b in blocks)

def core_pair(v):
    groups=[[2*i,2*i+1] for i in range(lax.axis_size("fsdp")//2)]
    return lax.all_gather(v,"fsdp",axis=0,tiled=False,axis_index_groups=groups)

def column_half(both):
    c=lax.axis_index("fsdp")%2
    half=both.shape[2]//2
    return lax.dynamic_slice_in_dim(both,c*half,half,axis=2).reshape(-1,half)

def total_over_devices(mine,other,meanwhile):
    n=device_count()
    mine=mine+exchange(other,1)
    got=[exchange(mine,m) for m in range(2,n//4,2)]
    for g in got: mine=mine+g
    got=[exchange(mine,m) for m in (n//4,n//2,3*n//4)]
    got,done=tie(got,meanwhile())
    for g in got: mine=mine+g
    return mine,exchange(mine,1),done

def finish_kernel(scale,sc_ref,mine_ref,other_ref,*outs):
    core=lax.rem(sc_ref[0],2)
    for c,halves in enumerate(((mine_ref,other_ref),(other_ref,mine_ref))):
        @pl.when(core==c)
        def _():
            for i,o in enumerate(outs): o[...]=halves[i//2][8*(i%2):8*(i%2)+8,:]*scale

def finish(scalars,mine,other,scale):
    D=mine.shape[1]
    return pl.pallas_call(functools.partial(finish_kernel,scale),in_specs=[SCALARS,HELD,HELD],out_specs=[HELD]*4,
        out_shape=[sd((8,D),F32)]*4,compiler_params=params(8),cost_estimate=takes(1),name="finish")(scalars,mine,other)

def tie(*v):
    return lax.optimization_barrier(v)

def by_hops(scalars,x,wq,wk,wv,wo,wi,wt,ag,ash,fg,fsh,qd,qu,vd,vu,go):
    D=wq.shape[1]; FF=wi.shape[1]; bands=FF//D; r=wq.shape[0]
    top=device_count()//4
    both=core_pair(jnp.concatenate([wq,wk,wv],0))
    s1=jnp.concatenate([column_half(both[:,r*t:r*t+r]) for t in range(3)],0)
    z1=along_z(s1)
    wo,wi,wt,qd,s1=tie(wo,wi,wt,qd,s1)
    bo,bi,bt=core_pair(wo),core_pair(wi),core_pair(wt)
    s2=jnp.concatenate([column_half(bo)]+[column_half(bi[:,:,D*t:D*t+D]) for t in range(bands)],0)
    s3=column_half(bt)
    dn,upq,upv,dnt,nm=prep(qd,qu,vd,vu,ag,ash,fg,fsh)
    n3=near_hop(s3)
    z1,s2,dn,scalars=tie(z1,s2,dn,scalars)
    a1=jnp.stack(z1,0)
    n1=near_hop(a1)
    z2=exchange(s2,2*top)
    b3=jnp.stack([s3,n3],0)
    y3=exchange(b3,top)
    n1,z2,s2,n3,dn=tie(n1,z2,s2,n3,dn)
    f1=jnp.concatenate([a1,n1],0)
    h1=far_hop(f1); of1=exchange(f1,1)
    e2=jnp.stack([s2,z2],0)
    y2=exchange(e2,top)
    m2=near_hop(e2)
    low,lq,lv=low_rank(x,dn,upq,upv)
    y2,y3,lq=tie(y2,y3,lq)
    n2=near_hop(y2)
    g3=jnp.stack([b3,y3],0)
    z3=exchange(g3,2*top)
    h1,of1=tie(h1,of1)
    oh1=exchange(h1,1)
    oh1,=tie(oh1)
    f2=jnp.stack([e2[0],y2[0],e2[1],y2[1],m2[0],n2[0],m2[1],n2[1]],0)
    h2=far_hop(f2); of2=exchange(f2,1)
    qkv,wqkv=project(scalars,x,lq,lv,in_bands(3,f1,h1,of1,oh1))
    e,ot,o,rt=attend(scalars,qkv,x.shape[0]//SLOT)
    h2,o,of2,z3=tie(h2,o,of2,z3)
    oh2=exchange(h2,1)
    f3=jnp.concatenate([g3,z3],0).swapaxes(0,1).reshape(8,-1,D//2)
    h3=far_hop(f3); of3=exchange(f3,1)
    oh2,=tie(oh2)
    nn,r1,act,gp,w=feed_in(scalars,x,o,nm,in_bands(1+bands,f2,h2,of2,oh2),FF)
    h3,nn,of3=tie(h3,nn,of3)
    oh3=exchange(h3,1)
    out,gfs,gmt=feed_out(scalars,nn,r1,act,gp,go,w,nm,in_bands(1,f3,h3,of3,oh3))
    return qkv,low,wqkv,e,ot,rt,out,gfs,gmt,upq,upv,dnt

def by_all_gather(scalars,x,wq,wk,wv,wo,wi,wt,ag,ash,fg,fsh,qd,qu,vd,vu,go):
    wq,wk,wv,wo,wi,wt=(lax.all_gather(w,AXES,axis=0,tiled=True) for w in (wq,wk,wv,wo,wi,wt))
    D=wq.shape[1]; FF=wi.shape[1]
    dn,upq,upv,dnt,nm=prep(qd,qu,vd,vu,ag,ash,fg,fsh)
    low,lq,lv=low_rank(x,dn,upq,upv)
    qkv,wqkv=project(scalars,x,lq,lv,(jnp.stack([wq,wk,wv],0),))
    e,ot,o,rt=attend(scalars,qkv,x.shape[0]//SLOT)
    nn,r1,act,gp,w=feed_in(scalars,x,o,nm,(jnp.stack([wo]+[wi[:,c:c+D] for c in range(0,FF,D)],0),),FF)
    out,gfs,gmt=feed_out(scalars,nn,r1,act,gp,go,w,nm,(wt[None],))
    return qkv,low,wqkv,e,ot,rt,out,gfs,gmt,upq,upv,dnt

def shards(x,lengths,wq,wk,wv,wo,wi,wt,ag,ash,fg,fsh,qd,qu,vd,vu,go):
    n=device_count()
    valid=lengths[:,0]+lengths[:,1]+4
    me=(lax.axis_index("dp")*lax.axis_size("fsdp")+lax.axis_index("fsdp")).reshape(1)
    scalars=jnp.concatenate([me,valid]).astype(jnp.int32)
    forward=by_hops if n==32 and wq.shape[0]%8==0 else by_all_gather
    qkv,low,wqkv,e,ot,rt,out,gfs,gmt,upq,upv,dnt=forward(scalars,x,wq,wk,wv,wo,wi,wt,ag,ash,fg,fsh,qd,qu,vd,vu,go)
    d,gl,mine,other=attend_back(scalars,qkv,e,ot,rt,gmt,x,low,upq,upv)
    mine,other,gx=total_over_devices(mine,other,lambda: inputs_grad(gfs,d,gl,wqkv,dnt))
    qd,vd,qu,vu=finish(scalars,mine,other,1.0/(lengths.shape[0]*n))
    return out,gx,qd.T,qu,vd.T,vu

def solution(mesh):
    sp=P(AXES,None)
    return jax.shard_map(shards,mesh=mesh,in_specs=(sp,)*8+(P(),)*8+(sp,),
        out_specs=(sp,sp,P(),P(),P(),P()),check_vma=False)
```

```python
import functools
import jax
import jax.numpy as jnp
from jax import lax
from jax.experimental import pallas as pl
from jax.experimental.pallas import tpu as pltpu
from jax.sharding import PartitionSpec as P

HEAD_DIM=64; SLOT=512
F32=jnp.float32; BF=jnp.bfloat16
MIB=1024*1024
AXES=("dp","fsdp")
sd=jax.ShapeDtypeStruct
ANY=pl.BlockSpec(memory_space=pl.ANY)
HELD=pl.BlockSpec(memory_space=pltpu.VMEM)
SCALARS=pl.BlockSpec(memory_space=pltpu.SMEM)


def params(mib=56):
    return pltpu.CompilerParams(vmem_limit_bytes=mib*MIB)

def takes(us):
    return pl.CostEstimate(flops=int(us*1.1e9),bytes_accessed=0,transcendentals=0)


def dg(a,b,ca,cb):
    return lax.dot_general(a,b,(((ca,),(cb,)),((),())),preferred_element_type=F32)

def far(v):
    return pltpu.with_memory_space_constraint(v,pltpu.HBM)


def block_copies(me,bufs,to,sems):
    if len(bufs)==1:
        return [pltpu.make_async_copy(bufs[0],to,sems.at[0])]
    chip=lax.div(me,2); core=lax.rem(me,2)
    copies=[]
    for which,buf in enumerate(bufs):
        origin=core if which<2 else 1-core
        _,_,rows,half=buf.shape
        for i in range(8):
            dst=lax.bitwise_xor(chip,(which%2)*(2-origin)+(i//4)*(1+origin)+4*(i%4))
            at=to.at[:,pl.ds(pl.multiple_of(dst*rows,16),rows),pl.ds(pl.multiple_of(origin*half,128),half)]
            copies.append(pltpu.make_async_copy(buf.at[i],at,sems.at[len(copies)]))
    return copies

def start_all(copies):
    for c in copies: c.start()

def wait_all(copies):
    for c in copies: c.wait()

BLOCK_COPIES=32

def prep_kernel(qdt_ref,vdt_ref,qu_ref,vu_ref,ag_ref,ash_ref,fg_ref,fsh_ref,dn_ref,upq_ref,upv_ref,dnt_ref,nm_ref):
    D=qu_ref.shape[1]
    both=jnp.concatenate([qdt_ref[...],vdt_ref[...]],axis=0)
    dnt_ref[...]=both.astype(BF)
    dn_ref[...]=jnp.concatenate([both,jnp.zeros((112,D),F32)],axis=0).T.astype(BF)
    z8=jnp.zeros((8,D),F32); z=jnp.zeros((112,D),F32)
    upq_ref[...]=jnp.concatenate([qu_ref[...],z8,z],axis=0).astype(BF)
    upv_ref[...]=jnp.concatenate([z8,vu_ref[...],z],axis=0).astype(BF)
    for i,r in enumerate((ag_ref,ash_ref,fg_ref,fsh_ref)):
        nm_ref[i:i+1,:]=r[...].astype(F32)
    nm_ref[4:8,:]=jnp.zeros((4,D),F32)

def prep(qd,qu,vd,vu,ag,ash,fg,fsh):
    D=qu.shape[1]
    return pl.pallas_call(prep_kernel,out_shape=[sd((D,128),BF),sd((128,D),BF),sd((128,D),BF),sd((16,D),BF),sd((8,D),F32)],
        compiler_params=params(8),cost_estimate=takes(1),name="prep")(qd.T,vd.T,qu,vu,*(v.reshape(1,D) for v in (ag,ash,fg,fsh)))


def low_kernel(x_ref,dn_ref,upq_ref,upv_ref,low_ref,lq_ref,lv_ref):
    for s in range(x_ref.shape[0]//SLOT):
        r=slice(s*SLOT,(s+1)*SLOT)
        low=dg(x_ref[r,:],dn_ref[...],1,0).astype(BF)
        low_ref[:,r]=low.T[:32]
        lq_ref[r,:]=2.0*dg(low,upq_ref[...],1,0)
        lv_ref[r,:]=2.0*dg(low,upv_ref[...],1,0)

def low_rank(x,dn,upq,upv):
    rows,D=x.shape
    return pl.pallas_call(low_kernel,in_specs=[HELD]*4,out_specs=[HELD]*3,
        out_shape=[sd((32,rows),BF),pltpu.VMEM((rows,D),F32),pltpu.VMEM((rows,D),F32)],
        compiler_params=params(LIM["low_rank"]),cost_estimate=takes(3),name="low_rank")(x,dn,upq,upv)

def project_kernel(sc_ref,x_ref,lq_ref,lv_ref,*rest):
    *blocks,qkv_ref,wo,w,sems,osem=rest
    rows,D=x_ref.shape
    copies=block_copies(sc_ref[0],blocks,w,sems)
    start_all(copies)
    wait_all(copies)
    whole=[pltpu.make_async_copy(w,wo,osem.at[0])]
    start_all(whole)
    for t,up in enumerate((lq_ref,None,lv_ref)):
        for s in range(rows//SLOT):
            r=slice(s*SLOT,(s+1)*SLOT)
            v=dg(x_ref[r,:],w[t],1,0)
            if up is not None: v=v+up[r,:]
            qkv_ref[r,t*D:(t+1)*D]=v.astype(BF)
    wait_all(whole)

def project(scalars,x,lq,lv,blocks):
    rows,D=x.shape
    return pl.pallas_call(project_kernel,
        in_specs=[SCALARS,HELD,HELD,HELD]+[ANY]*len(blocks),
        out_specs=[HELD,ANY],
        out_shape=[pltpu.VMEM((rows,3*D),BF),pltpu.HBM((3,D,D),BF)],
        scratch_shapes=[pltpu.VMEM((3,D,D),BF),pltpu.SemaphoreType.DMA((BLOCK_COPIES,)),pltpu.SemaphoreType.DMA((1,))],
        compiler_params=params(LIM["project"]),cost_estimate=takes(8),name="project")(scalars,x,lq,lv,*blocks)

def attend_kernel(sc_ref,qkv_ref,e_ref,ot_ref,o_ref,rt_ref):
    s=pl.program_id(0); j=pl.program_id(1); J=pl.num_programs(1); D=256*J
    lane=lax.broadcasted_iota(jnp.int32,(SLOT,128),1)
    row=lax.broadcasted_iota(jnp.int32,(SLOT,128),0)
    bias=jnp.where(row<sc_ref[1+s],0.0,-1e30).astype(F32)
    rows=pl.ds(pl.multiple_of(s*SLOT,SLOT),SLOT)
    def part(which,p):
        return qkv_ref[rows,pl.ds(pl.multiple_of(which*D+256*j+128*p,128),128)].astype(F32)
    heads=[]
    for p in range(2):
        qp,kp,vp=part(0,p)*0.125,part(1,p),part(2,p)
        for h in range(2):
            own=(lane<64) if h==0 else (lane>=64)
            aux=64 if h==0 else 0
            one=jnp.where(lane==aux,1.0,0.0)
            heads.append((64*h,aux,jnp.where(own,qp,one).astype(BF),
                          jnp.where(own,kp,jnp.where(lane==aux,bias,0.0)).astype(BF),jnp.where(own,vp,one).astype(BF)))
    totals=[]; os=[]
    def weights(n,st):
        e_ref[n]=jnp.exp(st-jnp.max(st,axis=0,keepdims=True)).astype(BF)
    def mix(n):
        lo,aux,_,_,vm=heads[n]
        ot=dg(vm,e_ref[n],0,0)
        r=1.0/ot[aux:aux+1]
        totals.append(r)
        os.append((ot[lo:lo+64]*r).astype(BF))
    before=None
    for n in range(4):
        st=dg(heads[n][3],heads[n][2],1,1)
        if before is not None:
            weights(n-1,before)
            if n>1: mix(n-2)
        before=st
    weights(3,before)
    mix(2); mix(3)
    ot=jnp.concatenate(os,axis=0)
    ot_ref[...]=ot
    o_ref[rows,pl.ds(pl.multiple_of(256*j,256),256)]=ot.T
    rt_ref[0]=jnp.concatenate(totals+totals,axis=0)

def attend(scalars,qkv,slots):
    rows=qkv.shape[0]; D=qkv.shape[1]//3; J=D//256; H=D//HEAD_DIM
    return pl.pallas_call(attend_kernel,grid=(slots,J),
        in_specs=[SCALARS,HELD],
        out_specs=[pl.BlockSpec((4,SLOT,SLOT),lambda s,j:(s*J+j,0,0)),pl.BlockSpec((256,SLOT),lambda s,j:(s*J+j,0)),HELD,pl.BlockSpec((1,8,SLOT),lambda s,j:(s*J+j,0,0))],
        out_shape=[pltpu.HBM((slots*H,SLOT,SLOT),BF),pltpu.HBM((slots*D,SLOT),BF),pltpu.VMEM((rows,D),BF),pltpu.HBM((slots*J,8,SLOT),F32)],
        compiler_params=params(LIM["attend"]),cost_estimate=takes(16),name="attend")(scalars,qkv)


def norm_stats(value):
    mean=jnp.mean(value,axis=-1,keepdims=True)
    c=value-mean
    r=lax.rsqrt(jnp.mean(c*c,axis=-1,keepdims=True)+1e-5)
    return c*r,r

def norm_back(g,n,r):
    return r*(g-jnp.mean(g,axis=-1,keepdims=True)-n*jnp.mean(g*n,axis=-1,keepdims=True))

def gelu_pair(v):
    cdf=0.5+0.5*lax.erf(v*0.7071067811865476)
    return v*cdf, cdf+(0.3989422804014327*v)*jnp.exp(-0.5*v*v)

CH=256
LIM={"project":10,"attend":12,"feed_in":8,"feed_out":18,"attend_back":12,"inputs_grad":10,"low_rank":10}

def feed_in_kernel(sc_ref,x_ref,o_ref,nm_ref,*rest):
    *blocks,n1_ref,r1_ref,act_ref,gp_ref,w,sems=rest
    D=x_ref.shape[1]
    copies=block_copies(sc_ref[0],blocks,w,sems)
    start_all(copies); wait_all(copies)
    parts=[]
    for s in range(x_ref.shape[0]//SLOT):
        rows=slice(s*SLOT,(s+1)*SLOT)
        first=x_ref[rows,:].astype(F32)+dg(o_ref[rows,:],w[0],1,0)
        n1,r1=norm_stats(first)
        n1_ref[rows,:]=n1; r1_ref[rows,:]=jnp.broadcast_to(r1,(SLOT,128))
        parts.append((rows,(n1*nm_ref[0:1,:]+nm_ref[1:2,:]).astype(BF)))
    for c in range(0,act_ref.shape[1],CH):
        for rows,hb in parts:
            act,gp=gelu_pair(dg(hb,w[1+c//D,:,c%D:c%D+CH],1,0))
            act_ref[rows,c:c+CH]=act.astype(BF)
            gp_ref[rows,c:c+CH]=gp.astype(BF)

def feed_in(scalars,x,o,nm,blocks,FF):
    rows,D=x.shape
    return pl.pallas_call(feed_in_kernel,
        in_specs=[SCALARS,HELD,HELD,HELD]+[ANY]*len(blocks),
        out_specs=[HELD]*5,
        out_shape=[pltpu.VMEM((rows,D),F32),pltpu.VMEM((rows,128),F32),pltpu.VMEM((rows,FF),BF),pltpu.VMEM((rows,FF),BF),pltpu.VMEM((1+FF//D,D,D),BF)],
        scratch_shapes=[pltpu.SemaphoreType.DMA((BLOCK_COPIES,))],
        compiler_params=params(LIM["feed_in"]),cost_estimate=takes(14),name="feed_in")(scalars,x,o,nm,*blocks)

def feed_out_kernel(sc_ref,n1_ref,r1_ref,act_ref,gp_ref,go_ref,nm_ref,w,*rest):
    *blocks,out_ref,gfs_ref,gmt_ref,gi_ref,wt,held,sems,osems=rest
    copies=block_copies(sc_ref[0],blocks,wt,sems)
    start_all(copies); wait_all(copies)
    rows,D=go_ref.shape; FF=gi_ref.shape[1]
    ag,ash,fg,fsh=(nm_ref[i:i+1,:] for i in range(4))
    part=[slice(s*SLOT,(s+1)*SLOT) for s in range(rows//SLOT)]
    acc={}; g2={}; g1={}
    outs=[pltpu.make_async_copy(held.at[pl.ds(s*SLOT,SLOT),:],out_ref.at[pl.ds(s*SLOT,SLOT),:],osems.at[s]) for s in range(len(part))]
    def second_sum(s):
        acc[s]=n1_ref[part[s],:]*ag+ash+dg(act_ref[part[s],:],wt[0],1,0)
    def second_norm(s):
        n2,r2=norm_stats(acc[s])
        held[part[s],:]=(n2*fg+fsh).astype(BF)
        g2[s]=norm_back(go_ref[part[s],:].astype(F32)*fg,n2,r2)
    def inner_grad(s):
        g=g2[s].astype(BF)
        for c in range(0,FF,CH):
            ga=dg(g,wt[0,c:c+CH,:],1,1)
            gi_ref[part[s],c:c+CH]=(ga*gp_ref[part[s],c:c+CH].astype(F32)).astype(BF)
    def first_grad(s):
        v=g2[s]
        for b in range(FF//D): v=v+dg(gi_ref[part[s],b*D:(b+1)*D],w[1+b],1,1)
        acc[s]=v
    def first_norm(s):
        g=norm_back(acc[s]*ag,n1_ref[part[s],:],r1_ref[part[s],0:1])
        gfs_ref[part[s],:]=g
        g1[s]=g.astype(BF)
    def mixed_grad(s):
        gmt_ref[:,part[s]]=dg(w[0],g1[s],1,1).astype(BF)
    stages=(second_sum,second_norm,inner_grad,first_grad,first_norm,mixed_grad)
    order=sorted((2*k+(3*s if k else 0),s,k) for s in range(len(part)) for k in range(len(stages)))
    for _,s,k in order:
        stages[k](s)
    start_all(outs); wait_all(outs)

def feed_out(scalars,n1,r1,act,gp,go,w,nm,blocks):
    rows,D=n1.shape; FF=act.shape[1]
    return pl.pallas_call(feed_out_kernel,
        in_specs=[SCALARS]+[HELD]*7+[ANY]*len(blocks),
        out_specs=[ANY,HELD,HELD,HELD],
        out_shape=[sd((rows,D),BF),pltpu.VMEM((rows,D),F32),pltpu.VMEM((D,rows),BF),pltpu.VMEM((rows,FF),BF)],
        input_output_aliases={3:3},
        scratch_shapes=[pltpu.VMEM((1,FF,D),BF),pltpu.VMEM((rows,D),BF),
                        pltpu.SemaphoreType.DMA((BLOCK_COPIES,)),pltpu.SemaphoreType.DMA((rows//SLOT,))],
        compiler_params=params(LIM["feed_out"]),cost_estimate=takes(24),name="feed_out")(scalars,n1,r1,act,gp,go,nm,w,*blocks)[:3]


def attend_back_kernel(sc_ref,q_ref,k_ref,v_ref,e_ref,ot_ref,rt_ref,gmt_ref,x_ref,low_ref,upq_ref,upv_ref,
                       d_ref,gl_ref,mine_ref,other_ref,glacc,ad_ref):
    s=pl.program_id(0); j=pl.program_id(1); J=pl.num_programs(1)
    lane=lax.broadcasted_iota(jnp.int32,(SLOT,128),1)
    rowi=lax.broadcasted_iota(jnp.int32,(128,SLOT),0)
    D=256*J
    rows=pl.ds(pl.multiple_of(s*SLOT,SLOT),SLOT)
    def place_of(which,p):
        return rows,pl.ds(pl.multiple_of(which*D+256*j+128*p,128),128)
    gmq=gmt_ref[pl.ds(pl.multiple_of(256*j,256),256),rows]
    otq=ot_ref[...]
    dqts=[]; dvs=[]
    for p in range(2):
        cols=slice(128*p,128*p+128)
        qp,kp,vp=(w[:,cols].astype(F32) for w in (q_ref,k_ref,v_ref))
        qp=qp*0.125; kp=kp*0.125
        gm=gmq[cols,:].astype(F32); om=otq[cols,:].astype(F32)
        pr=gm*om
        dkp=None; dvp=None; dqt=None
        for h in range(2):
            own=(lane<64) if h==0 else (lane>=64)
            ownr=(rowi<64) if h==0 else (rowi>=64)
            aux=64 if h==0 else 0
            r=rt_ref[0,2*p+h:2*p+h+1,:]
            d=-jnp.sum(pr[64*h:64*h+64],axis=0,keepdims=True)*r
            dhi=d.astype(BF).astype(F32)
            dlo=d-dhi
            gs=gm*r
            gaug=jnp.where(ownr,gs,jnp.where(rowi==aux,dhi,jnp.where(rowi==aux+1,dlo,0.0))).astype(BF)
            gown=jnp.where(ownr,gs,0.0).astype(BF)
            vm=jnp.where(own,vp,jnp.where((lane==aux)|(lane==aux+1),1.0,0.0)).astype(BF)
            e=e_ref[2*p+h]
            ds=(dg(vm,gaug,1,0)*e.astype(F32)).astype(BF)
            qm=jnp.where(own,qp,0.0).astype(BF)
            km=jnp.where(own,kp,0.0).astype(BF)
            dv=dg(e,gown,1,1)
            dk=dg(ds,qm,1,0)
            dq=dg(km,ds,0,0)
            dvp=dv if dvp is None else dvp+dv
            dkp=dk if dkp is None else dkp+dk
            dqt=dq if dqt is None else dqt+dq
        d_ref[place_of(1,p)]=dkp.astype(BF)
        dvs.append(dvp.astype(BF))
        d_ref[place_of(2,p)]=dvs[p]
        dqts.append(dqt.astype(BF))
    dqt=jnp.concatenate(dqts,axis=0)
    dqb=dqt.T
    d_ref[rows,pl.ds(pl.multiple_of(256*j,256),256)]=dqb
    dvb=jnp.concatenate(dvs,axis=1)
    glq=dg(upq_ref[...],dqt,1,0)
    glv=dg(upv_ref[...],dvb,1,1)
    part=2.0*(glq+glv)
    @pl.when(j==0)
    def _(): glacc[...]=part
    @pl.when(j>0)
    def _(): glacc[...]+=part
    low=low_ref[...]
    c0=pl.multiple_of(j*256,256)
    upq=2.0*dg(low[:16],dqb,1,0)
    upv=2.0*dg(low[:16],dvb,1,0)
    upg=jnp.concatenate([upq[0:8],upv[8:16]],axis=0)
    def add(rows,cols,v):
        @pl.when(s==0)
        def _(): ad_ref[rows,cols]=v
        @pl.when(s>0)
        def _(): ad_ref[rows,cols]+=v
    add(slice(16,32),pl.ds(c0,256),upg)
    @pl.when(j==J-1)
    def _():
        gl=glacc[...].astype(BF)
        gl_ref[...]=gl
        add(slice(0,16),slice(None),dg(gl,x_ref[...],1,0))
        core=lax.rem(sc_ref[0],2)
        for c,(a,b) in enumerate(((mine_ref,other_ref),(other_ref,mine_ref))):
            @pl.when((s==pl.num_programs(0)-1)&(core==c))
            def _():
                a[...]=ad_ref[0:16,:]
                b[...]=ad_ref[16:32,:]

def attend_back(scalars,qkv,e,ot,rt,gmt,x,low,upq,upv):
    rows,D=x.shape; J=D//256; S=rows//SLOT
    up=pl.BlockSpec((16,256),lambda s,j:(0,j))
    return pl.pallas_call(attend_back_kernel,grid=(S,J),
        in_specs=[SCALARS,*[pl.BlockSpec((SLOT,256),lambda s,j,w=w:(s,w*J+j)) for w in range(3)],
                  pl.BlockSpec((4,SLOT,SLOT),lambda s,j:(s*J+j,0,0)),pl.BlockSpec((256,SLOT),lambda s,j:(s*J+j,0)),
                  pl.BlockSpec((1,8,SLOT),lambda s,j:(s*J+j,0,0)),HELD,
                  pl.BlockSpec((SLOT,D),lambda s,j:(s,0)),pl.BlockSpec((32,SLOT),lambda s,j:(0,s)),up,up],
        out_specs=[HELD,pl.BlockSpec((16,SLOT),lambda s,j:(0,s)),HELD,HELD],
        out_shape=[pltpu.VMEM((rows,3*D),BF),sd((16,rows),BF),pltpu.VMEM((16,D),F32),pltpu.VMEM((16,D),F32)],
        scratch_shapes=[pltpu.VMEM((16,SLOT),F32),pltpu.VMEM((32,D),F32)],
        compiler_params=params(LIM["attend_back"]),cost_estimate=takes(18),name="attend_back")(scalars,far(qkv),far(qkv),far(qkv),far(e),far(ot),rt,gmt,x,low,upq,upv)

def inputs_kernel(gfs_ref,d_ref,gl,w_ref,dnt_ref,out_ref):
    T=gfs_ref.shape[0]
    rows=pl.ds(pl.multiple_of(pl.program_id(0)*T,T),T)
    D=gfs_ref.shape[1]
    v=gfs_ref[...]+dg(gl[...],dnt_ref[...],0,0)
    for t in range(3): v=v+dg(d_ref[rows,t*D:(t+1)*D],w_ref[t],1,1)
    out_ref[...]=v

def inputs_grad(gfs,d,gl,w,dnt):
    rows,D=gfs.shape
    row=pl.BlockSpec((SLOT,D),lambda i:(i,0))
    return pl.pallas_call(inputs_kernel,grid=(rows//SLOT,),
        in_specs=[row,HELD,pl.BlockSpec((16,SLOT),lambda i:(0,i)),HELD,HELD],
        out_specs=row,out_shape=sd((rows,D),F32),
        compiler_params=params(LIM["inputs_grad"]),cost_estimate=takes(7),name="inputs_grad")(gfs,d,gl,w,dnt)


def device_count():
    return lax.axis_size("dp")*lax.axis_size("fsdp")

def permute(v,target):
    return lax.ppermute(v,AXES,[(i,target(i)) for i in range(device_count())])

def exchange(v,mask):
    return permute(v,lambda i:i^mask)

def along_z(block):
    top=device_count()//4
    return [block]+[exchange(block,top*m) for m in (1,2,3)]

def near_hop(v):
    return permute(v,lambda i:i^(4 if i%2 else 2))

def far_hop(v):
    return permute(v,lambda i:i^(2 if i%2 else 4))

def in_bands(bands,*blocks):
    return tuple(b.reshape(8,bands,-1,b.shape[2]) for b in blocks)

def core_pair(v):
    groups=[[2*i,2*i+1] for i in range(lax.axis_size("fsdp")//2)]
    return lax.all_gather(v,"fsdp",axis=0,tiled=False,axis_index_groups=groups)

def column_half(both):
    c=lax.axis_index("fsdp")%2
    half=both.shape[2]//2
    return lax.dynamic_slice_in_dim(both,c*half,half,axis=2).reshape(-1,half)

def total_over_devices(mine,other,meanwhile):
    n=device_count()
    mine=mine+exchange(other,1)
    got=[exchange(mine,m) for m in range(2,n//4,2)]
    for g in got: mine=mine+g
    got=[exchange(mine,m) for m in (n//4,n//2,3*n//4)]
    got,done=tie(got,meanwhile())
    for g in got: mine=mine+g
    return mine,exchange(mine,1),done

def finish_kernel(scale,sc_ref,mine_ref,other_ref,*outs):
    core=lax.rem(sc_ref[0],2)
    for c,halves in enumerate(((mine_ref,other_ref),(other_ref,mine_ref))):
        @pl.when(core==c)
        def _():
            for i,o in enumerate(outs): o[...]=halves[i//2][8*(i%2):8*(i%2)+8,:]*scale

def finish(scalars,mine,other,scale):
    D=mine.shape[1]
    return pl.pallas_call(functools.partial(finish_kernel,scale),in_specs=[SCALARS,HELD,HELD],out_specs=[HELD]*4,
        out_shape=[sd((8,D),F32)]*4,compiler_params=params(8),cost_estimate=takes(1),name="finish")(scalars,mine,other)

def tie(*v):
    return lax.optimization_barrier(v)

def by_hops(scalars,x,wq,wk,wv,wo,wi,wt,ag,ash,fg,fsh,qd,qu,vd,vu,go):
    D=wq.shape[1]; FF=wi.shape[1]; bands=FF//D; r=wq.shape[0]
    top=device_count()//4
    both=core_pair(jnp.concatenate([wq,wk,wv],0))
    s1=jnp.concatenate([column_half(both[:,r*t:r*t+r]) for t in range(3)],0)
    z1=along_z(s1)
    wo,wi,wt,qd,s1=tie(wo,wi,wt,qd,s1)
    bo,bi,bt=core_pair(wo),core_pair(wi),core_pair(wt)
    s2=jnp.concatenate([column_half(bo)]+[column_half(bi[:,:,D*t:D*t+D]) for t in range(bands)],0)
    s3=column_half(bt)
    dn,upq,upv,dnt,nm=prep(qd,qu,vd,vu,ag,ash,fg,fsh)
    n3=near_hop(s3)
    z1,s2,dn,scalars=tie(z1,s2,dn,scalars)
    a1=jnp.stack(z1,0)
    n1=near_hop(a1)
    z2=exchange(s2,2*top)
    b3=jnp.stack([s3,n3],0)
    y3=exchange(b3,top)
    n1,z2,s2,n3,dn=tie(n1,z2,s2,n3,dn)
    f1=jnp.concatenate([a1,n1],0)
    h1=far_hop(f1); of1=exchange(f1,1)
    e2=jnp.stack([s2,z2],0)
    y2=exchange(e2,top)
    m2=near_hop(e2)
    low,lq,lv=low_rank(x,dn,upq,upv)
    y2,y3,lq=tie(y2,y3,lq)
    n2=near_hop(y2)
    g3=jnp.stack([b3,y3],0)
    z3=exchange(g3,2*top)
    h1,of1=tie(h1,of1)
    oh1=exchange(h1,1)
    oh1,=tie(oh1)
    f2=jnp.stack([e2[0],y2[0],e2[1],y2[1],m2[0],n2[0],m2[1],n2[1]],0)
    h2=far_hop(f2); of2=exchange(f2,1)
    qkv,wqkv=project(scalars,x,lq,lv,in_bands(3,f1,h1,of1,oh1))
    e,ot,o,rt=attend(scalars,qkv,x.shape[0]//SLOT)
    h2,o,of2,z3=tie(h2,o,of2,z3)
    oh2=exchange(h2,1)
    f3=jnp.concatenate([g3,z3],0).swapaxes(0,1).reshape(8,-1,D//2)
    h3=far_hop(f3); of3=exchange(f3,1)
    oh2,=tie(oh2)
    nn,r1,act,gp,w=feed_in(scalars,x,o,nm,in_bands(1+bands,f2,h2,of2,oh2),FF)
    h3,nn,of3=tie(h3,nn,of3)
    oh3=exchange(h3,1)
    out,gfs,gmt=feed_out(scalars,nn,r1,act,gp,go,w,nm,in_bands(1,f3,h3,of3,oh3))
    return qkv,low,wqkv,e,ot,rt,out,gfs,gmt,upq,upv,dnt

def by_all_gather(scalars,x,wq,wk,wv,wo,wi,wt,ag,ash,fg,fsh,qd,qu,vd,vu,go):
    wq,wk,wv,wo,wi,wt=(lax.all_gather(w,AXES,axis=0,tiled=True) for w in (wq,wk,wv,wo,wi,wt))
    D=wq.shape[1]; FF=wi.shape[1]
    dn,upq,upv,dnt,nm=prep(qd,qu,vd,vu,ag,ash,fg,fsh)
    low,lq,lv=low_rank(x,dn,upq,upv)
    qkv,wqkv=project(scalars,x,lq,lv,(jnp.stack([wq,wk,wv],0),))
    e,ot,o,rt=attend(scalars,qkv,x.shape[0]//SLOT)
    nn,r1,act,gp,w=feed_in(scalars,x,o,nm,(jnp.stack([wo]+[wi[:,c:c+D] for c in range(0,FF,D)],0),),FF)
    out,gfs,gmt=feed_out(scalars,nn,r1,act,gp,go,w,nm,(wt[None],))
    return qkv,low,wqkv,e,ot,rt,out,gfs,gmt,upq,upv,dnt

def shards(x,lengths,wq,wk,wv,wo,wi,wt,ag,ash,fg,fsh,qd,qu,vd,vu,go):
    n=device_count()
    valid=lengths[:,0]+lengths[:,1]+4
    me=(lax.axis_index("dp")*lax.axis_size("fsdp")+lax.axis_index("fsdp")).reshape(1)
    scalars=jnp.concatenate([me,valid]).astype(jnp.int32)
    forward=by_hops if n==32 and wq.shape[0]%8==0 else by_all_gather
    qkv,low,wqkv,e,ot,rt,out,gfs,gmt,upq,upv,dnt=forward(scalars,x,wq,wk,wv,wo,wi,wt,ag,ash,fg,fsh,qd,qu,vd,vu,go)
    d,gl,mine,other=attend_back(scalars,qkv,e,ot,rt,gmt,x,low,upq,upv)
    mine,other,gx=total_over_devices(mine,other,lambda: inputs_grad(gfs,d,gl,wqkv,dnt))
    qd,vd,qu,vu=finish(scalars,mine,other,1.0/(lengths.shape[0]*n))
    return out,gx,qd.T,qu,vd.T,vu

def solution(mesh):
    sp=P(AXES,None)
    return jax.shard_map(shards,mesh=mesh,in_specs=(sp,)*8+(P(),)*8+(sp,),
        out_specs=(sp,sp,P(),P(),P(),P()),check_vma=False)
```

```python
import functools
import jax
import jax.numpy as jnp
from jax import lax
from jax.experimental import pallas as pl
from jax.experimental.pallas import tpu as pltpu
from jax.sharding import PartitionSpec as P

HEAD_DIM=64; SLOT=512
F32=jnp.float32; BF=jnp.bfloat16
MIB=1024*1024
AXES=("dp","fsdp")
sd=jax.ShapeDtypeStruct
ANY=pl.BlockSpec(memory_space=pl.ANY)
HELD=pl.BlockSpec(memory_space=pltpu.VMEM)
SCALARS=pl.BlockSpec(memory_space=pltpu.SMEM)


def params(mib=56):
    return pltpu.CompilerParams(vmem_limit_bytes=mib*MIB)

def takes(us):
    return pl.CostEstimate(flops=int(us*1.1e9),bytes_accessed=0,transcendentals=0)


def dg(a,b,ca,cb):
    return lax.dot_general(a,b,(((ca,),(cb,)),((),())),preferred_element_type=F32)

def far(v):
    return pltpu.with_memory_space_constraint(v,pltpu.HBM)


def block_copies(me,bufs,to,sems):
    if len(bufs)==1:
        return [pltpu.make_async_copy(bufs[0],to,sems.at[0])]
    chip=lax.div(me,2); core=lax.rem(me,2)
    copies=[]
    for which,buf in enumerate(bufs):
        origin=core if which<2 else 1-core
        _,_,rows,half=buf.shape
        for i in range(8):
            dst=lax.bitwise_xor(chip,(which%2)*(2-origin)+(i//4)*(1+origin)+4*(i%4))
            at=to.at[:,pl.ds(pl.multiple_of(dst*rows,16),rows),pl.ds(pl.multiple_of(origin*half,128),half)]
            copies.append(pltpu.make_async_copy(buf.at[i],at,sems.at[len(copies)]))
    return copies

def start_all(copies):
    for c in copies: c.start()

def wait_all(copies):
    for c in copies: c.wait()

BLOCK_COPIES=32

def prep_kernel(qdt_ref,vdt_ref,qu_ref,vu_ref,ag_ref,ash_ref,fg_ref,fsh_ref,dn_ref,upq_ref,upv_ref,dnt_ref,nm_ref):
    D=qu_ref.shape[1]
    both=jnp.concatenate([qdt_ref[...],vdt_ref[...]],axis=0)
    dnt_ref[...]=both.astype(BF)
    dn_ref[...]=jnp.concatenate([both,jnp.zeros((112,D),F32)],axis=0).T.astype(BF)
    z8=jnp.zeros((8,D),F32); z=jnp.zeros((112,D),F32)
    upq_ref[...]=jnp.concatenate([qu_ref[...],z8,z],axis=0).astype(BF)
    upv_ref[...]=jnp.concatenate([z8,vu_ref[...],z],axis=0).astype(BF)
    for i,r in enumerate((ag_ref,ash_ref,fg_ref,fsh_ref)):
        nm_ref[i:i+1,:]=r[...].astype(F32)
    nm_ref[4:8,:]=jnp.zeros((4,D),F32)

def prep(qd,qu,vd,vu,ag,ash,fg,fsh):
    D=qu.shape[1]
    return pl.pallas_call(prep_kernel,out_shape=[sd((D,128),BF),sd((128,D),BF),sd((128,D),BF),sd((16,D),BF),sd((8,D),F32)],
        compiler_params=params(8),cost_estimate=takes(1),name="prep")(qd.T,vd.T,qu,vu,*(v.reshape(1,D) for v in (ag,ash,fg,fsh)))


def low_kernel(x_ref,dn_ref,upq_ref,upv_ref,low_ref,lq_ref,lv_ref):
    for s in range(x_ref.shape[0]//SLOT):
        r=slice(s*SLOT,(s+1)*SLOT)
        low=dg(x_ref[r,:],dn_ref[...],1,0).astype(BF)
        low_ref[:,r]=low.T[:32]
        lq_ref[r,:]=2.0*dg(low,upq_ref[...],1,0)
        lv_ref[r,:]=2.0*dg(low,upv_ref[...],1,0)

def low_rank(x,dn,upq,upv):
    rows,D=x.shape
    return pl.pallas_call(low_kernel,in_specs=[HELD]*4,out_specs=[HELD]*3,
        out_shape=[sd((32,rows),BF),pltpu.VMEM((rows,D),F32),pltpu.VMEM((rows,D),F32)],
        compiler_params=params(LIM["low_rank"]),cost_estimate=takes(3),name="low_rank")(x,dn,upq,upv)

def project_kernel(sc_ref,x_ref,lq_ref,lv_ref,*rest):
    *blocks,qkv_ref,wo,w,sems,osem=rest
    i=pl.program_id(0); D=x_ref.shape[1]
    whole=[pltpu.make_async_copy(w,wo,osem.at[0])]
    @pl.when(i==0)
    def _():
        copies=block_copies(sc_ref[0],blocks,w,sems)
        start_all(copies); wait_all(copies); start_all(whole)
    r=pl.ds(pl.multiple_of(i*SLOT,SLOT),SLOT)
    for t,up in enumerate((lq_ref,None,lv_ref)):
        v=dg(x_ref[r,:],w[t],1,0)
        if up is not None: v=v+up[r,:]
        qkv_ref[r,t*D:(t+1)*D]=v.astype(BF)
    @pl.when(i==pl.num_programs(0)-1)
    def _(): wait_all(whole)

def project(scalars,x,lq,lv,blocks):
    rows,D=x.shape
    return pl.pallas_call(project_kernel,grid=(rows//SLOT,),
        in_specs=[SCALARS,HELD,HELD,HELD]+[ANY]*len(blocks),
        out_specs=[HELD,ANY],
        out_shape=[pltpu.VMEM((rows,3*D),BF),pltpu.HBM((3,D,D),BF)],
        scratch_shapes=[pltpu.VMEM((3,D,D),BF),pltpu.SemaphoreType.DMA((BLOCK_COPIES,)),pltpu.SemaphoreType.DMA((1,))],
        compiler_params=params(LIM["project"]),cost_estimate=takes(8),name="project")(scalars,x,lq,lv,*blocks)

def attend_kernel(sc_ref,qkv_ref,e_ref,ot_ref,o_ref,rt_ref):
    s=pl.program_id(0); j=pl.program_id(1); J=pl.num_programs(1); D=256*J
    lane=lax.broadcasted_iota(jnp.int32,(SLOT,128),1)
    row=lax.broadcasted_iota(jnp.int32,(SLOT,128),0)
    bias=jnp.where(row<sc_ref[1+s],0.0,-1e30).astype(F32)
    rows=pl.ds(pl.multiple_of(s*SLOT,SLOT),SLOT)
    def part(which,p):
        return qkv_ref[rows,pl.ds(pl.multiple_of(which*D+256*j+128*p,128),128)].astype(F32)
    heads=[]
    for p in range(2):
        qp,kp,vp=part(0,p)*0.125,part(1,p),part(2,p)
        for h in range(2):
            own=(lane<64) if h==0 else (lane>=64)
            aux=64 if h==0 else 0
            one=jnp.where(lane==aux,1.0,0.0)
            heads.append((64*h,aux,jnp.where(own,qp,one).astype(BF),
                          jnp.where(own,kp,jnp.where(lane==aux,bias,0.0)).astype(BF),jnp.where(own,vp,one).astype(BF)))
    totals=[]; os=[]
    def weights(n,st):
        e_ref[n]=jnp.exp(st-jnp.max(st,axis=0,keepdims=True)).astype(BF)
    def mix(n):
        lo,aux,_,_,vm=heads[n]
        ot=dg(vm,e_ref[n],0,0)
        r=1.0/ot[aux:aux+1]
        totals.append(r)
        os.append((ot[lo:lo+64]*r).astype(BF))
    before=None
    for n in range(4):
        st=dg(heads[n][3],heads[n][2],1,1)
        if before is not None:
            weights(n-1,before)
            if n>1: mix(n-2)
        before=st
    weights(3,before)
    mix(2); mix(3)
    ot=jnp.concatenate(os,axis=0)
    ot_ref[...]=ot
    o_ref[rows,pl.ds(pl.multiple_of(256*j,256),256)]=ot.T
    rt_ref[0]=jnp.concatenate(totals+totals,axis=0)

def attend(scalars,qkv,slots):
    rows=qkv.shape[0]; D=qkv.shape[1]//3; J=D//256; H=D//HEAD_DIM
    return pl.pallas_call(attend_kernel,grid=(slots,J),
        in_specs=[SCALARS,HELD],
        out_specs=[pl.BlockSpec((4,SLOT,SLOT),lambda s,j:(s*J+j,0,0)),pl.BlockSpec((256,SLOT),lambda s,j:(s*J+j,0)),HELD,pl.BlockSpec((1,8,SLOT),lambda s,j:(s*J+j,0,0))],
        out_shape=[pltpu.HBM((slots*H,SLOT,SLOT),BF),pltpu.HBM((slots*D,SLOT),BF),pltpu.VMEM((rows,D),BF),pltpu.HBM((slots*J,8,SLOT),F32)],
        compiler_params=params(LIM["attend"]),cost_estimate=takes(16),name="attend")(scalars,qkv)


def norm_stats(value):
    mean=jnp.mean(value,axis=-1,keepdims=True)
    c=value-mean
    r=lax.rsqrt(jnp.mean(c*c,axis=-1,keepdims=True)+1e-5)
    return c*r,r

def norm_back(g,n,r):
    return r*(g-jnp.mean(g,axis=-1,keepdims=True)-n*jnp.mean(g*n,axis=-1,keepdims=True))

def gelu_pair(v):
    cdf=0.5+0.5*lax.erf(v*0.7071067811865476)
    return v*cdf, cdf+(0.3989422804014327*v)*jnp.exp(-0.5*v*v)

CH=256
LIM={"project":10,"attend":12,"feed_in":8,"feed_out":18,"attend_back":12,"inputs_grad":10,"low_rank":10}

def feed_in_kernel(sc_ref,x_ref,o_ref,nm_ref,*rest):
    *blocks,n1_ref,r1_ref,act_ref,gp_ref,w,sems=rest
    i=pl.program_id(0); D=x_ref.shape[1]
    @pl.when(i==0)
    def _():
        copies=block_copies(sc_ref[0],blocks,w,sems)
        start_all(copies); wait_all(copies)
    rows=pl.ds(pl.multiple_of(i*SLOT,SLOT),SLOT)
    first=x_ref[rows,:].astype(F32)+dg(o_ref[rows,:],w[0],1,0)
    n1,r1=norm_stats(first)
    n1_ref[rows,:]=n1; r1_ref[rows,:]=jnp.broadcast_to(r1,(SLOT,128))
    hb=(n1*nm_ref[0:1,:]+nm_ref[1:2,:]).astype(BF)
    for c in range(0,act_ref.shape[1],CH):
        act,gp=gelu_pair(dg(hb,w[1+c//D,:,c%D:c%D+CH],1,0))
        act_ref[rows,c:c+CH]=act.astype(BF)
        gp_ref[rows,c:c+CH]=gp.astype(BF)

def feed_in(scalars,x,o,nm,blocks,FF):
    rows,D=x.shape
    return pl.pallas_call(feed_in_kernel,grid=(rows//SLOT,),
        in_specs=[SCALARS,HELD,HELD,HELD]+[ANY]*len(blocks),
        out_specs=[HELD]*5,
        out_shape=[pltpu.VMEM((rows,D),F32),pltpu.VMEM((rows,128),F32),pltpu.VMEM((rows,FF),BF),pltpu.VMEM((rows,FF),BF),pltpu.VMEM((1+FF//D,D,D),BF)],
        scratch_shapes=[pltpu.SemaphoreType.DMA((BLOCK_COPIES,))],
        compiler_params=params(LIM["feed_in"]),cost_estimate=takes(14),name="feed_in")(scalars,x,o,nm,*blocks)

def feed_out_kernel(sc_ref,n1_ref,r1_ref,act_ref,gp_ref,go_ref,nm_ref,w,*rest):
    *blocks,out_ref,gfs_ref,gmt_ref,gi_ref,wt,sems=rest
    copies=block_copies(sc_ref[0],blocks,wt,sems)
    start_all(copies); wait_all(copies)
    rows,D=go_ref.shape; FF=gi_ref.shape[1]
    ag,ash,fg,fsh=(nm_ref[i:i+1,:] for i in range(4))
    part=[slice(s*SLOT,(s+1)*SLOT) for s in range(rows//SLOT)]
    acc={}; g2={}; g1={}
    def second_sum(s):
        acc[s]=n1_ref[part[s],:]*ag+ash+dg(act_ref[part[s],:],wt[0],1,0)
    def second_norm(s):
        n2,r2=norm_stats(acc[s])
        out_ref[part[s],:]=(n2*fg+fsh).astype(BF)
        g2[s]=norm_back(go_ref[part[s],:].astype(F32)*fg,n2,r2)
    def inner_grad(s):
        g=g2[s].astype(BF)
        for c in range(0,FF,CH):
            ga=dg(g,wt[0,c:c+CH,:],1,1)
            gi_ref[part[s],c:c+CH]=(ga*gp_ref[part[s],c:c+CH].astype(F32)).astype(BF)
    def first_grad(s):
        v=g2[s]
        for b in range(FF//D): v=v+dg(gi_ref[part[s],b*D:(b+1)*D],w[1+b],1,1)
        acc[s]=v
    def first_norm(s):
        g=norm_back(acc[s]*ag,n1_ref[part[s],:],r1_ref[part[s],0:1])
        gfs_ref[part[s],:]=g
        g1[s]=g.astype(BF)
    def mixed_grad(s):
        gmt_ref[:,part[s]]=dg(w[0],g1[s],1,1).astype(BF)
    stages=(second_sum,second_norm,inner_grad,first_grad,first_norm,mixed_grad)
    order=sorted((2*k+(3*s if k else 0),s,k) for s in range(len(part)) for k in range(len(stages)))
    for _,s,k in order:
        stages[k](s)

def feed_out(scalars,n1,r1,act,gp,go,w,nm,blocks):
    rows,D=n1.shape; FF=act.shape[1]
    return pl.pallas_call(feed_out_kernel,
        in_specs=[SCALARS]+[HELD]*7+[ANY]*len(blocks),
        out_specs=[HELD]*4,
        out_shape=[sd((rows,D),BF),pltpu.VMEM((rows,D),F32),pltpu.VMEM((D,rows),BF),pltpu.VMEM((rows,FF),BF)],
        input_output_aliases={3:3},
        scratch_shapes=[pltpu.VMEM((1,FF,D),BF),pltpu.SemaphoreType.DMA((BLOCK_COPIES,))],
        compiler_params=params(LIM["feed_out"]),cost_estimate=takes(24),name="feed_out")(scalars,n1,r1,act,gp,go,nm,w,*blocks)[:3]


def attend_back_kernel(sc_ref,q_ref,k_ref,v_ref,e_ref,ot_ref,rt_ref,gmt_ref,x_ref,low_ref,upq_ref,upv_ref,
                       d_ref,gl_ref,mine_ref,other_ref,glacc,ad_ref):
    s=pl.program_id(0); j=pl.program_id(1); J=pl.num_programs(1)
    lane=lax.broadcasted_iota(jnp.int32,(SLOT,128),1)
    rowi=lax.broadcasted_iota(jnp.int32,(128,SLOT),0)
    D=256*J
    rows=pl.ds(pl.multiple_of(s*SLOT,SLOT),SLOT)
    def place_of(which,p):
        return rows,pl.ds(pl.multiple_of(which*D+256*j+128*p,128),128)
    gmq=gmt_ref[pl.ds(pl.multiple_of(256*j,256),256),rows]
    otq=ot_ref[...]
    dqts=[]; dvs=[]
    for p in range(2):
        cols=slice(128*p,128*p+128)
        qp,kp,vp=(w[:,cols].astype(F32) for w in (q_ref,k_ref,v_ref))
        qp=qp*0.125; kp=kp*0.125
        gm=gmq[cols,:].astype(F32); om=otq[cols,:].astype(F32)
        pr=gm*om
        dkp=None; dvp=None; dqt=None
        for h in range(2):
            own=(lane<64) if h==0 else (lane>=64)
            ownr=(rowi<64) if h==0 else (rowi>=64)
            aux=64 if h==0 else 0
            r=rt_ref[0,2*p+h:2*p+h+1,:]
            d=-jnp.sum(pr[64*h:64*h+64],axis=0,keepdims=True)*r
            dhi=d.astype(BF).astype(F32)
            dlo=d-dhi
            gs=gm*r
            gaug=jnp.where(ownr,gs,jnp.where(rowi==aux,dhi,jnp.where(rowi==aux+1,dlo,0.0))).astype(BF)
            gown=jnp.where(ownr,gs,0.0).astype(BF)
            vm=jnp.where(own,vp,jnp.where((lane==aux)|(lane==aux+1),1.0,0.0)).astype(BF)
            e=e_ref[2*p+h]
            ds=(dg(vm,gaug,1,0)*e.astype(F32)).astype(BF)
            qm=jnp.where(own,qp,0.0).astype(BF)
            km=jnp.where(own,kp,0.0).astype(BF)
            dv=dg(e,gown,1,1)
            dk=dg(ds,qm,1,0)
            dq=dg(km,ds,0,0)
            dvp=dv if dvp is None else dvp+dv
            dkp=dk if dkp is None else dkp+dk
            dqt=dq if dqt is None else dqt+dq
        d_ref[place_of(1,p)]=dkp.astype(BF)
        dvs.append(dvp.astype(BF))
        d_ref[place_of(2,p)]=dvs[p]
        dqts.append(dqt.astype(BF))
    dqt=jnp.concatenate(dqts,axis=0)
    dqb=dqt.T
    d_ref[rows,pl.ds(pl.multiple_of(256*j,256),256)]=dqb
    dvb=jnp.concatenate(dvs,axis=1)
    glq=dg(upq_ref[...],dqt,1,0)
    glv=dg(upv_ref[...],dvb,1,1)
    part=2.0*(glq+glv)
    @pl.when(j==0)
    def _(): glacc[...]=part
    @pl.when(j>0)
    def _(): glacc[...]+=part
    low=low_ref[...]
    c0=pl.multiple_of(j*256,256)
    upq=2.0*dg(low[:16],dqb,1,0)
    upv=2.0*dg(low[:16],dvb,1,0)
    upg=jnp.concatenate([upq[0:8],upv[8:16]],axis=0)
    def add(rows,cols,v):
        @pl.when(s==0)
        def _(): ad_ref[rows,cols]=v
        @pl.when(s>0)
        def _(): ad_ref[rows,cols]+=v
    add(slice(16,32),pl.ds(c0,256),upg)
    @pl.when(j==J-1)
    def _():
        gl=glacc[...].astype(BF)
        gl_ref[...]=gl
        add(slice(0,16),slice(None),dg(gl,x_ref[...],1,0))
        core=lax.rem(sc_ref[0],2)
        for c,(a,b) in enumerate(((mine_ref,other_ref),(other_ref,mine_ref))):
            @pl.when((s==pl.num_programs(0)-1)&(core==c))
            def _():
                a[...]=ad_ref[0:16,:]
                b[...]=ad_ref[16:32,:]

def attend_back(scalars,qkv,e,ot,rt,gmt,x,low,upq,upv):
    rows,D=x.shape; J=D//256; S=rows//SLOT
    up=pl.BlockSpec((16,256),lambda s,j:(0,j))
    return pl.pallas_call(attend_back_kernel,grid=(S,J),
        in_specs=[SCALARS,*[pl.BlockSpec((SLOT,256),lambda s,j,w=w:(s,w*J+j)) for w in range(3)],
                  pl.BlockSpec((4,SLOT,SLOT),lambda s,j:(s*J+j,0,0)),pl.BlockSpec((256,SLOT),lambda s,j:(s*J+j,0)),
                  pl.BlockSpec((1,8,SLOT),lambda s,j:(s*J+j,0,0)),HELD,
                  pl.BlockSpec((SLOT,D),lambda s,j:(s,0)),pl.BlockSpec((32,SLOT),lambda s,j:(0,s)),up,up],
        out_specs=[HELD,pl.BlockSpec((16,SLOT),lambda s,j:(0,s)),HELD,HELD],
        out_shape=[pltpu.VMEM((rows,3*D),BF),sd((16,rows),BF),pltpu.VMEM((16,D),F32),pltpu.VMEM((16,D),F32)],
        scratch_shapes=[pltpu.VMEM((16,SLOT),F32),pltpu.VMEM((32,D),F32)],
        compiler_params=params(LIM["attend_back"]),cost_estimate=takes(18),name="attend_back")(scalars,far(qkv),far(qkv),far(qkv),far(e),far(ot),rt,gmt,x,low,upq,upv)

def inputs_kernel(gfs_ref,d_ref,gl,w_ref,dnt_ref,out_ref):
    T=gfs_ref.shape[0]
    rows=pl.ds(pl.multiple_of(pl.program_id(0)*T,T),T)
    D=gfs_ref.shape[1]
    v=gfs_ref[...]+dg(gl[...],dnt_ref[...],0,0)
    for t in range(3): v=v+dg(d_ref[rows,t*D:(t+1)*D],w_ref[t],1,1)
    out_ref[...]=v

def inputs_grad(gfs,d,gl,w,dnt):
    rows,D=gfs.shape
    row=pl.BlockSpec((SLOT,D),lambda i:(i,0))
    return pl.pallas_call(inputs_kernel,grid=(rows//SLOT,),
        in_specs=[row,HELD,pl.BlockSpec((16,SLOT),lambda i:(0,i)),HELD,HELD],
        out_specs=row,out_shape=sd((rows,D),F32),
        compiler_params=params(LIM["inputs_grad"]),cost_estimate=takes(7),name="inputs_grad")(gfs,d,gl,w,dnt)


def device_count():
    return lax.axis_size("dp")*lax.axis_size("fsdp")

def permute(v,target):
    return lax.ppermute(v,AXES,[(i,target(i)) for i in range(device_count())])

def exchange(v,mask):
    return permute(v,lambda i:i^mask)

def along_z(block):
    top=device_count()//4
    return [block]+[exchange(block,top*m) for m in (1,2,3)]

def near_hop(v):
    return permute(v,lambda i:i^(4 if i%2 else 2))

def far_hop(v):
    return permute(v,lambda i:i^(2 if i%2 else 4))

def in_bands(bands,*blocks):
    return tuple(b.reshape(8,bands,-1,b.shape[2]) for b in blocks)

def core_pair(v):
    groups=[[2*i,2*i+1] for i in range(lax.axis_size("fsdp")//2)]
    return lax.all_gather(v,"fsdp",axis=0,tiled=False,axis_index_groups=groups)

def column_half(both):
    c=lax.axis_index("fsdp")%2
    half=both.shape[2]//2
    return lax.dynamic_slice_in_dim(both,c*half,half,axis=2).reshape(-1,half)

def total_over_devices(mine,other,meanwhile):
    n=device_count()
    mine=mine+exchange(other,1)
    got=[exchange(mine,m) for m in range(2,n//4,2)]
    for g in got: mine=mine+g
    got=[exchange(mine,m) for m in (n//4,n//2,3*n//4)]
    got,done=tie(got,meanwhile())
    for g in got: mine=mine+g
    return mine,exchange(mine,1),done

def finish_kernel(scale,sc_ref,mine_ref,other_ref,*outs):
    core=lax.rem(sc_ref[0],2)
    for c,halves in enumerate(((mine_ref,other_ref),(other_ref,mine_ref))):
        @pl.when(core==c)
        def _():
            for i,o in enumerate(outs): o[...]=halves[i//2][8*(i%2):8*(i%2)+8,:]*scale

def finish(scalars,mine,other,scale):
    D=mine.shape[1]
    return pl.pallas_call(functools.partial(finish_kernel,scale),in_specs=[SCALARS,HELD,HELD],out_specs=[HELD]*4,
        out_shape=[sd((8,D),F32)]*4,compiler_params=params(8),cost_estimate=takes(1),name="finish")(scalars,mine,other)

def tie(*v):
    return lax.optimization_barrier(v)

def by_hops(scalars,x,wq,wk,wv,wo,wi,wt,ag,ash,fg,fsh,qd,qu,vd,vu,go):
    D=wq.shape[1]; FF=wi.shape[1]; bands=FF//D; r=wq.shape[0]
    top=device_count()//4
    both=core_pair(jnp.concatenate([wq,wk,wv],0))
    s1=jnp.concatenate([column_half(both[:,r*t:r*t+r]) for t in range(3)],0)
    z1=along_z(s1)
    wo,wi,wt,qd,s1=tie(wo,wi,wt,qd,s1)
    bo,bi,bt=core_pair(wo),core_pair(wi),core_pair(wt)
    s2=jnp.concatenate([column_half(bo)]+[column_half(bi[:,:,D*t:D*t+D]) for t in range(bands)],0)
    s3=column_half(bt)
    dn,upq,upv,dnt,nm=prep(qd,qu,vd,vu,ag,ash,fg,fsh)
    n3=near_hop(s3)
    z1,s2,dn,scalars=tie(z1,s2,dn,scalars)
    a1=jnp.stack(z1,0)
    n1=near_hop(a1)
    z2=exchange(s2,2*top)
    b3=jnp.stack([s3,n3],0)
    y3=exchange(b3,top)
    n1,z2,s2,n3,dn=tie(n1,z2,s2,n3,dn)
    f1=jnp.concatenate([a1,n1],0)
    h1=far_hop(f1); of1=exchange(f1,1)
    e2=jnp.stack([s2,z2],0)
    y2=exchange(e2,top)
    m2=near_hop(e2)
    low,lq,lv=low_rank(x,dn,upq,upv)
    y2,y3,lq=tie(y2,y3,lq)
    n2=near_hop(y2)
    g3=jnp.stack([b3,y3],0)
    z3=exchange(g3,2*top)
    h1,of1=tie(h1,of1)
    oh1=exchange(h1,1)
    oh1,=tie(oh1)
    f2=jnp.stack([e2[0],y2[0],e2[1],y2[1],m2[0],n2[0],m2[1],n2[1]],0)
    h2=far_hop(f2); of2=exchange(f2,1)
    qkv,wqkv=project(scalars,x,lq,lv,in_bands(3,f1,h1,of1,oh1))
    e,ot,o,rt=attend(scalars,qkv,x.shape[0]//SLOT)
    h2,o,of2,z3=tie(h2,o,of2,z3)
    oh2=exchange(h2,1)
    f3=jnp.concatenate([g3,z3],0).swapaxes(0,1).reshape(8,-1,D//2)
    h3=far_hop(f3); of3=exchange(f3,1)
    oh2,=tie(oh2)
    nn,r1,act,gp,w=feed_in(scalars,x,o,nm,in_bands(1+bands,f2,h2,of2,oh2),FF)
    h3,nn,of3=tie(h3,nn,of3)
    oh3=exchange(h3,1)
    out,gfs,gmt=feed_out(scalars,nn,r1,act,gp,go,w,nm,in_bands(1,f3,h3,of3,oh3))
    return qkv,low,wqkv,e,ot,rt,out,gfs,gmt,upq,upv,dnt

def by_all_gather(scalars,x,wq,wk,wv,wo,wi,wt,ag,ash,fg,fsh,qd,qu,vd,vu,go):
    wq,wk,wv,wo,wi,wt=(lax.all_gather(w,AXES,axis=0,tiled=True) for w in (wq,wk,wv,wo,wi,wt))
    D=wq.shape[1]; FF=wi.shape[1]
    dn,upq,upv,dnt,nm=prep(qd,qu,vd,vu,ag,ash,fg,fsh)
    low,lq,lv=low_rank(x,dn,upq,upv)
    qkv,wqkv=project(scalars,x,lq,lv,(jnp.stack([wq,wk,wv],0),))
    e,ot,o,rt=attend(scalars,qkv,x.shape[0]//SLOT)
    nn,r1,act,gp,w=feed_in(scalars,x,o,nm,(jnp.stack([wo]+[wi[:,c:c+D] for c in range(0,FF,D)],0),),FF)
    out,gfs,gmt=feed_out(scalars,nn,r1,act,gp,go,w,nm,(wt[None],))
    return qkv,low,wqkv,e,ot,rt,out,gfs,gmt,upq,upv,dnt

def shards(x,lengths,wq,wk,wv,wo,wi,wt,ag,ash,fg,fsh,qd,qu,vd,vu,go):
    n=device_count()
    valid=lengths[:,0]+lengths[:,1]+4
    me=(lax.axis_index("dp")*lax.axis_size("fsdp")+lax.axis_index("fsdp")).reshape(1)
    scalars=jnp.concatenate([me,valid]).astype(jnp.int32)
    forward=by_hops if n==32 and wq.shape[0]%8==0 else by_all_gather
    qkv,low,wqkv,e,ot,rt,out,gfs,gmt,upq,upv,dnt=forward(scalars,x,wq,wk,wv,wo,wi,wt,ag,ash,fg,fsh,qd,qu,vd,vu,go)
    d,gl,mine,other=attend_back(scalars,qkv,e,ot,rt,gmt,x,low,upq,upv)
    mine,other,gx=total_over_devices(mine,other,lambda: inputs_grad(gfs,d,gl,wqkv,dnt))
    qd,vd,qu,vu=finish(scalars,mine,other,1.0/(lengths.shape[0]*n))
    return out,gx,qd.T,qu,vd.T,vu

def solution(mesh):
    sp=P(AXES,None)
    return jax.shard_map(shards,mesh=mesh,in_specs=(sp,)*8+(P(),)*8+(sp,),
        out_specs=(sp,sp,P(),P(),P(),P()),check_vma=False)
```

```python
import functools
import jax
import jax.numpy as jnp
from jax import lax
from jax.experimental import pallas as pl
from jax.experimental.pallas import tpu as pltpu
from jax.sharding import PartitionSpec as P

HEAD_DIM=64; SLOT=512
F32=jnp.float32; BF=jnp.bfloat16
MIB=1024*1024
AXES=("dp","fsdp")
sd=jax.ShapeDtypeStruct
ANY=pl.BlockSpec(memory_space=pl.ANY)
HELD=pl.BlockSpec(memory_space=pltpu.VMEM)
SCALARS=pl.BlockSpec(memory_space=pltpu.SMEM)


def params(mib=56):
    return pltpu.CompilerParams(vmem_limit_bytes=mib*MIB)

def takes(us):
    return pl.CostEstimate(flops=int(us*1.1e9),bytes_accessed=0,transcendentals=0)


def dg(a,b,ca,cb):
    return lax.dot_general(a,b,(((ca,),(cb,)),((),())),preferred_element_type=F32)

def far(v):
    return pltpu.with_memory_space_constraint(v,pltpu.HBM)


def block_copies(me,bufs,to,sems):
    if len(bufs)==1:
        return [pltpu.make_async_copy(bufs[0],to,sems.at[0])]
    chip=lax.div(me,2); core=lax.rem(me,2)
    copies=[]
    for which,buf in enumerate(bufs):
        origin=core if which<2 else 1-core
        _,_,rows,half=buf.shape
        for i in range(8):
            dst=lax.bitwise_xor(chip,(which%2)*(2-origin)+(i//4)*(1+origin)+4*(i%4))
            at=to.at[:,pl.ds(pl.multiple_of(dst*rows,16),rows),pl.ds(pl.multiple_of(origin*half,128),half)]
            copies.append(pltpu.make_async_copy(buf.at[i],at,sems.at[len(copies)]))
    return copies

def start_all(copies):
    for c in copies: c.start()

def wait_all(copies):
    for c in copies: c.wait()

BLOCK_COPIES=32

def prep_kernel(qdt_ref,vdt_ref,qu_ref,vu_ref,ag_ref,ash_ref,fg_ref,fsh_ref,dn_ref,upq_ref,upv_ref,dnt_ref,nm_ref):
    D=qu_ref.shape[1]
    both=jnp.concatenate([qdt_ref[...],vdt_ref[...]],axis=0)
    dnt_ref[...]=both.astype(BF)
    dn_ref[...]=jnp.concatenate([both,jnp.zeros((112,D),F32)],axis=0).T.astype(BF)
    z8=jnp.zeros((8,D),F32); z=jnp.zeros((112,D),F32)
    upq_ref[...]=jnp.concatenate([qu_ref[...],z8,z],axis=0).astype(BF)
    upv_ref[...]=jnp.concatenate([z8,vu_ref[...],z],axis=0).astype(BF)
    for i,r in enumerate((ag_ref,ash_ref,fg_ref,fsh_ref)):
        nm_ref[i:i+1,:]=r[...].astype(F32)
    nm_ref[4:8,:]=jnp.zeros((4,D),F32)

def prep(qd,qu,vd,vu,ag,ash,fg,fsh):
    D=qu.shape[1]
    return pl.pallas_call(prep_kernel,out_shape=[sd((D,128),BF),sd((128,D),BF),sd((128,D),BF),sd((16,D),BF),sd((8,D),F32)],
        compiler_params=params(8),cost_estimate=takes(1),name="prep")(qd.T,vd.T,qu,vu,*(v.reshape(1,D) for v in (ag,ash,fg,fsh)))


def low_kernel(x_ref,dn_ref,upq_ref,upv_ref,low_ref,lq_ref,lv_ref):
    for s in range(x_ref.shape[0]//SLOT):
        r=slice(s*SLOT,(s+1)*SLOT)
        low=dg(x_ref[r,:],dn_ref[...],1,0).astype(BF)
        low_ref[:,r]=low.T[:32]
        lq_ref[r,:]=2.0*dg(low,upq_ref[...],1,0)
        lv_ref[r,:]=2.0*dg(low,upv_ref[...],1,0)

def low_rank(x,dn,upq,upv):
    rows,D=x.shape
    return pl.pallas_call(low_kernel,in_specs=[HELD]*4,out_specs=[HELD]*3,
        out_shape=[sd((32,rows),BF),pltpu.VMEM((rows,D),F32),pltpu.VMEM((rows,D),F32)],
        compiler_params=params(LIM["low_rank"]),cost_estimate=takes(3),name="low_rank")(x,dn,upq,upv)

def project_kernel(sc_ref,x_ref,lq_ref,lv_ref,*rest):
    *blocks,qkv_ref,wo,w,sems,osem=rest
    i=pl.program_id(0); D=x_ref.shape[1]
    whole=[pltpu.make_async_copy(w,wo,osem.at[0])]
    @pl.when(i==0)
    def _():
        copies=block_copies(sc_ref[0],blocks,w,sems)
        start_all(copies); wait_all(copies); start_all(whole)
    r=pl.ds(pl.multiple_of(i*SLOT,SLOT),SLOT)
    for t,up in enumerate((lq_ref,None,lv_ref)):
        v=dg(x_ref[r,:],w[t],1,0)
        if up is not None: v=v+up[r,:]
        qkv_ref[r,t*D:(t+1)*D]=v.astype(BF)
    @pl.when(i==pl.num_programs(0)-1)
    def _(): wait_all(whole)

def project(scalars,x,lq,lv,blocks):
    rows,D=x.shape
    return pl.pallas_call(project_kernel,grid=(rows//SLOT,),
        in_specs=[SCALARS,HELD,HELD,HELD]+[ANY]*len(blocks),
        out_specs=[HELD,ANY],
        out_shape=[pltpu.VMEM((rows,3*D),BF),pltpu.HBM((3,D,D),BF)],
        scratch_shapes=[pltpu.VMEM((3,D,D),BF),pltpu.SemaphoreType.DMA((BLOCK_COPIES,)),pltpu.SemaphoreType.DMA((1,))],
        compiler_params=params(LIM["project"]),cost_estimate=takes(8),name="project")(scalars,x,lq,lv,*blocks)

def attend_kernel(sc_ref,qkv_ref,e_ref,ot_ref,o_ref,rt_ref):
    s=pl.program_id(0); j=pl.program_id(1); J=pl.num_programs(1); D=256*J
    lane=lax.broadcasted_iota(jnp.int32,(SLOT,128),1)
    row=lax.broadcasted_iota(jnp.int32,(SLOT,128),0)
    bias=jnp.where(row<sc_ref[1+s],0.0,-1e30).astype(F32)
    rows=pl.ds(pl.multiple_of(s*SLOT,SLOT),SLOT)
    def part(which,p):
        return qkv_ref[rows,pl.ds(pl.multiple_of(which*D+256*j+128*p,128),128)].astype(F32)
    heads=[]
    for p in range(2):
        qp,kp,vp=part(0,p)*0.125,part(1,p),part(2,p)
        for h in range(2):
            own=(lane<64) if h==0 else (lane>=64)
            aux=64 if h==0 else 0
            one=jnp.where(lane==aux,1.0,0.0)
            heads.append((64*h,aux,jnp.where(own,qp,one).astype(BF),
                          jnp.where(own,kp,jnp.where(lane==aux,bias,0.0)).astype(BF),jnp.where(own,vp,one).astype(BF)))
    totals=[]; os=[]
    def weights(n,st):
        e_ref[n]=jnp.exp(st-jnp.max(st,axis=0,keepdims=True)).astype(BF)
    def mix(n):
        lo,aux,_,_,vm=heads[n]
        ot=dg(vm,e_ref[n],0,0)
        r=1.0/ot[aux:aux+1]
        totals.append(r)
        os.append((ot[lo:lo+64]*r).astype(BF))
    before=None
    for n in range(4):
        st=dg(heads[n][3],heads[n][2],1,1)
        if before is not None:
            weights(n-1,before)
            if n>1: mix(n-2)
        before=st
    weights(3,before)
    mix(2); mix(3)
    ot=jnp.concatenate(os,axis=0)
    ot_ref[...]=ot
    o_ref[rows,pl.ds(pl.multiple_of(256*j,256),256)]=ot.T
    rt_ref[0]=jnp.concatenate(totals+totals,axis=0)

def attend(scalars,qkv,slots):
    rows=qkv.shape[0]; D=qkv.shape[1]//3; J=D//256; H=D//HEAD_DIM
    return pl.pallas_call(attend_kernel,grid=(slots,J),
        in_specs=[SCALARS,HELD],
        out_specs=[pl.BlockSpec((4,SLOT,SLOT),lambda s,j:(s*J+j,0,0)),pl.BlockSpec((256,SLOT),lambda s,j:(s*J+j,0)),HELD,pl.BlockSpec((1,8,SLOT),lambda s,j:(s*J+j,0,0))],
        out_shape=[pltpu.HBM((slots*H,SLOT,SLOT),BF),pltpu.HBM((slots*D,SLOT),BF),pltpu.VMEM((rows,D),BF),pltpu.HBM((slots*J,8,SLOT),F32)],
        compiler_params=params(LIM["attend"]),cost_estimate=takes(16),name="attend")(scalars,qkv)


def norm_stats(value):
    mean=jnp.mean(value,axis=-1,keepdims=True)
    c=value-mean
    r=lax.rsqrt(jnp.mean(c*c,axis=-1,keepdims=True)+1e-5)
    return c*r,r

def norm_back(g,n,r):
    return r*(g-jnp.mean(g,axis=-1,keepdims=True)-n*jnp.mean(g*n,axis=-1,keepdims=True))

def gelu_pair(v):
    cdf=0.5+0.5*lax.erf(v*0.7071067811865476)
    return v*cdf, cdf+(0.3989422804014327*v)*jnp.exp(-0.5*v*v)

CH=256
LIM={"project":10,"attend":12,"feed_in":8,"feed_out":18,"attend_back":12,"inputs_grad":10,"low_rank":10}

def feed_in_kernel(sc_ref,x_ref,o_ref,nm_ref,*rest):
    *blocks,n1_ref,r1_ref,act_ref,gp_ref,w,sems=rest
    i=pl.program_id(0); D=x_ref.shape[1]
    @pl.when(i==0)
    def _():
        copies=block_copies(sc_ref[0],blocks,w,sems)
        start_all(copies); wait_all(copies)
    rows=pl.ds(pl.multiple_of(i*SLOT,SLOT),SLOT)
    first=x_ref[rows,:].astype(F32)+dg(o_ref[rows,:],w[0],1,0)
    n1,r1=norm_stats(first)
    n1_ref[rows,:]=n1; r1_ref[rows,:]=jnp.broadcast_to(r1,(SLOT,128))
    hb=(n1*nm_ref[0:1,:]+nm_ref[1:2,:]).astype(BF)
    for c in range(0,act_ref.shape[1],CH):
        act,gp=gelu_pair(dg(hb,w[1+c//D,:,c%D:c%D+CH],1,0))
        act_ref[rows,c:c+CH]=act.astype(BF)
        gp_ref[rows,c:c+CH]=gp.astype(BF)

def feed_in(scalars,x,o,nm,blocks,FF):
    rows,D=x.shape
    return pl.pallas_call(feed_in_kernel,grid=(rows//SLOT,),
        in_specs=[SCALARS,HELD,HELD,HELD]+[ANY]*len(blocks),
        out_specs=[HELD]*5,
        out_shape=[pltpu.VMEM((rows,D),F32),pltpu.VMEM((rows,128),F32),pltpu.VMEM((rows,FF),BF),pltpu.VMEM((rows,FF),BF),pltpu.VMEM((1+FF//D,D,D),BF)],
        scratch_shapes=[pltpu.SemaphoreType.DMA((BLOCK_COPIES,))],
        compiler_params=params(LIM["feed_in"]),cost_estimate=takes(14),name="feed_in")(scalars,x,o,nm,*blocks)

def feed_out_kernel(sc_ref,n1_ref,r1_ref,act_ref,gp_ref,go_ref,nm_ref,w,*rest):
    *blocks,out_ref,gfs_ref,gmt_ref,gi_ref,wt,sems=rest
    copies=block_copies(sc_ref[0],blocks,wt,sems)
    start_all(copies); wait_all(copies)
    rows,D=go_ref.shape; FF=gi_ref.shape[1]
    ag,ash,fg,fsh=(nm_ref[i:i+1,:] for i in range(4))
    part=[slice(s*SLOT,(s+1)*SLOT) for s in range(rows//SLOT)]
    acc={}; g2={}; g1={}
    def second_sum(s):
        acc[s]=n1_ref[part[s],:]*ag+ash+dg(act_ref[part[s],:],wt[0],1,0)
    def second_norm(s):
        n2,r2=norm_stats(acc[s])
        out_ref[part[s],:]=(n2*fg+fsh).astype(BF)
        g2[s]=norm_back(go_ref[part[s],:].astype(F32)*fg,n2,r2)
    def inner_grad(s):
        g=g2[s].astype(BF)
        for c in range(0,FF,CH):
            ga=dg(g,wt[0,c:c+CH,:],1,1)
            gi_ref[part[s],c:c+CH]=(ga*gp_ref[part[s],c:c+CH].astype(F32)).astype(BF)
    def first_grad(s):
        v=g2[s]
        for b in range(FF//D): v=v+dg(gi_ref[part[s],b*D:(b+1)*D],w[1+b],1,1)
        acc[s]=v
    def first_norm(s):
        g=norm_back(acc[s]*ag,n1_ref[part[s],:],r1_ref[part[s],0:1])
        gfs_ref[part[s],:]=g
        g1[s]=g.astype(BF)
    def mixed_grad(s):
        gmt_ref[:,part[s]]=dg(w[0],g1[s],1,1).astype(BF)
    stages=(second_sum,second_norm,inner_grad,first_grad,first_norm,mixed_grad)
    order=sorted((2*k+(3*s if k else 0),s,k) for s in range(len(part)) for k in range(len(stages)))
    for _,s,k in order:
        stages[k](s)

def feed_out(scalars,n1,r1,act,gp,go,w,nm,blocks):
    rows,D=n1.shape; FF=act.shape[1]
    return pl.pallas_call(feed_out_kernel,
        in_specs=[SCALARS]+[HELD]*7+[ANY]*len(blocks),
        out_specs=[HELD]*4,
        out_shape=[sd((rows,D),BF),pltpu.VMEM((rows,D),F32),pltpu.VMEM((D,rows),BF),pltpu.VMEM((rows,FF),BF)],
        input_output_aliases={3:3},
        scratch_shapes=[pltpu.VMEM((1,FF,D),BF),pltpu.SemaphoreType.DMA((BLOCK_COPIES,))],
        compiler_params=params(LIM["feed_out"]),cost_estimate=takes(24),name="feed_out")(scalars,n1,r1,act,gp,go,nm,w,*blocks)[:3]


def attend_back_kernel(sc_ref,q_ref,k_ref,v_ref,e_ref,ot_ref,rt_ref,gmt_ref,x_ref,low_ref,upq_ref,upv_ref,
                       d_ref,gl_ref,mine_ref,other_ref,glacc,ad_ref):
    s=pl.program_id(0); j=pl.program_id(1); J=pl.num_programs(1)
    lane=lax.broadcasted_iota(jnp.int32,(SLOT,128),1)
    rowi=lax.broadcasted_iota(jnp.int32,(128,SLOT),0)
    D=256*J
    rows=pl.ds(pl.multiple_of(s*SLOT,SLOT),SLOT)
    def place_of(which,p):
        return rows,pl.ds(pl.multiple_of(which*D+256*j+128*p,128),128)
    gmq=gmt_ref[pl.ds(pl.multiple_of(256*j,256),256),rows]
    otq=ot_ref[...]
    dqts=[]; dvs=[]
    for p in range(2):
        cols=slice(128*p,128*p+128)
        qp,kp,vp=(w[:,cols].astype(F32) for w in (q_ref,k_ref,v_ref))
        qp=qp*0.125; kp=kp*0.125
        gm=gmq[cols,:].astype(F32); om=otq[cols,:].astype(F32)
        pr=gm*om
        dkp=None; dvp=None; dqt=None
        for h in range(2):
            own=(lane<64) if h==0 else (lane>=64)
            ownr=(rowi<64) if h==0 else (rowi>=64)
            aux=64 if h==0 else 0
            r=rt_ref[0,2*p+h:2*p+h+1,:]
            d=-jnp.sum(pr[64*h:64*h+64],axis=0,keepdims=True)*r
            dhi=d.astype(BF).astype(F32)
            dlo=d-dhi
            gs=gm*r
            gaug=jnp.where(ownr,gs,jnp.where(rowi==aux,dhi,jnp.where(rowi==aux+1,dlo,0.0))).astype(BF)
            gown=jnp.where(ownr,gs,0.0).astype(BF)
            vm=jnp.where(own,vp,jnp.where((lane==aux)|(lane==aux+1),1.0,0.0)).astype(BF)
            e=e_ref[2*p+h]
            ds=(dg(vm,gaug,1,0)*e.astype(F32)).astype(BF)
            qm=jnp.where(own,qp,0.0).astype(BF)
            km=jnp.where(own,kp,0.0).astype(BF)
            dv=dg(e,gown,1,1)
            dk=dg(ds,qm,1,0)
            dq=dg(km,ds,0,0)
            dvp=dv if dvp is None else dvp+dv
            dkp=dk if dkp is None else dkp+dk
            dqt=dq if dqt is None else dqt+dq
        d_ref[place_of(1,p)]=dkp.astype(BF)
        dvs.append(dvp.astype(BF))
        d_ref[place_of(2,p)]=dvs[p]
        dqts.append(dqt.astype(BF))
    dqt=jnp.concatenate(dqts,axis=0)
    dqb=dqt.T
    d_ref[rows,pl.ds(pl.multiple_of(256*j,256),256)]=dqb
    dvb=jnp.concatenate(dvs,axis=1)
    glq=dg(upq_ref[...],dqt,1,0)
    glv=dg(upv_ref[...],dvb,1,1)
    part=2.0*(glq+glv)
    @pl.when(j==0)
    def _(): glacc[...]=part
    @pl.when(j>0)
    def _(): glacc[...]+=part
    low=low_ref[...]
    c0=pl.multiple_of(j*256,256)
    upq=2.0*dg(low[:16],dqb,1,0)
    upv=2.0*dg(low[:16],dvb,1,0)
    upg=jnp.concatenate([upq[0:8],upv[8:16]],axis=0)
    def add(rows,cols,v):
        @pl.when(s==0)
        def _(): ad_ref[rows,cols]=v
        @pl.when(s>0)
        def _(): ad_ref[rows,cols]+=v
    add(slice(16,32),pl.ds(c0,256),upg)
    @pl.when(j==J-1)
    def _():
        gl=glacc[...].astype(BF)
        gl_ref[...]=gl
        add(slice(0,16),slice(None),dg(gl,x_ref[...],1,0))
        core=lax.rem(sc_ref[0],2)
        for c,(a,b) in enumerate(((mine_ref,other_ref),(other_ref,mine_ref))):
            @pl.when((s==pl.num_programs(0)-1)&(core==c))
            def _():
                a[...]=ad_ref[0:16,:]
                b[...]=ad_ref[16:32,:]

def attend_back(scalars,qkv,e,ot,rt,gmt,x,low,upq,upv):
    rows,D=x.shape; J=D//256; S=rows//SLOT
    up=pl.BlockSpec((16,256),lambda s,j:(0,j))
    return pl.pallas_call(attend_back_kernel,grid=(S,J),
        in_specs=[SCALARS,*[pl.BlockSpec((SLOT,256),lambda s,j,w=w:(s,w*J+j)) for w in range(3)],
                  pl.BlockSpec((4,SLOT,SLOT),lambda s,j:(s*J+j,0,0)),pl.BlockSpec((256,SLOT),lambda s,j:(s*J+j,0)),
                  pl.BlockSpec((1,8,SLOT),lambda s,j:(s*J+j,0,0)),HELD,
                  pl.BlockSpec((SLOT,D),lambda s,j:(s,0)),pl.BlockSpec((32,SLOT),lambda s,j:(0,s)),up,up],
        out_specs=[HELD,pl.BlockSpec((16,SLOT),lambda s,j:(0,s)),HELD,HELD],
        out_shape=[pltpu.VMEM((rows,3*D),BF),sd((16,rows),BF),pltpu.VMEM((16,D),F32),pltpu.VMEM((16,D),F32)],
        scratch_shapes=[pltpu.VMEM((16,SLOT),F32),pltpu.VMEM((32,D),F32)],
        compiler_params=params(LIM["attend_back"]),cost_estimate=takes(18),name="attend_back")(scalars,far(qkv),far(qkv),far(qkv),far(e),far(ot),rt,gmt,x,low,upq,upv)

def inputs_kernel(s,gfs_ref,d_ref,gl,w_ref,dnt_ref,*rest):
    D=gfs_ref.shape[1]
    rows=slice(s*SLOT,(s+1)*SLOT)
    v=gfs_ref[rows,:]+dg(gl[...],dnt_ref[...],0,0)
    for t in range(3): v=v+dg(d_ref[rows,t*D:(t+1)*D],w_ref[t],1,1)
    rest[-1][...]=v

def inputs_grad(s,gfs,d,gl,w,dnt,into=()):
    rows,D=gfs.shape
    return pl.pallas_call(functools.partial(inputs_kernel,s),grid=(1,),
        in_specs=[HELD,HELD,pl.BlockSpec((16,SLOT),lambda i:(0,s)),HELD,HELD]+[ANY]*len(into),
        out_specs=pl.BlockSpec((SLOT,D),lambda i:(s,0)),out_shape=sd((rows,D),F32),input_output_aliases={5:0} if into else {},
        compiler_params=params(LIM["inputs_grad"]),cost_estimate=takes(3),name="inputs_grad")(gfs,d,gl,w,dnt,*into)


def device_count():
    return lax.axis_size("dp")*lax.axis_size("fsdp")

def permute(v,target):
    return lax.ppermute(v,AXES,[(i,target(i)) for i in range(device_count())])

def exchange(v,mask):
    return permute(v,lambda i:i^mask)

def along_z(block):
    top=device_count()//4
    return [block]+[exchange(block,top*m) for m in (1,2,3)]

def near_hop(v):
    return permute(v,lambda i:i^(4 if i%2 else 2))

def far_hop(v):
    return permute(v,lambda i:i^(2 if i%2 else 4))

def in_bands(bands,*blocks):
    return tuple(b.reshape(8,bands,-1,b.shape[2]) for b in blocks)

def core_pair(v):
    groups=[[2*i,2*i+1] for i in range(lax.axis_size("fsdp")//2)]
    return lax.all_gather(v,"fsdp",axis=0,tiled=False,axis_index_groups=groups)

def column_half(both):
    c=lax.axis_index("fsdp")%2
    half=both.shape[2]//2
    return lax.dynamic_slice_in_dim(both,c*half,half,axis=2).reshape(-1,half)

def total_over_devices(mine,other,beside_near,beside_z):
    n=device_count()
    mine=mine+exchange(other,1)
    got=[exchange(mine,m) for m in range(2,n//4,2)]
    got,done=tie(got,beside_near())
    for g in got: mine=mine+g
    got=[exchange(mine,m) for m in (n//4,n//2,3*n//4)]
    got,done=tie(got,beside_z(done))
    for g in got: mine=mine+g
    return mine,exchange(mine,1),done

def finish_kernel(scale,sc_ref,mine_ref,other_ref,*outs):
    core=lax.rem(sc_ref[0],2)
    for c,halves in enumerate(((mine_ref,other_ref),(other_ref,mine_ref))):
        @pl.when(core==c)
        def _():
            for i,o in enumerate(outs): o[...]=halves[i//2][8*(i%2):8*(i%2)+8,:]*scale

def finish(scalars,mine,other,scale):
    D=mine.shape[1]
    return pl.pallas_call(functools.partial(finish_kernel,scale),in_specs=[SCALARS,HELD,HELD],out_specs=[HELD]*4,
        out_shape=[sd((8,D),F32)]*4,compiler_params=params(8),cost_estimate=takes(1),name="finish")(scalars,mine,other)

def tie(*v):
    return lax.optimization_barrier(v)

def by_hops(scalars,x,wq,wk,wv,wo,wi,wt,ag,ash,fg,fsh,qd,qu,vd,vu,go):
    D=wq.shape[1]; FF=wi.shape[1]; bands=FF//D; r=wq.shape[0]
    top=device_count()//4
    both=core_pair(jnp.concatenate([wq,wk,wv],0))
    s1=jnp.concatenate([column_half(both[:,r*t:r*t+r]) for t in range(3)],0)
    z1=along_z(s1)
    wo,wi,wt,qd,s1=tie(wo,wi,wt,qd,s1)
    bo,bi,bt=core_pair(wo),core_pair(wi),core_pair(wt)
    s2=jnp.concatenate([column_half(bo)]+[column_half(bi[:,:,D*t:D*t+D]) for t in range(bands)],0)
    s3=column_half(bt)
    dn,upq,upv,dnt,nm=prep(qd,qu,vd,vu,ag,ash,fg,fsh)
    n3=near_hop(s3)
    z1,s2,dn,scalars=tie(z1,s2,dn,scalars)
    a1=jnp.stack(z1,0)
    n1=near_hop(a1)
    z2=exchange(s2,2*top)
    b3=jnp.stack([s3,n3],0)
    y3=exchange(b3,top)
    n1,z2,s2,n3,dn=tie(n1,z2,s2,n3,dn)
    f1=jnp.concatenate([a1,n1],0)
    h1=far_hop(f1); of1=exchange(f1,1)
    e2=jnp.stack([s2,z2],0)
    y2=exchange(e2,top)
    m2=near_hop(e2)
    low,lq,lv=low_rank(x,dn,upq,upv)
    y2,y3,lq=tie(y2,y3,lq)
    n2=near_hop(y2)
    g3=jnp.stack([b3,y3],0)
    z3=exchange(g3,2*top)
    h1,of1=tie(h1,of1)
    oh1=exchange(h1,1)
    oh1,=tie(oh1)
    f2=jnp.stack([e2[0],y2[0],e2[1],y2[1],m2[0],n2[0],m2[1],n2[1]],0)
    h2=far_hop(f2); of2=exchange(f2,1)
    qkv,wqkv=project(scalars,x,lq,lv,in_bands(3,f1,h1,of1,oh1))
    e,ot,o,rt=attend(scalars,qkv,x.shape[0]//SLOT)
    h2,o,of2,z3=tie(h2,o,of2,z3)
    oh2=exchange(h2,1)
    f3=jnp.concatenate([g3,z3],0).swapaxes(0,1).reshape(8,-1,D//2)
    h3=far_hop(f3); of3=exchange(f3,1)
    oh2,=tie(oh2)
    nn,r1,act,gp,w=feed_in(scalars,x,o,nm,in_bands(1+bands,f2,h2,of2,oh2),FF)
    h3,nn,of3=tie(h3,nn,of3)
    oh3=exchange(h3,1)
    out,gfs,gmt=feed_out(scalars,nn,r1,act,gp,go,w,nm,in_bands(1,f3,h3,of3,oh3))
    return qkv,low,wqkv,e,ot,rt,out,gfs,gmt,upq,upv,dnt

def by_all_gather(scalars,x,wq,wk,wv,wo,wi,wt,ag,ash,fg,fsh,qd,qu,vd,vu,go):
    wq,wk,wv,wo,wi,wt=(lax.all_gather(w,AXES,axis=0,tiled=True) for w in (wq,wk,wv,wo,wi,wt))
    D=wq.shape[1]; FF=wi.shape[1]
    dn,upq,upv,dnt,nm=prep(qd,qu,vd,vu,ag,ash,fg,fsh)
    low,lq,lv=low_rank(x,dn,upq,upv)
    qkv,wqkv=project(scalars,x,lq,lv,(jnp.stack([wq,wk,wv],0),))
    e,ot,o,rt=attend(scalars,qkv,x.shape[0]//SLOT)
    nn,r1,act,gp,w=feed_in(scalars,x,o,nm,(jnp.stack([wo]+[wi[:,c:c+D] for c in range(0,FF,D)],0),),FF)
    out,gfs,gmt=feed_out(scalars,nn,r1,act,gp,go,w,nm,(wt[None],))
    return qkv,low,wqkv,e,ot,rt,out,gfs,gmt,upq,upv,dnt

def shards(x,lengths,wq,wk,wv,wo,wi,wt,ag,ash,fg,fsh,qd,qu,vd,vu,go):
    n=device_count()
    valid=lengths[:,0]+lengths[:,1]+4
    me=(lax.axis_index("dp")*lax.axis_size("fsdp")+lax.axis_index("fsdp")).reshape(1)
    scalars=jnp.concatenate([me,valid]).astype(jnp.int32)
    forward=by_hops if n==32 and wq.shape[0]%8==0 else by_all_gather
    qkv,low,wqkv,e,ot,rt,out,gfs,gmt,upq,upv,dnt=forward(scalars,x,wq,wk,wv,wo,wi,wt,ag,ash,fg,fsh,qd,qu,vd,vu,go)
    d,gl,mine,other=attend_back(scalars,qkv,e,ot,rt,gmt,x,low,upq,upv)
    def later_rows(gx):
        for s in range(1,x.shape[0]//SLOT): gx=inputs_grad(s,gfs,d,gl,wqkv,dnt,(gx,))
        return gx
    mine,other,gx=total_over_devices(mine,other,lambda: inputs_grad(0,gfs,d,gl,wqkv,dnt),later_rows)
    qd,vd,qu,vu=finish(scalars,mine,other,1.0/(lengths.shape[0]*n))
    return out,gx,qd.T,qu,vd.T,vu

def solution(mesh):
    sp=P(AXES,None)
    return jax.shard_map(shards,mesh=mesh,in_specs=(sp,)*8+(P(),)*8+(sp,),
        out_specs=(sp,sp,P(),P(),P(),P()),check_vma=False)
```
